256 devices in a mesh: row: 16 (over y_lo, z), col: 16 (over y_hi, x, core).
Axes of the slice: x: 4, y: 4 (y_hi: 2, y_lo: 2; y = y_hi * 2 + y_lo), z: 8, core: 2. Of those that a mesh axis runs over, the one named last changes fastest.
Arguments:
- node_features: bfloat16 [16, 16, 256, 256], P('col', 'row'), may hold values from -6 to 6
- tile_values: bfloat16 [16, 16, 192, 128, 128], P('row', 'col'), may hold values from -0.078125 to 0.078125
- tile_rows: int32 [16, 16, 192], replicated, may hold values from 0 to 31, as said below
- tile_cols: int32 [16, 16, 192], replicated, may hold values from 0 to 31, as said below
- tile_count: int32 [16, 16], replicated, may hold values from 48 to 192, as said below
- weight: bfloat16 [256, 256], replicated, may hold values from -0.375 to 0.375
- cotangent: bfloat16 [16, 16, 256, 256], P('row', 'col'), may hold values from -6 to 6
Outputs:
- activations: bfloat16 [16, 16, 256, 256], P('row', 'col')
- feature_grad: bfloat16 [16, 16, 256, 256], P('col', 'row')
- weight_grad: float32 [256, 256], replicated
The draws below stay inside these ranges and needn't reach their ends.
Inputs may be any that keep to these rules, and one draw needn't show every extreme that they name: tile_count is 192 on the block whose row group and column group share nodes, and between 48 and 96 on every other block. `tile_rows`: within one device block the slots name distinct (tile row, tile column) pairs. `tile_cols`: within one device block the slots name distinct (tile row, tile column) pairs.
All inputs are finite; a program needn't handle non-finite values.
Results may differ from the reference program's by a relative error of at most 0.023.
Values may be sent and summed in bfloat16 or wider, within the bound.
A program may use at most 128 MiB of HBM per device.

```python
import math
import jax
import jax.numpy as jnp
from jax import lax

F = 256
TILE = 128
NODE_DEV = 256
NODES = 65536
ROW_TILES = 32
COL_TILES = 32
TILES = 192
N_ROW = 16
N_COL = 16


def slot_positions(key):
    device_total = N_ROW * N_COL
    device_keys = jax.random.split(key, device_total)

    def single(device_key):
        return jax.random.permutation(device_key, ROW_TILES * COL_TILES)[:TILES]
    places = jax.vmap(single)(device_keys).astype(jnp.int32)
    return places.reshape(N_ROW, N_COL, TILES)


def draw_tile_rows(key, part):
    places = slot_positions(key)
    return (places // COL_TILES).astype(jnp.int32)


def draw_tile_cols(key, part):
    places = slot_positions(key)
    return (places % COL_TILES).astype(jnp.int32)


def draw_tile_count(key, part):
    key = jax.random.fold_in(key, 7)
    light = jax.random.randint(key, (N_ROW, N_COL), TILES // 4, TILES // 2 + 1)
    row_ids = jnp.arange(N_ROW, dtype=jnp.int32)[:, None]
    col_ids = jnp.arange(N_COL, dtype=jnp.int32)[None, :]
    heavy = col_ids == row_ids // (N_ROW // N_COL)
    return jnp.where(heavy, TILES, light).astype(jnp.int32)


def shard_levels(stream_key, dims, cuts, smallest, top_value):
    def one(dim, blocks):
        heights = jax.random.uniform(jax.random.fold_in(jax.random.fold_in(stream_key, 6), dim), (blocks,), jnp.float32, smallest / len(cuts), top_value / len(cuts))
        return jnp.repeat(jnp.exp(heights), dims[dim] // blocks).reshape((-1,) + (1,) * (len(dims) - dim - 1))

    loudness = one(*cuts[0])
    for cut in cuts[1:]:
        loudness = loudness * one(*cut)
    return loudness


def noise(own_key, extent, deviation, reach, cuts=(), held_as=jnp.bfloat16):
    factor_of = shard_levels(own_key, extent, cuts, -0.22, 0.18) if cuts else 1.0
    drawn = jax.random.normal(own_key, extent, jnp.float32) * deviation * factor_of
    return jnp.minimum(jnp.maximum(drawn, -reach), reach).astype(held_as)


def setup_inputs(seed: int = 0) -> dict:
    key_of = jax.random.split(jax.random.key(seed), 8)
    node_features = noise(key_of[0], (N_COL, N_ROW, NODE_DEV, F), 1.0, 6.0, ((0, 16), (1, 16)))
    tile_values = noise(key_of[1], (N_ROW, N_COL, TILES, TILE, TILE), (TILE * TILES * (8 + 3 * N_COL) // (8 * ROW_TILES)) ** -0.5, 0.078125, ((0, 16), (1, 16)))
    tile_rows = draw_tile_rows(jax.random.fold_in(key_of[7], 71), 0)
    tile_cols = draw_tile_cols(jax.random.fold_in(key_of[7], 71), 0)
    tile_count = draw_tile_count(jax.random.fold_in(key_of[7], 71), 0)
    weight = noise(key_of[5], (F, F), F ** -0.5, 0.375)
    cotangent = noise(key_of[6], (N_ROW, N_COL, NODE_DEV, F), 1.0, 6.0, ((0, 16), (1, 16)))
    return dict(node_features=node_features, tile_values=tile_values, tile_rows=tile_rows, tile_cols=tile_cols, tile_count=tile_count, weight=weight, cotangent=cotangent)


def aggregate(values, rows, cols, counts, table, flip, out_tiles):
    device_total = N_ROW * N_COL
    flat_values = values.reshape(device_total, TILES, TILE, TILE)
    flat_rows = rows.reshape(device_total, TILES).astype(jnp.int32)
    flat_cols = cols.reshape(device_total, TILES).astype(jnp.int32)
    flat_counts = counts.reshape(device_total).astype(jnp.int32)
    devices = jnp.arange(device_total, dtype=jnp.int32)
    lanes = jnp.arange(TILES, dtype=jnp.int32)

    def visit(carried, item):
        tiles, row_ids, col_ids, live_count, device = item
        group_row = device // N_COL
        group_col = device % N_COL
        global_rows = group_row * ROW_TILES + row_ids
        global_cols = group_col * COL_TILES + col_ids
        if flip:
            source, target, pattern = (global_rows, global_cols, 'kba,kbf->kaf')
        else:
            source, target, pattern = (global_cols, global_rows, 'kab,kbf->kaf')
        operand = table[source].astype(jnp.float32)
        product = jnp.einsum(pattern, tiles.astype(jnp.float32), operand, precision=lax.Precision.HIGHEST)
        product = jnp.where((lanes < live_count)[:, None, None], product, jnp.float32(0.0))
        return (carried.at[target].add(product), None)
    start_sum = jnp.zeros((out_tiles, TILE, F), jnp.float32)
    result, _ = lax.scan(visit, start_sum, (flat_values, flat_rows, flat_cols, flat_counts, devices))
    return result

def reference(node_features, tile_values, tile_rows, tile_cols, tile_count, weight, cotangent):
    out_tiles = NODES // TILE
    feature_table = node_features.reshape(out_tiles, TILE, F)
    summed = aggregate(tile_values, tile_rows, tile_cols, tile_count, feature_table, False, out_tiles)
    aggregated = summed.reshape(NODES, F).astype(jnp.bfloat16)
    pre_act = jnp.dot(aggregated, weight, preferred_element_type=jnp.float32)
    activations = jax.nn.silu(pre_act).astype(jnp.bfloat16)
    upstream = cotangent.reshape(NODES, F).astype(jnp.float32)
    logistic = jax.nn.sigmoid(pre_act)
    d_pre = (upstream * logistic * (1.0 + pre_act * (1.0 - logistic))).astype(jnp.bfloat16)
    weight_grad = jnp.dot(aggregated.T, d_pre, preferred_element_type=jnp.float32) * (1.0 / math.sqrt(NODES))
    grad_rows = jnp.dot(d_pre, weight.T, preferred_element_type=jnp.float32).astype(jnp.bfloat16)
    grad_table = grad_rows.reshape(out_tiles, TILE, F)
    back_sum = aggregate(tile_values, tile_rows, tile_cols, tile_count, grad_table, True, out_tiles)
    feature_grad = back_sum.reshape(NODES, F).astype(jnp.bfloat16)
    return (activations.reshape(N_ROW, N_COL, NODE_DEV, F), feature_grad.reshape(N_COL, N_ROW, NODE_DEV, F), weight_grad)
```

```python
import functools
import math

import jax
import jax.numpy as jnp
from jax import lax
from jax.experimental import pallas as pl
from jax.experimental.pallas import tpu as pltpu
from jax.sharding import PartitionSpec as P

MESH = pl.DeviceIdType.MESH
F32 = jnp.float32
BF16 = jnp.bfloat16

NZ = 8
NX = 4


class Sender:
    def __init__(self, send_sem, recv_sem):
        self.send_sem = send_sem
        self.recv_sem = recv_sem
        self.ids = {}
        self.sent = []

    def slot(self, key):
        if key not in self.ids:
            self.ids[key] = len(self.ids)
        return self.ids[key]

    def copy(self, key, src, dst, device_id):
        n = self.slot(key)
        return pltpu.make_async_remote_copy(
            src_ref=src,
            dst_ref=dst,
            send_sem=self.send_sem.at[n],
            recv_sem=self.recv_sem.at[n],
            device_id=device_id,
            device_id_type=MESH,
        )

    def send(self, key, src, dst, device_id):
        c = self.copy(key, src, dst, device_id)
        c.start()
        self.sent.append(c)

    def wait(self, key, dst, device_id):
        self.copy(key, dst, dst, device_id).wait_recv()

    def finish(self):
        for c in self.sent:
            c.wait_send()
        self.sent = []


def greet(peers):
    barrier = pltpu.get_barrier_semaphore()
    for peer in peers:
        pl.semaphore_signal(barrier, inc=1, device_id=peer, device_id_type=MESH)
    pl.semaphore_wait(barrier, len(peers))


class RowPlace:
    def __init__(self):
        me = lax.axis_index("row")
        self.yl = me // NZ
        self.z = lax.rem(me, NZ)
        self.right = {"row": self.at(self.yl, 1)}
        self.left = {"row": self.at(self.yl, NZ - 1)}
        self.across = {"row": self.at(1 - self.yl, 0)}
        self.peers = [self.right, self.left, self.across]

    def at(self, yl, hops):
        return yl * NZ + lax.rem(self.z + hops + NZ, NZ)


class ColPlace:
    def __init__(self):
        me = lax.axis_index("col")
        self.yh = me // (2 * NX)
        self.x = lax.rem(me // 2, NX)
        self.core = lax.rem(me, 2)
        self.right = {"col": self.at(self.yh, 1, self.core)}
        self.left = {"col": self.at(self.yh, NX - 1, self.core)}
        self.across = {"col": self.at(1 - self.yh, 0, self.core)}
        self.sibling = {"col": self.at(self.yh, 0, 1 - self.core)}
        self.peers = [self.right, self.left, self.across, self.sibling]

    def xat(self, hops):
        return lax.rem(self.x + hops + NX, NX)

    def at(self, yh, hops, core):
        return (yh * NX + self.xat(hops)) * 2 + core


def gather_row_kernel(own_ref, tab, send_sem, recv_sem, local_sem):
    rows = own_ref.shape[0]
    cut = (rows * 7 // 16) // 16 * 16
    half = rows // 2
    cut_half = (cut * 4 // 7) // 16 * 16
    p = RowPlace()
    me = p.at(p.yl, 0)
    local = pltpu.make_async_copy(own_ref, tab.at[me], local_sem)
    local.start()
    s = Sender(send_sem, recv_sem)
    greet(p.peers)

    def part(yl, hops, lo, hi):
        return tab.at[p.at(yl, hops), pl.ds(lo, hi - lo)]

    mine, other = p.yl, 1 - p.yl
    s.send("ya", own_ref.at[pl.ds(0, cut)], part(mine, 0, 0, cut), p.across)
    s.send(("o", 1, 1), own_ref, tab.at[me], p.right)
    s.send(("o", -1, 1), own_ref, tab.at[me], p.left)
    s.send(("yb", 0), own_ref.at[pl.ds(cut, rows - cut)], part(mine, 0, cut, rows), p.across)
    s.wait("ya", part(other, 0, 0, cut), p.across)
    for d, to in ((1, p.right), (-1, p.left)):
        s.send(("a", d, 1), part(other, 0, 0, cut), part(other, 0, 0, cut), to)

    last_own = {1: (0, half), -1: (half, rows)}
    last_cut = {1: (0, cut_half), -1: (cut_half, cut)}
    for h in range(1, NZ // 2 + 1):
        last = h == NZ // 2
        for d, to in ((1, p.right), (-1, p.left)):
            lo, hi = last_own[d] if last else (0, rows)
            s.wait(("o", d, h), part(mine, -d * h, lo, hi), to)
            if not last:
                lo, hi = last_own[d] if h == NZ // 2 - 1 else (0, rows)
                block = part(mine, -d * h, lo, hi)
                s.send(("o", d, h + 1), block, block, to)
                block = part(mine, -d * h, cut, rows)
                s.send(("yb", -d * h), block, block, p.across)
        if last:
            block = part(mine, h, cut, rows)
            s.send(("yb", h), block, block, p.across)
        for d, to in ((1, p.right), (-1, p.left)):
            lo, hi = last_cut[d] if last else (0, cut)
            s.wait(("a", d, h), part(other, -d * h, lo, hi), to)
            if not last:
                lo, hi = last_cut[d] if h == NZ // 2 - 1 else (0, cut)
                block = part(other, -d * h, lo, hi)
                s.send(("a", d, h + 1), block, block, to)
    for k in (0, 1, -1, 2, -2, 3, -3, NZ // 2):
        s.wait(("yb", k), part(other, k, cut, rows), p.across)
    local.wait()
    s.finish()


def gather_row(own):
    rows, feats = own.shape
    n_row = lax.axis_size("row")
    return pl.pallas_call(
        gather_row_kernel,
        out_shape=jax.ShapeDtypeStruct((n_row, rows, feats), own.dtype),
        in_specs=[pl.BlockSpec(memory_space=pltpu.VMEM)],
        out_specs=pl.BlockSpec(memory_space=pltpu.VMEM),
        scratch_shapes=[
            pltpu.SemaphoreType.DMA((40,)),
            pltpu.SemaphoreType.DMA((40,)),
            pltpu.SemaphoreType.DMA,
        ],
        compiler_params=pltpu.CompilerParams(
            collective_id=1, has_side_effects=True, vmem_limit_bytes=32 << 20
        ),
        name="gather_row",
    )(own)


CHUNK = 16
GROUP = 4


def sparse_kernel(flip, tr_ref, tc_ref, cnt_ref, tiles_ref, tab_ref, out_ref, tr, tc, cnt, tiles, acc, sems, isems):
    slots = tiles_ref.shape[0]
    mr, mc = lax.axis_index("row"), lax.axis_index("col")
    ints = [
        pltpu.make_async_copy(tr_ref.at[mr], tr, isems.at[0]),
        pltpu.make_async_copy(tc_ref.at[mr], tc, isems.at[1]),
        pltpu.make_async_copy(cnt_ref, cnt, isems.at[2]),
    ]
    for c in ints:
        c.start()

    def fetch(c):
        piece = pl.ds(c * CHUNK, CHUNK)
        return pltpu.make_async_copy(tiles_ref.at[piece], tiles.at[piece], sems.at[c])

    for c in range(slots // CHUNK):
        fetch(c).start()
    acc[...] = jnp.zeros_like(acc)
    for c in ints:
        c.wait()
    live = cnt[mr, mc]

    def chunk(c, _):
        fetch(c).wait()

        def group(g, _):
            for u in range(GROUP):
                k = c * CHUNK + g * GROUP + u
                r, q = tr[mc, k], tc[mc, k]
                if flip:
                    prod = lax.dot_general(
                        tiles[k], tab_ref[r], (((0,), (0,)), ((), ())), preferred_element_type=F32
                    )
                    to = q
                else:
                    prod = jnp.dot(tiles[k], tab_ref[q], preferred_element_type=F32)
                    to = r
                acc[to] += jnp.where(k < live, prod, 0.0)
            return 0

        left = jnp.clip(live - c * CHUNK, 0, CHUNK)
        lax.fori_loop(0, (left + GROUP - 1) // GROUP, group, 0)
        return 0

    lax.fori_loop(0, slots // CHUNK, chunk, 0)
    out_ref[...] = acc[...].astype(out_ref.dtype)


def sparse(flip, tile_rows, tile_cols, tile_count, tiles, table):
    slots, edge, _ = tiles.shape
    n_tiles, _, feats = table.shape
    n_row, n_col, _ = tile_rows.shape
    hbm = pl.BlockSpec(memory_space=pl.ANY)
    vmem = pl.BlockSpec(memory_space=pltpu.VMEM)
    return pl.pallas_call(
        functools.partial(sparse_kernel, flip),
        out_shape=jax.ShapeDtypeStruct((n_tiles, edge, feats), BF16),
        in_specs=[hbm, hbm, hbm, hbm, vmem],
        out_specs=vmem,
        scratch_shapes=[
            pltpu.SMEM((n_col, slots), jnp.int32),
            pltpu.SMEM((n_col, slots), jnp.int32),
            pltpu.SMEM((n_row, n_col), jnp.int32),
            pltpu.VMEM((slots, edge, edge), BF16),
            pltpu.VMEM((n_tiles, edge, feats), F32),
            pltpu.SemaphoreType.DMA((slots // CHUNK,)),
            pltpu.SemaphoreType.DMA((3,)),
        ],
        compiler_params=pltpu.CompilerParams(vmem_limit_bytes=48 << 20),
        name="sparse_back" if flip else "sparse_forward",
    )(tile_rows, tile_cols, tile_count, tiles, table)


def add_into(dst, src):
    dst[...] = (dst[...].astype(F32) + src[...].astype(F32)).astype(dst.dtype)


def reduce_col(s, p, tag, part, cbuf, xbuf, ybuf, lo, hi):
    half = (hi - lo) // 2
    n = hi - lo
    rows = pl.ds(lo, n)
    sib = 1 - p.core
    for h in (2, 1, 3, 0):
        x = p.xat(h)
        s.send((tag, "c", h), part.at[:, x, sib, rows], cbuf.at[:, x, rows], p.sibling)
    yield

    def take(h):
        x = p.xat(h)
        s.wait((tag, "c", h), cbuf.at[:, x, rows], p.sibling)
        add_into(part.at[:, x, p.core, rows], cbuf.at[:, x, rows])

    way = {1: (p.right, pl.ds(lo, half)), -1: (p.left, pl.ds(lo + half, n - half))}
    take(2)
    for d in (1, -1):
        to, piece = way[d]
        s.send((tag, "x2", d), part.at[:, p.xat(2), p.core, piece], xbuf.at[0, :, piece], to)
    take(1)
    take(3)
    yield
    for d in (1, -1):
        to, piece = way[d]
        x = p.xat(d)
        s.wait((tag, "x2", d), xbuf.at[0, :, piece], to)
        add_into(part.at[:, x, p.core, piece], xbuf.at[0, :, piece])
        slot = 1 if d == 1 else 2
        s.send((tag, "x1", d), part.at[:, x, p.core, rows], xbuf.at[slot, :, rows], to)
    take(0)
    yield
    for d in (1, -1):
        slot = 1 if d == 1 else 2
        s.wait((tag, "x1", d), xbuf.at[slot, :, rows], way[d][0])
    total = part.at[:, p.x, p.core, rows]
    total[...] = (
        total[...].astype(F32) + xbuf[1, :, rows].astype(F32) + xbuf[2, :, rows].astype(F32)
    ).astype(total.dtype)
    s.send((tag, "y"), part.at[1 - p.yh, p.x, p.core, rows], ybuf.at[rows], p.across)
    yield
    s.wait((tag, "y"), ybuf.at[rows], p.across)
    add_into(part.at[p.yh, p.x, p.core, rows], ybuf.at[rows])


def gather_col(s, p, tag, tab, lo, hi):
    n = hi - lo
    half = n // 2
    rows = pl.ds(lo, n)
    mine, other = p.yh, 1 - p.yh
    way = {1: (p.right, pl.ds(lo, half)), -1: (p.left, pl.ds(lo + half, n - half))}

    def block(yh, h, piece):
        return tab.at[yh, p.xat(h), p.core, piece]

    def push(key, b, to):
        s.send((tag,) + key, b, b, to)

    push(("y",), block(mine, 0, rows), p.across)
    for d in (1, -1):
        push(("o", d), block(mine, 0, rows), way[d][0])
    push(("c", 0, 0), block(mine, 0, rows), p.sibling)
    yield
    s.wait((tag, "y"), block(other, 0, rows), p.across)
    for d in (1, -1):
        push(("t", d), block(other, 0, rows), way[d][0])
    push(("c", 1, 0), block(other, 0, rows), p.sibling)
    yield
    for d in (1, -1):
        to, piece = way[d]
        s.wait((tag, "o", d), block(mine, -d, rows), to)
        push(("o2", d), block(mine, -d, piece), to)
        push(("c", 0, -d), block(mine, -d, rows), p.sibling)
    for d in (1, -1):
        to, piece = way[d]
        s.wait((tag, "t", d), block(other, -d, rows), to)
        push(("t2", d), block(other, -d, piece), to)
        push(("c", 1, -d), block(other, -d, rows), p.sibling)
    yield
    for k, (key, yh) in enumerate((("o2", mine), ("t2", other))):
        for d in (1, -1):
            to, piece = way[d]
            s.wait((tag, key, d), block(yh, -2 * d, piece), to)
        push(("c", k, 2), block(yh, 2, rows), p.sibling)
    yield
    for k, yh in ((0, mine), (1, other)):
        for h in (0, -1, 1, 2):
            s.wait((tag, "c", k, h), tab.at[yh, p.xat(h), 1 - p.core, rows], p.sibling)


def drain(*steps):
    steps = list(steps)
    while steps:
        for g in list(steps):
            try:
                next(g)
            except StopIteration:
                steps.remove(g)


def middle_kernel(
    part_ref, w_ref, g_ref, act_ref, etab, wg_ref, part, cbuf, xbuf, ybuf, wpart, wcbuf, wxbuf, wybuf, zbuf,
    send_sem, recv_sem, part_sems,
):
    rows = g_ref.shape[0]
    p = ColPlace()
    q = RowPlace()
    loads = []
    order = [(core, h) for h in (2, 1, 3, 0) for core in (1, 0)]
    for n, (c, h) in enumerate(order):
        core = 1 - p.core if c else p.core
        x = p.xat(h)
        loads.append(pltpu.make_async_copy(part_ref.at[:, x, core], part.at[:, x, core], part_sems.at[n]))
    for c in loads:
        c.start()
    s = Sender(send_sem, recv_sem)
    far = [{"row": q.at(q.yl, h)} for h in (2, 4, 6)]
    greet(p.peers + q.peers + far)
    for c in loads:
        c.wait()
    pieces = 2
    step = rows // pieces
    drain(*[
        reduce_col(s, p, ("r", i), part, cbuf, xbuf, ybuf, i * step, (i + 1) * step) for i in range(pieces)
    ])
    agg = part[p.yh, p.x, p.core]
    pre = jnp.dot(agg, w_ref[...], preferred_element_type=F32)
    logistic = jax.nn.sigmoid(pre)
    upstream = g_ref[...].astype(F32)
    d_pre = (upstream * logistic * (1.0 + pre * (1.0 - logistic))).astype(BF16)
    grad = lax.dot_general(d_pre, w_ref[...], (((1,), (1,)), ((), ())), preferred_element_type=F32)
    etab[p.yh, p.x, p.core] = grad.astype(BF16)

    gathers = [gather_col(s, p, ("g", i), etab, i * step, (i + 1) * step) for i in range(pieces)]
    for g in gathers:
        next(g)

    def weight_sum():
        act_ref[...] = (pre * logistic).astype(act_ref.dtype)
        wg = lax.dot_general(agg, d_pre, (((0,), (0,)), ((), ())), preferred_element_type=F32)
        wpart[...] = wg.reshape(wpart.shape)
        n = wpart.shape[3]
        yield from reduce_col(s, p, "w", wpart, wcbuf, wxbuf, wybuf, 0, n)
        zbuf[0] = wpart[p.yh, p.x, p.core]
        flip = [p_ for p_ in (q.across,)]
        for bit in (1, 2, 4):
            up = lax.rem(q.z // bit, 2)
            z = q.z + bit * (1 - 2 * up)
            flip.append({"row": q.yl * NZ + z})
        for n_, to in enumerate(flip):
            s.send(("wz", n_), zbuf.at[2 * n_], zbuf.at[2 * n_ + 1], to)
            yield
            s.wait(("wz", n_), zbuf.at[2 * n_ + 1], to)
            zbuf[2 * n_ + 2] = zbuf[2 * n_] + zbuf[2 * n_ + 1]

    drain(*gathers, weight_sum())
    wg_ref[...] = zbuf[8]
    s.finish()


def middle(part, weight, cot):
    n_yh, n_x, n_core, rows, feats = part.shape
    n_w = weight.shape[0] // (n_yh * n_x * n_core)
    hbm = pl.BlockSpec(memory_space=pl.ANY)
    vmem = pl.BlockSpec(memory_space=pltpu.VMEM)
    return pl.pallas_call(
        middle_kernel,
        out_shape=(
            jax.ShapeDtypeStruct((rows, feats), BF16),
            jax.ShapeDtypeStruct(part.shape, BF16),
            jax.ShapeDtypeStruct((n_w, feats), F32),
        ),
        in_specs=[hbm, vmem, vmem],
        out_specs=(vmem, vmem, vmem),
        scratch_shapes=[
            pltpu.VMEM(part.shape, BF16),
            pltpu.VMEM((n_yh, n_x, rows, feats), BF16),
            pltpu.VMEM((3, n_yh, rows, feats), BF16),
            pltpu.VMEM((rows, feats), BF16),
            pltpu.VMEM((n_yh, n_x, n_core, n_w, feats), F32),
            pltpu.VMEM((n_yh, n_x, n_w, feats), F32),
            pltpu.VMEM((3, n_yh, n_w, feats), F32),
            pltpu.VMEM((n_w, feats), F32),
            pltpu.VMEM((9, n_w, feats), F32),
            pltpu.SemaphoreType.DMA((100,)),
            pltpu.SemaphoreType.DMA((100,)),
            pltpu.SemaphoreType.DMA((8,)),
        ],
        compiler_params=pltpu.CompilerParams(
            collective_id=2, has_side_effects=True, vmem_limit_bytes=48 << 20
        ),
        name="middle",
    )(part, weight, cot)


def reduce_row(s, p, part, ybuf, obuf, abuf, fbuf):
    rows = part.shape[1]
    cut = (rows * 7 // 16) // 16 * 16
    half = rows // 2
    cut_half = (cut * 4 // 7) // 16 * 16
    mine, other = p.yl, 1 - p.yl
    ways = ((1, p.right), (-1, p.left))
    last_own = {1: (0, half), -1: (half, rows)}
    last_cut = {1: (0, cut_half), -1: (cut_half, cut)}
    top = NZ // 2

    def blk(yl, hops, lo, hi):
        return part.at[p.at(yl, hops), pl.ds(lo, hi - lo)]

    for d, to in ways:
        lo, hi = last_cut[d]
        s.send(("a", d, top), blk(other, top, lo, hi), abuf.at[(top - 1) * 2 + int(d == 1), pl.ds(lo, hi - lo)], to)
    for k in (4, 3, -3, 2, -2, 1, -1, 0):
        s.send(("yb", k), blk(other, k, cut, rows), ybuf.at[k + 3], p.across)
    yield

    def crossed(k):
        s.wait(("yb", k), ybuf.at[k + 3], p.across)
        add_into(blk(mine, k, cut, rows), ybuf.at[k + 3])

    crossed(top)
    for d, to in ways:
        lo, hi = last_own[d]
        s.send(("o", d, top), blk(mine, top, lo, hi), obuf.at[(top - 1) * 2 + int(d == 1), pl.ds(lo, hi - lo)], to)
    for h in range(top - 1, 0, -1):
        yield
        for d, to in ways:
            lo, hi = last_cut[d] if h == top - 1 else (0, cut)
            got = abuf.at[h * 2 + int(d == 1), pl.ds(lo, hi - lo)]
            s.wait(("a", d, h + 1), got, to)
            add_into(blk(other, d * h, lo, hi), got)
            s.send(
                ("a", d, h), blk(other, d * h, 0, cut), abuf.at[(h - 1) * 2 + int(d == 1), pl.ds(0, cut)], to
            )
        for d, to in ways:
            crossed(d * h)
            lo, hi = last_own[d] if h == top - 1 else (0, rows)
            got = obuf.at[h * 2 + int(d == 1), pl.ds(lo, hi - lo)]
            s.wait(("o", d, h + 1), got, to)
            add_into(blk(mine, d * h, lo, hi), got)
            s.send(("o", d, h), blk(mine, d * h, 0, rows), obuf.at[(h - 1) * 2 + int(d == 1)], to)
    crossed(0)
    yield
    for d, to in ways:
        s.wait(("a", d, 1), abuf.at[int(d == 1), pl.ds(0, cut)], to)
    send = blk(other, 0, 0, cut)
    send[...] = (
        send[...].astype(F32) + abuf[0, pl.ds(0, cut)].astype(F32) + abuf[1, pl.ds(0, cut)].astype(F32)
    ).astype(BF16)
    s.send("fin", send, fbuf, p.across)
    for d, to in ways:
        s.wait(("o", d, 1), obuf.at[int(d == 1)], to)
    yield
    s.wait("fin", fbuf, p.across)


def last_kernel(part_ref, wg_ref, out_ref, wout_ref, part, ybuf, obuf, abuf, fbuf, send_sem, recv_sem, part_sems):
    rows, feats = out_ref.shape
    cut = fbuf.shape[0]
    p = RowPlace()
    c = ColPlace()
    loads = []
    order = [(yl, h) for h in (4, 3, -3, 2, -2, 1, -1, 0) for yl in (1, 0)]
    for n, (o, h) in enumerate(order):
        b = p.at(1 - p.yl if o else p.yl, h)
        loads.append(pltpu.make_async_copy(part_ref.at[b], part.at[b], part_sems.at[n]))
    for x in loads:
        x.start()
    s = Sender(send_sem, recv_sem)
    wout_ref[c.yh, c.x, c.core] = wg_ref[...]
    greet(p.peers + c.peers)
    for x in loads:
        x.wait()
    drain(
        reduce_row(s, p, part, ybuf, obuf, abuf, fbuf),
        gather_col(s, c, "w", wout_ref, 0, wg_ref.shape[0]),
    )
    me = p.at(p.yl, 0)
    total = part[me].astype(F32) + obuf[0].astype(F32) + obuf[1].astype(F32)
    out_ref[pl.ds(0, cut)] = (total[:cut] + fbuf[...].astype(F32)).astype(out_ref.dtype)
    out_ref[pl.ds(cut, rows - cut)] = total[cut:].astype(out_ref.dtype)
    s.finish()


def last(part, wg, shape5):
    n_row, rows, feats = part.shape
    cut = (rows * 7 // 16) // 16 * 16
    hbm = pl.BlockSpec(memory_space=pl.ANY)
    vmem = pl.BlockSpec(memory_space=pltpu.VMEM)
    n_yh, n_x, n_core = shape5
    return pl.pallas_call(
        last_kernel,
        out_shape=(
            jax.ShapeDtypeStruct((rows, feats), BF16),
            jax.ShapeDtypeStruct((n_yh, n_x, n_core) + wg.shape, F32),
        ),
        in_specs=[hbm, vmem],
        out_specs=(vmem, vmem),
        scratch_shapes=[
            pltpu.VMEM(part.shape, BF16),
            pltpu.VMEM((NZ, rows - cut, feats), BF16),
            pltpu.VMEM((NZ, rows, feats), BF16),
            pltpu.VMEM((NZ, cut, feats), BF16),
            pltpu.VMEM((cut, feats), BF16),
            pltpu.SemaphoreType.DMA((60,)),
            pltpu.SemaphoreType.DMA((60,)),
            pltpu.SemaphoreType.DMA((16,)),
        ],
        compiler_params=pltpu.CompilerParams(
            collective_id=3, has_side_effects=True, vmem_limit_bytes=48 << 20
        ),
        name="last",
    )(part, wg)


def per_device(node_features, tile_values, tile_rows, tile_cols, tile_count, weight, cotangent):
    rows, feats = node_features.shape[2:]
    edge = tile_values.shape[3]
    n_row = lax.axis_size("row")
    n_col = lax.axis_size("col")
    shape5 = (n_col // (2 * NX), NX, 2)
    tiles = tile_values[0, 0]
    table = gather_row(node_features[0, 0])
    table = table.reshape(n_row * rows // edge, edge, feats)
    part = sparse(False, tile_rows, tile_cols, tile_count, tiles, table)
    part = part.reshape(shape5 + (rows, feats))
    act, etab, wg = middle(part, weight, cotangent[0, 0])
    etab = etab.reshape(n_col * rows // edge, edge, feats)
    back = sparse(True, tile_rows, tile_cols, tile_count, tiles, etab)
    grad, wgrad = last(back.reshape(n_row, rows, feats), wg, shape5)
    wgrad = wgrad.reshape(feats, feats) * (1.0 / math.sqrt(rows * n_row * n_col))
    return act[None, None], grad[None, None], wgrad


def solution(mesh):
    in_specs = (
        P("col", "row", None, None),
        P("row", "col", None, None, None),
        P(),
        P(),
        P(),
        P(),
        P("row", "col", None, None),
    )
    out_specs = (P("row", "col", None, None), P("col", "row", None, None), P())
    return jax.shard_map(
        per_device, mesh=mesh, in_specs=in_specs, out_specs=out_specs, check_vma=False
    )
```

```python
import functools
import math

import jax
import jax.numpy as jnp
from jax import lax
from jax.experimental import pallas as pl
from jax.experimental.pallas import tpu as pltpu
from jax.sharding import PartitionSpec as P

MESH = pl.DeviceIdType.MESH
F32 = jnp.float32
BF16 = jnp.bfloat16

NZ = 8
NX = 4
TILE = 128
PLACES = 256


class Sender:
    def __init__(self, send_sem, recv_sem):
        self.send_sem = send_sem
        self.recv_sem = recv_sem
        self.ids = {}
        self.sent = []

    def slot(self, key):
        if key not in self.ids:
            self.ids[key] = len(self.ids)
        return self.ids[key]

    def copy(self, key, src, dst, device_id):
        n = self.slot(key)
        return pltpu.make_async_remote_copy(
            src_ref=src,
            dst_ref=dst,
            send_sem=self.send_sem.at[n],
            recv_sem=self.recv_sem.at[n],
            device_id=device_id,
            device_id_type=MESH,
        )

    def send(self, key, src, dst, device_id):
        c = self.copy(key, src, dst, device_id)
        c.start()
        self.sent.append(c)

    def wait(self, key, dst, device_id):
        self.copy(key, dst, dst, device_id).wait_recv()

    def finish(self):
        for c in self.sent:
            c.wait_send()
        self.sent = []


def greet(peers):
    barrier = pltpu.get_barrier_semaphore()
    for peer in peers:
        pl.semaphore_signal(barrier, inc=1, device_id=peer, device_id_type=MESH)
    pl.semaphore_wait(barrier, len(peers))


class RowPlace:
    def __init__(self):
        me = lax.axis_index("row")
        self.yl = me // NZ
        self.z = lax.rem(me, NZ)
        self.right = {"row": self.at(self.yl, 1)}
        self.left = {"row": self.at(self.yl, NZ - 1)}
        self.across = {"row": self.at(1 - self.yl, 0)}
        self.peers = [self.right, self.left, self.across]

    def at(self, yl, hops):
        return yl * NZ + lax.rem(self.z + hops + NZ, NZ)


class ColPlace:
    def __init__(self):
        me = lax.axis_index("col")
        self.yh = me // (2 * NX)
        self.x = lax.rem(me // 2, NX)
        self.core = lax.rem(me, 2)
        self.right = {"col": self.at(self.yh, 1, self.core)}
        self.left = {"col": self.at(self.yh, NX - 1, self.core)}
        self.across = {"col": self.at(1 - self.yh, 0, self.core)}
        self.sibling = {"col": self.at(self.yh, 0, 1 - self.core)}
        self.peers = [self.right, self.left, self.across, self.sibling]
        self.mates = [(dy, h) for dy in (0, 1) for h in range(NX) if (dy, h) != (0, 0)]

    def mate(self, dy, h):
        return {"col": self.at(self.yh + dy - 2 * self.yh * dy, h, self.core)}

    def xat(self, hops):
        return lax.rem(self.x + hops + NX, NX)

    def at(self, yh, hops, core):
        return (yh * NX + self.xat(hops)) * 2 + core


def order_slots(rows, cols, live, n_tiles, plan):
    slots = rows.shape[1]
    places = plan.shape[1]
    steps = (slots + n_tiles) // 2
    sub = lax.broadcasted_iota(jnp.int32, (slots, slots), 0)
    lane = lax.broadcasted_iota(jnp.int32, (slots, slots), 1)
    k_row, k_col = lane[:1].astype(F32), sub[:, :1].astype(F32)
    live_row, live_col = lane[:1] < live, sub[:, :1] < live
    tile = lax.broadcasted_iota(jnp.int32, (n_tiles, slots), 0).astype(F32)
    place = lax.broadcasted_iota(jnp.int32, (slots, places), 1).astype(F32)
    tile_sub = lax.broadcasted_iota(jnp.int32, (n_tiles, places), 0)
    tile_lane = lax.broadcasted_iota(jnp.int32, (n_tiles, places), 1)

    def turn(row):
        return jnp.sum(jnp.where(sub == lane, row, 0.0), axis=1, keepdims=True)

    out = []
    for key, source in ((rows, cols), (cols, rows)):
        key, source = key.astype(F32), source.astype(F32)
        same = (turn(key) == key) & (sub < lane) & live_col
        rank = jnp.sum(jnp.where(same, 1.0, 0.0), axis=0, keepdims=True)
        number = jnp.sum(jnp.where((tile == key) & live_row, 1.0, 0.0), axis=1, keepdims=True)
        pairs = jnp.floor((number + 1.0) * 0.5)
        base = 2.0 * jnp.sum(jnp.where(tile < key, pairs, 0.0), axis=0, keepdims=True)
        at = turn(jnp.where(live_row, base + rank, -1.0))
        hit = at == place
        slot = slots + jnp.sum(jnp.where(hit, k_col - slots, 0.0), axis=0, keepdims=True)
        read = jnp.sum(jnp.where(hit, turn(source), 0.0), axis=0, keepdims=True)
        fresh = jnp.sum(jnp.where(hit & (turn(rank) == 0.0), 1.0, 0.0), axis=0, keepdims=True)
        upto = jnp.sum(jnp.where(tile_sub <= tile_lane, pairs, 0.0), axis=0, keepdims=True)
        some = jnp.sum(jnp.where(tile_sub == tile_lane, number, 0.0), axis=0, keepdims=True)
        final = jnp.where(some > 0.0, upto - 1.0, float(steps))
        out += [slot, read, fresh, final]
    for n, x in enumerate(out):
        plan[pl.ds(n, 1)] = x.astype(jnp.int32)


def gather_row_kernel(tr_ref, tc_ref, cnt_ref, own_ref, tab, plan_ref, tr, tc, cnt, send_sem, recv_sem, local_sem):
    rows = own_ref.shape[0]
    cut = (rows * 7 // 16) // 16 * 16
    half = rows // 2
    cut_half = (cut * 4 // 7) // 16 * 16
    p = RowPlace()
    me = p.at(p.yl, 0)
    mr, mc = lax.axis_index("row"), lax.axis_index("col")
    local = [
        pltpu.make_async_copy(tr_ref.at[mr], tr, local_sem.at[0]),
        pltpu.make_async_copy(tc_ref.at[mr], tc, local_sem.at[1]),
        pltpu.make_async_copy(cnt_ref, cnt, local_sem.at[2]),
        pltpu.make_async_copy(own_ref, tab.at[me], local_sem.at[3]),
    ]
    for c in local:
        c.start()
    s = Sender(send_sem, recv_sem)
    greet(p.peers)

    def part(yl, hops, lo, hi):
        return tab.at[p.at(yl, hops), pl.ds(lo, hi - lo)]

    mine, other = p.yl, 1 - p.yl
    s.send("ya", own_ref.at[pl.ds(0, cut)], part(mine, 0, 0, cut), p.across)
    s.send(("o", 1, 1), own_ref, tab.at[me], p.right)
    s.send(("o", -1, 1), own_ref, tab.at[me], p.left)
    s.send(("yb", 0), own_ref.at[pl.ds(cut, rows - cut)], part(mine, 0, cut, rows), p.across)
    for c in local:
        c.wait()
    order_slots(tr[pl.ds(mc, 1)], tc[pl.ds(mc, 1)], cnt[mr, mc], tab.shape[0] * rows // TILE, plan_ref)
    s.wait("ya", part(other, 0, 0, cut), p.across)
    for d, to in ((1, p.right), (-1, p.left)):
        s.send(("a", d, 1), part(other, 0, 0, cut), part(other, 0, 0, cut), to)

    last_own = {1: (0, half), -1: (half, rows)}
    last_cut = {1: (0, cut_half), -1: (cut_half, cut)}
    for h in range(1, NZ // 2 + 1):
        last = h == NZ // 2
        for d, to in ((1, p.right), (-1, p.left)):
            lo, hi = last_own[d] if last else (0, rows)
            s.wait(("o", d, h), part(mine, -d * h, lo, hi), to)
            if not last:
                lo, hi = last_own[d] if h == NZ // 2 - 1 else (0, rows)
                block = part(mine, -d * h, lo, hi)
                s.send(("o", d, h + 1), block, block, to)
                block = part(mine, -d * h, cut, rows)
                s.send(("yb", -d * h), block, block, p.across)
        if last:
            block = part(mine, h, cut, rows)
            s.send(("yb", h), block, block, p.across)
        for d, to in ((1, p.right), (-1, p.left)):
            lo, hi = last_cut[d] if last else (0, cut)
            s.wait(("a", d, h), part(other, -d * h, lo, hi), to)
            if not last:
                lo, hi = last_cut[d] if h == NZ // 2 - 1 else (0, cut)
                block = part(other, -d * h, lo, hi)
                s.send(("a", d, h + 1), block, block, to)
    for k in (0, 1, -1, 2, -2, 3, -3, NZ // 2):
        s.wait(("yb", k), part(other, k, cut, rows), p.across)
    s.finish()


def gather_row(own, tile_rows, tile_cols, tile_count):
    rows, feats = own.shape
    n_row, n_col, slots = tile_rows.shape
    hbm = pl.BlockSpec(memory_space=pl.ANY)
    vmem = pl.BlockSpec(memory_space=pltpu.VMEM)
    return pl.pallas_call(
        gather_row_kernel,
        out_shape=(
            jax.ShapeDtypeStruct((n_row, rows, feats), own.dtype),
            jax.ShapeDtypeStruct((8, PLACES), jnp.int32),
        ),
        in_specs=[hbm, hbm, hbm, vmem],
        out_specs=(vmem, vmem),
        scratch_shapes=[
            pltpu.VMEM((n_col, slots), jnp.int32),
            pltpu.VMEM((n_col, slots), jnp.int32),
            pltpu.SMEM((n_row, n_col), jnp.int32),
            pltpu.SemaphoreType.DMA((40,)),
            pltpu.SemaphoreType.DMA((40,)),
            pltpu.SemaphoreType.DMA((4,)),
        ],
        compiler_params=pltpu.CompilerParams(
            collective_id=1, has_side_effects=True, vmem_limit_bytes=32 << 20
        ),
        name="gather_row",
    )(tile_rows, tile_cols, tile_count, own)


CHUNK = 16
GROUP = 4


def multiply(flip, plan, tiles, tab, stash, out):
    steps = stash.shape[0] - 1
    first = 4 if flip else 0
    side = (0, 0) if flip else (1, 0)
    shape = stash.shape[1:]

    def some(g, acc):
        for u in range(GROUP):
            p = g * GROUP + u
            k = [plan[first, 2 * p + i] for i in (0, 1)]
            q = [plan[first + 1, 2 * p + i] for i in (0, 1)]
            left = jnp.concatenate([tiles[i] for i in k], axis=side[0])
            right = jnp.concatenate([tab[i] for i in q], axis=0)
            prod = lax.dot_general(left, right, (((side[0],), (0,)), ((), ())), preferred_element_type=F32)
            fresh = plan[first + 2, 2 * p] == 1
            acc = jnp.where(fresh, 0.0, acc) + prod
            stash[p] = acc.astype(stash.dtype)
        return acc

    lax.fori_loop(0, steps // GROUP, some, jnp.zeros(shape, F32))
    stash[steps] = jnp.zeros(shape, stash.dtype)
    for t in range(out.shape[0]):
        out[t] = stash[plan[first + 3, t]]


def sparse_kernel(flip, plan_ref, tiles_ref, tab_ref, out_ref, plan, tiles, stash, sems, psem):
    slots, edge, _ = tiles_ref.shape
    get = pltpu.make_async_copy(plan_ref, plan, psem)
    get.start()
    chunks = []
    for c in range(slots // CHUNK):
        piece = pl.ds(c * CHUNK, CHUNK)
        chunks.append(pltpu.make_async_copy(tiles_ref.at[piece], tiles.at[piece], sems.at[c]))
    for c in chunks:
        c.start()
    tiles[slots] = jnp.zeros((edge, edge), tiles.dtype)
    get.wait()
    for c in chunks:
        c.wait()
    multiply(flip, plan, tiles, tab_ref, stash, out_ref)


def sparse(flip, plan, tiles, table):
    slots, edge, _ = tiles.shape
    n_tiles, _, feats = table.shape
    hbm = pl.BlockSpec(memory_space=pl.ANY)
    vmem = pl.BlockSpec(memory_space=pltpu.VMEM)
    return pl.pallas_call(
        functools.partial(sparse_kernel, flip),
        out_shape=jax.ShapeDtypeStruct((n_tiles, edge, feats), BF16),
        in_specs=[hbm, hbm, vmem],
        out_specs=vmem,
        scratch_shapes=[
            pltpu.SMEM(plan.shape, jnp.int32),
            pltpu.VMEM((slots + 1, edge, edge), BF16),
            pltpu.VMEM(((slots + n_tiles) // 2 + 1, edge, feats), BF16),
            pltpu.SemaphoreType.DMA((slots // CHUNK,)),
            pltpu.SemaphoreType.DMA,
        ],
        compiler_params=pltpu.CompilerParams(vmem_limit_bytes=48 << 20),
        name="sparse_back" if flip else "sparse_forward",
    )(plan, tiles, table)


def add_into(dst, *terms):
    total = dst[...].astype(F32)
    for t in terms:
        total = total + t[...].astype(F32)
    dst[...] = total.astype(dst.dtype)


def reduce_col(s, p, tag, part, cbuf, xa2, xa1, xb2, xb1, yb, ya):
    rows = part.shape[3]
    half = rows // 2
    qr = half // 2
    a_, b_ = pl.ds(0, half), pl.ds(half, half)
    mine, other, core, sib = p.yh, 1 - p.yh, p.core, 1 - p.core
    ways = ((1, p.right, 0), (-1, p.left, 1))

    def cuts(n, base):
        return pl.ds(base + n * qr, qr)

    def both(n, h, ds):
        s.send((tag, "c", n, h), part.at[:, p.xat(h), sib, ds], cbuf.at[:, p.xat(h), ds], p.sibling)

    def one(n, yh, h, ds):
        s.send((tag, "c", n, h), part.at[yh, p.xat(h), sib, ds], cbuf.at[yh, p.xat(h), ds], p.sibling)

    def took_both(n, h, ds):
        got = cbuf.at[:, p.xat(h), ds]
        s.wait((tag, "c", n, h), got, p.sibling)
        return got

    def took_one(n, yh, h, ds):
        got = cbuf.at[yh, p.xat(h), ds]
        s.wait((tag, "c", n, h), got, p.sibling)
        return got

    for h in (2, 1, -1, 0):
        one("o", other, h, b_)
    both("a", 2, a_)
    one("b", mine, 2, b_)
    for h in (1, -1):
        both("a", h, a_)
    for h in (1, -1):
        one("b", mine, h, b_)
    both("a", 0, a_)
    one("b", mine, 0, b_)
    yield
    for h in (2, 1, -1, 0):
        send = part.at[other, p.xat(h), core, b_]
        add_into(send, took_one("o", other, h, b_))
        s.send((tag, "yb", h), send, yb.at[h % NX], p.across)
        if h == 2:
            add_into(part.at[:, p.xat(2), core, a_], took_both("a", 2, a_))
            for d, to, n in ways:
                s.send((tag, "xa2", d), part.at[:, p.xat(2), core, cuts(n, 0)], xa2.at[:, cuts(n, 0)], to)
    add_into(part.at[mine, p.xat(2), core, b_], took_one("b", mine, 2, b_))
    for h in (1, -1):
        add_into(part.at[:, p.xat(h), core, a_], took_both("a", h, a_))
    for h in (1, -1):
        add_into(part.at[mine, p.xat(h), core, b_], took_one("b", mine, h, b_))
    yield
    s.wait((tag, "yb", 2), yb.at[2], p.across)
    add_into(part.at[mine, p.xat(2), core, b_], yb.at[2])
    for d, to, n in ways:
        s.send((tag, "xb2", d), part.at[mine, p.xat(2), core, cuts(n, half)], xb2.at[cuts(n, 0)], to)
    yield
    for d, to, n in ways:
        s.wait((tag, "xa2", d), xa2.at[:, cuts(n, 0)], to)
        add_into(part.at[:, p.xat(d), core, cuts(n, 0)], xa2.at[:, cuts(n, 0)])
        s.send((tag, "xa1", d), part.at[:, p.xat(d), core, a_], xa1.at[n], to)
    add_into(part.at[:, p.x, core, a_], took_both("a", 0, a_))
    add_into(part.at[mine, p.x, core, b_], took_one("b", mine, 0, b_))
    yield
    for d, to, n in ways:
        s.wait((tag, "yb", d), yb.at[d % NX], p.across)
        add_into(part.at[mine, p.xat(d), core, b_], yb.at[d % NX])
        s.wait((tag, "xb2", d), xb2.at[cuts(n, 0)], to)
        add_into(part.at[mine, p.xat(d), core, cuts(n, half)], xb2.at[cuts(n, 0)])
        s.send((tag, "xb1", d), part.at[mine, p.xat(d), core, b_], xb1.at[n], to)
    yield
    for d, to, n in ways:
        s.wait((tag, "xa1", d), xa1.at[n], to)
    add_into(part.at[:, p.x, core, a_], xa1.at[0], xa1.at[1])
    s.send((tag, "ya"), part.at[other, p.x, core, a_], ya, p.across)
    s.wait((tag, "yb", 0), yb.at[0], p.across)
    yield
    for d, to, n in ways:
        s.wait((tag, "xb1", d), xb1.at[n], to)
    add_into(part.at[mine, p.x, core, b_], yb.at[0], xb1.at[0], xb1.at[1])
    yield
    s.wait((tag, "ya"), ya, p.across)
    add_into(part.at[mine, p.x, core, a_], ya)


def reduce_col_scratch(n_yh, n_x, rows, feats):
    half = rows // 2
    return [
        pltpu.VMEM((n_yh, n_x, rows, feats), BF16),
        pltpu.VMEM((n_yh, half, feats), BF16),
        pltpu.VMEM((2, n_yh, half, feats), BF16),
        pltpu.VMEM((half, feats), BF16),
        pltpu.VMEM((2, half, feats), BF16),
        pltpu.VMEM((n_x, half, feats), BF16),
        pltpu.VMEM((half, feats), BF16),
    ]


def gather_col(s, p, tag, tab):
    rows = tab.shape[3]
    half = rows // 2
    qr = half // 2
    a_, b_, all_ = pl.ds(0, half), pl.ds(half, half), pl.ds(0, rows)
    mine, other = p.yh, 1 - p.yh
    ways = ((1, p.right, 0), (-1, p.left, 1))
    sibs = []

    def block(yh, h, ds):
        return tab.at[yh, p.xat(h), p.core, ds]

    def push(key, b, to):
        s.send((tag,) + key, b, b, to)

    def share(k, h, ds, name):
        push(("c", k, h, name), block((mine, other)[k], h, ds), p.sibling)
        sibs.append((k, h, ds, name))

    def took(key, yh, h, ds):
        s.wait((tag,) + key, block(yh, h, ds), p.sibling)

    push(("y",), block(mine, 0, a_), p.across)
    for d, to, n in ways:
        push(("ob", d), block(mine, 0, b_), to)
    for d, to, n in ways:
        push(("oa", d), block(mine, 0, a_), to)
    push(("yb", 0), block(mine, 0, b_), p.across)
    share(0, 0, all_, "f")
    yield
    took(("y",), other, 0, a_)
    for d, to, n in ways:
        push(("ta", d), block(other, 0, a_), to)
    share(1, 0, a_, "a")
    yield
    for d, to, n in ways:
        took(("ob", d), mine, -d, b_)
        push(("ob2", d), block(mine, -d, pl.ds(half + n * qr, qr)), to)
        push(("yb", -d), block(mine, -d, b_), p.across)
        share(0, -d, b_, "b")
    for d, to, n in ways:
        took(("oa", d), mine, -d, a_)
        push(("oa2", d), block(mine, -d, pl.ds(n * qr, qr)), to)
        share(0, -d, a_, "a")
    yield
    for d, to, n in ways:
        took(("ta", d), other, -d, a_)
        push(("ta2", d), block(other, -d, pl.ds(n * qr, qr)), to)
        share(1, -d, a_, "a")
    took(("yb", 0), other, 0, b_)
    share(1, 0, b_, "b")
    yield
    for d, to, n in ways:
        took(("ob2", d), mine, 2, pl.ds(half + n * qr, qr))
    push(("yb", 2), block(mine, 2, b_), p.across)
    share(0, 2, b_, "b")
    yield
    for d in (1, -1):
        took(("yb", d), other, d, b_)
        share(1, d, b_, "b")
    for d, to, n in ways:
        took(("oa2", d), mine, 2, pl.ds(n * qr, qr))
    share(0, 2, a_, "a")
    yield
    for d, to, n in ways:
        took(("ta2", d), other, 2, pl.ds(n * qr, qr))
    share(1, 2, a_, "a")
    took(("yb", 2), other, 2, b_)
    share(1, 2, b_, "b")
    yield
    for k, h, ds, name in sibs:
        s.wait((tag, "c", k, h, name), tab.at[(mine, other)[k], p.xat(h), 1 - p.core, ds], p.sibling)


def drain(*steps):
    steps = list(steps)
    while steps:
        for g in list(steps):
            try:
                next(g)
            except StopIteration:
                steps.remove(g)


def sum_weight(s, p, q, wpart, wc, wd, wy, wz, scale):
    core, sib = p.core, 1 - p.core
    s.send("wc", wpart.at[:, :, sib], wc, p.sibling)
    yield
    s.wait("wc", wc, p.sibling)
    mine = wpart.at[:, :, core]
    mine[...] = mine[...] + wc[...]
    for dy, h in p.mates:
        yh = p.yh + dy - 2 * p.yh * dy
        s.send(("wd", dy, h), wpart.at[yh, p.xat(h), core], wd.at[dy * NX + h], p.mate(dy, h))
    yield
    total = wpart[p.yh, p.x, core]
    for dy, h in p.mates:
        s.wait(("wd", dy, h), wd.at[dy * NX + h], p.mate(dy, h))
        total = total + wd[dy * NX + h]
    wy[0] = total
    s.send("wy", wy.at[0], wy.at[1], q.across)
    yield
    s.wait("wy", wy.at[1], q.across)
    wz[q.z] = wy[0] + wy[1]
    for h in range(1, NZ):
        s.send(("wz", h), wz.at[q.z], wz.at[q.z], {"row": q.at(q.yl, h)})
    yield
    for h in range(1, NZ):
        s.wait(("wz", h), wz.at[lax.rem(q.z - h + NZ, NZ)], q.across)
    total = wz[0]
    for z in range(1, NZ):
        total = total + wz[z]
    wy[2] = total * scale


def middle_kernel(scale, part_ref, w_ref, g_ref, act_ref, etab, wg_ref, part, *rest):
    bufs, (wpart, wc, wd, wy, wz, send_sem, recv_sem, part_sems) = rest[:7], rest[7:]
    p = ColPlace()
    q = RowPlace()
    loads = []
    for n in range(2):
        core = (1 - p.core, p.core)[n]
        loads.append(pltpu.make_async_copy(part_ref.at[:, :, core], part.at[:, :, core], part_sems.at[n]))
    for c in loads:
        c.start()
    s = Sender(send_sem, recv_sem)
    greet(
        [p.sibling, q.across]
        + [p.mate(dy, h) for dy, h in p.mates]
        + [{"row": q.at(q.yl, h)} for h in range(1, NZ)]
    )
    for c in loads:
        c.wait()
    drain(reduce_col(s, p, "r", part, *bufs))
    agg = part[p.yh, p.x, p.core]
    pre = jnp.dot(agg, w_ref[...], preferred_element_type=F32)
    logistic = jax.nn.sigmoid(pre)
    upstream = g_ref[...].astype(F32)
    d_pre = (upstream * logistic * (1.0 + pre * (1.0 - logistic))).astype(BF16)
    grad = lax.dot_general(d_pre, w_ref[...], (((1,), (1,)), ((), ())), preferred_element_type=F32)
    etab[p.yh, p.x, p.core] = grad.astype(BF16)
    gather = gather_col(s, p, "g", etab)
    next(gather)
    act_ref[...] = (pre * logistic).astype(act_ref.dtype)
    wg = lax.dot_general(agg, d_pre, (((0,), (0,)), ((), ())), preferred_element_type=F32)
    wpart[...] = wg.reshape(wpart.shape)
    drain(sum_weight(s, p, q, wpart, wc, wd, wy, wz, scale), gather)
    wg_ref[...] = wy[2]
    s.finish()


def middle(part, weight, cot, scale):
    n_yh, n_x, n_core, rows, feats = part.shape
    n_w = weight.shape[0] // (n_yh * n_x * n_core)
    hbm = pl.BlockSpec(memory_space=pl.ANY)
    vmem = pl.BlockSpec(memory_space=pltpu.VMEM)
    return pl.pallas_call(
        functools.partial(middle_kernel, scale),
        out_shape=(
            jax.ShapeDtypeStruct((rows, feats), BF16),
            jax.ShapeDtypeStruct(part.shape, BF16),
            jax.ShapeDtypeStruct((n_w, feats), F32),
        ),
        in_specs=[hbm, vmem, vmem],
        out_specs=(vmem, vmem, vmem),
        scratch_shapes=[pltpu.VMEM(part.shape, BF16)]
        + reduce_col_scratch(n_yh, n_x, rows, feats)
        + [
            pltpu.VMEM((n_yh, n_x, n_core, n_w, feats), F32),
            pltpu.VMEM((n_yh, n_x, n_w, feats), F32),
            pltpu.VMEM((n_yh * n_x, n_w, feats), F32),
            pltpu.VMEM((3, n_w, feats), F32),
            pltpu.VMEM((NZ, n_w, feats), F32),
            pltpu.SemaphoreType.DMA((100,)),
            pltpu.SemaphoreType.DMA((100,)),
            pltpu.SemaphoreType.DMA((2,)),
        ],
        compiler_params=pltpu.CompilerParams(
            collective_id=2, has_side_effects=True, vmem_limit_bytes=48 << 20
        ),
        name="middle",
    )(part, weight, cot)


def reduce_row(s, p, part, ybuf, obuf, abuf, fbuf):
    rows = part.shape[1]
    cut = (rows * 7 // 16) // 16 * 16
    half = rows // 2
    cut_half = (cut * 4 // 7) // 16 * 16
    mine, other = p.yl, 1 - p.yl
    ways = ((1, p.right), (-1, p.left))
    last_own = {1: (0, half), -1: (half, rows)}
    last_cut = {1: (0, cut_half), -1: (cut_half, cut)}
    top = NZ // 2

    def blk(yl, hops, lo, hi):
        return part.at[p.at(yl, hops), pl.ds(lo, hi - lo)]

    for d, to in ways:
        lo, hi = last_cut[d]
        s.send(("a", d, top), blk(other, top, lo, hi), abuf.at[(top - 1) * 2 + int(d == 1), pl.ds(lo, hi - lo)], to)
    for k in (4, 3, -3, 2, -2, 1, -1, 0):
        s.send(("yb", k), blk(other, k, cut, rows), ybuf.at[k + 3], p.across)
    yield

    def crossed(k):
        s.wait(("yb", k), ybuf.at[k + 3], p.across)
        add_into(blk(mine, k, cut, rows), ybuf.at[k + 3])

    crossed(top)
    for d, to in ways:
        lo, hi = last_own[d]
        s.send(("o", d, top), blk(mine, top, lo, hi), obuf.at[(top - 1) * 2 + int(d == 1), pl.ds(lo, hi - lo)], to)
    for h in range(top - 1, 0, -1):
        yield
        for d, to in ways:
            lo, hi = last_cut[d] if h == top - 1 else (0, cut)
            got = abuf.at[h * 2 + int(d == 1), pl.ds(lo, hi - lo)]
            s.wait(("a", d, h + 1), got, to)
            add_into(blk(other, d * h, lo, hi), got)
            s.send(
                ("a", d, h), blk(other, d * h, 0, cut), abuf.at[(h - 1) * 2 + int(d == 1), pl.ds(0, cut)], to
            )
        for d, to in ways:
            crossed(d * h)
            lo, hi = last_own[d] if h == top - 1 else (0, rows)
            got = obuf.at[h * 2 + int(d == 1), pl.ds(lo, hi - lo)]
            s.wait(("o", d, h + 1), got, to)
            add_into(blk(mine, d * h, lo, hi), got)
            s.send(("o", d, h), blk(mine, d * h, 0, rows), obuf.at[(h - 1) * 2 + int(d == 1)], to)
    crossed(0)
    yield
    for d, to in ways:
        s.wait(("a", d, 1), abuf.at[int(d == 1), pl.ds(0, cut)], to)
    send = blk(other, 0, 0, cut)
    send[...] = (
        send[...].astype(F32) + abuf[0, pl.ds(0, cut)].astype(F32) + abuf[1, pl.ds(0, cut)].astype(F32)
    ).astype(BF16)
    s.send("fin", send, fbuf, p.across)
    for d, to in ways:
        s.wait(("o", d, 1), obuf.at[int(d == 1)], to)
    yield
    s.wait("fin", fbuf, p.across)


def gather_weight(s, p, tab):
    own = tab.at[p.yh, p.x, p.core]
    for dy, h in p.mates:
        s.send(("w", dy, h), own, own, p.mate(dy, h))
    yield
    yield
    yield
    for dy, h in p.mates:
        yh = p.yh + dy - 2 * p.yh * dy
        s.wait(("w", dy, h), tab.at[yh, p.xat(-h), p.core], p.sibling)
    s.send("ws", tab.at[:, :, p.core], tab.at[:, :, p.core], p.sibling)
    yield
    yield
    s.wait("ws", tab.at[:, :, 1 - p.core], p.sibling)


def last_kernel(part_ref, wg_ref, out_ref, wout_ref, part, ybuf, obuf, abuf, fbuf, send_sem, recv_sem, part_sems):
    rows, feats = out_ref.shape
    cut = fbuf.shape[0]
    p = RowPlace()
    c = ColPlace()
    loads = [
        pltpu.make_async_copy(part_ref.at[pl.ds(yl * NZ, NZ)], part.at[pl.ds(yl * NZ, NZ)], part_sems.at[n])
        for n, yl in enumerate((1 - p.yl, p.yl))
    ]
    for x in loads:
        x.start()
    s = Sender(send_sem, recv_sem)
    wout_ref[c.yh, c.x, c.core] = wg_ref[...]
    greet(p.peers + [c.sibling] + [c.mate(dy, h) for dy, h in c.mates])
    for x in loads:
        x.wait()
    drain(
        reduce_row(s, p, part, ybuf, obuf, abuf, fbuf),
        gather_weight(s, c, wout_ref),
    )
    me = p.at(p.yl, 0)
    total = part[me].astype(F32) + obuf[0].astype(F32) + obuf[1].astype(F32)
    out_ref[pl.ds(0, cut)] = (total[:cut] + fbuf[...].astype(F32)).astype(out_ref.dtype)
    out_ref[pl.ds(cut, rows - cut)] = total[cut:].astype(out_ref.dtype)
    s.finish()


def last(part, wg, shape5):
    n_row, rows, feats = part.shape
    cut = (rows * 7 // 16) // 16 * 16
    hbm = pl.BlockSpec(memory_space=pl.ANY)
    vmem = pl.BlockSpec(memory_space=pltpu.VMEM)
    n_yh, n_x, n_core = shape5
    return pl.pallas_call(
        last_kernel,
        out_shape=(
            jax.ShapeDtypeStruct((rows, feats), BF16),
            jax.ShapeDtypeStruct((n_yh, n_x, n_core) + wg.shape, F32),
        ),
        in_specs=[hbm, vmem],
        out_specs=(vmem, vmem),
        scratch_shapes=[
            pltpu.VMEM(part.shape, BF16),
            pltpu.VMEM((NZ, rows - cut, feats), BF16),
            pltpu.VMEM((NZ, rows, feats), BF16),
            pltpu.VMEM((NZ, cut, feats), BF16),
            pltpu.VMEM((cut, feats), BF16),
            pltpu.SemaphoreType.DMA((60,)),
            pltpu.SemaphoreType.DMA((60,)),
            pltpu.SemaphoreType.DMA((2,)),
        ],
        compiler_params=pltpu.CompilerParams(
            collective_id=3, has_side_effects=True, vmem_limit_bytes=48 << 20
        ),
        name="last",
    )(part, wg)


def per_device(node_features, tile_values, tile_rows, tile_cols, tile_count, weight, cotangent):
    rows, feats = node_features.shape[2:]
    edge = tile_values.shape[3]
    n_row = lax.axis_size("row")
    n_col = lax.axis_size("col")
    shape5 = (n_col // (2 * NX), NX, 2)
    tiles = tile_values[0, 0]
    table, plan = gather_row(node_features[0, 0], tile_rows, tile_cols, tile_count)
    table = table.reshape(n_row * rows // edge, edge, feats)
    part = sparse(False, plan, tiles, table)
    part = part.reshape(shape5 + (rows, feats))
    act, etab, wg = middle(part, weight, cotangent[0, 0], 1.0 / math.sqrt(rows * n_row * n_col))
    etab = etab.reshape(n_col * rows // edge, edge, feats)
    back = sparse(True, plan, tiles, etab)
    grad, wgrad = last(back.reshape(n_row, rows, feats), wg, shape5)
    return act[None, None], grad[None, None], wgrad.reshape(feats, feats)


def solution(mesh):
    in_specs = (
        P("col", "row", None, None),
        P("row", "col", None, None, None),
        P(),
        P(),
        P(),
        P(),
        P("row", "col", None, None),
    )
    out_specs = (P("row", "col", None, None), P("col", "row", None, None), P())
    return jax.shard_map(
        per_device, mesh=mesh, in_specs=in_specs, out_specs=out_specs, check_vma=False
    )
```

```python
import functools
import math

import jax
import jax.numpy as jnp
from jax import lax
from jax.experimental import pallas as pl
from jax.experimental.pallas import tpu as pltpu
from jax.sharding import PartitionSpec as P

MESH = pl.DeviceIdType.MESH
F32 = jnp.float32
BF16 = jnp.bfloat16

NZ = 8
NX = 4
TILE = 128
PLACES = 256


class Sender:
    def __init__(self, send_sem, recv_sem):
        self.send_sem = send_sem
        self.recv_sem = recv_sem
        self.ids = {}
        self.sent = []

    def slot(self, key):
        if key not in self.ids:
            self.ids[key] = len(self.ids)
        return self.ids[key]

    def copy(self, key, src, dst, device_id):
        n = self.slot(key)
        return pltpu.make_async_remote_copy(
            src_ref=src,
            dst_ref=dst,
            send_sem=self.send_sem.at[n],
            recv_sem=self.recv_sem.at[n],
            device_id=device_id,
            device_id_type=MESH,
        )

    def send(self, key, src, dst, device_id):
        c = self.copy(key, src, dst, device_id)
        c.start()
        self.sent.append(c)

    def wait(self, key, dst, device_id):
        self.copy(key, dst, dst, device_id).wait_recv()

    def finish(self):
        for c in self.sent:
            c.wait_send()
        self.sent = []


class RowPlace:
    def __init__(self):
        me = lax.axis_index("row")
        self.yl = me // NZ
        self.z = lax.rem(me, NZ)
        self.right = {"row": self.at(self.yl, 1)}
        self.left = {"row": self.at(self.yl, NZ - 1)}
        self.across = {"row": self.at(1 - self.yl, 0)}

    def zat(self, hops):
        return lax.rem(self.z + hops + NZ, NZ)

    def at(self, yl, hops):
        return yl * NZ + self.zat(hops)


class ColPlace:
    def __init__(self):
        me = lax.axis_index("col")
        self.yh = me // (2 * NX)
        self.x = lax.rem(me // 2, NX)
        self.core = lax.rem(me, 2)
        self.right = {"col": self.at(self.yh, 1, self.core)}
        self.left = {"col": self.at(self.yh, NX - 1, self.core)}
        self.across = {"col": self.at(1 - self.yh, 0, self.core)}
        self.sibling = {"col": self.at(self.yh, 0, 1 - self.core)}
        self.mates = [(dy, h) for dy in (0, 1) for h in range(NX) if (dy, h) != (0, 0)]

    def mate(self, dy, h):
        return {"col": self.at(self.yh + dy - 2 * self.yh * dy, h, self.core)}

    def xat(self, hops):
        return lax.rem(self.x + hops + NX, NX)

    def at(self, yh, hops, core):
        return (yh * NX + self.xat(hops)) * 2 + core


def order_slots(rows, cols, live, n_tiles, plan):
    slots = rows.shape[1]
    places = plan.shape[1]
    steps = (slots + n_tiles) // 2
    sub = lax.broadcasted_iota(jnp.int32, (slots, slots), 0)
    lane = lax.broadcasted_iota(jnp.int32, (slots, slots), 1)
    k_col = sub[:, :1]
    live_row, live_col = lane[:1] < live, sub[:, :1] < live
    tile = lax.broadcasted_iota(jnp.int32, (n_tiles, slots), 0)
    place = lax.broadcasted_iota(jnp.int32, (slots, places), 1)
    tile_sub = lax.broadcasted_iota(jnp.int32, (n_tiles, places), 0)
    tile_lane = lax.broadcasted_iota(jnp.int32, (n_tiles, places), 1)

    def turn(row):
        return jnp.sum(jnp.where(sub == lane, row, 0), axis=1, keepdims=True)

    out = []
    for key, source in ((rows, cols), (cols, rows)):
        same = (turn(key) == key) & (sub < lane) & live_col
        rank = jnp.sum(jnp.where(same, 1, 0), axis=0, keepdims=True)
        number = jnp.sum(jnp.where((tile == key) & live_row, 1, 0), axis=1, keepdims=True)
        pairs = (number + 1) >> 1
        base = 2 * jnp.sum(jnp.where(tile < key, pairs, 0), axis=0, keepdims=True)
        at = turn(jnp.where(live_row, base + rank, -1))
        hit = at == place
        slot = slots + jnp.sum(jnp.where(hit, k_col - slots, 0), axis=0, keepdims=True)
        read = jnp.sum(jnp.where(hit, turn(source), 0), axis=0, keepdims=True)
        fresh = jnp.sum(jnp.where(hit & (turn(rank) == 0), 1, 0), axis=0, keepdims=True)
        upto = jnp.sum(jnp.where(tile_sub <= tile_lane, pairs, 0), axis=0, keepdims=True)
        some = jnp.sum(jnp.where(tile_sub == tile_lane, number, 0), axis=0, keepdims=True)
        final = jnp.where(some > 0, upto - 1, steps)
        out += [slot, read, fresh, final]
    for n, x in enumerate(out):
        plan[pl.ds(n, 1)] = x


GROUP = 16


def multiply(flip, plan, tiles, tab, stash):
    steps = stash.shape[0] - 1
    first = 4 if flip else 0
    side = 0 if flip else 1
    shape = stash.shape[1:]

    def some(g, acc):
        for u in range(GROUP):
            p = g * GROUP + u
            k = [plan[first, 2 * p + i] for i in (0, 1)]
            q = [plan[first + 1, 2 * p + i] for i in (0, 1)]
            left = jnp.concatenate([tiles[i] for i in k], axis=side)
            right = jnp.concatenate([tab[i] for i in q], axis=0)
            prod = lax.dot_general(left, right, (((side,), (0,)), ((), ())), preferred_element_type=F32)
            fresh = plan[first + 2, 2 * p] == 1
            acc = jnp.where(fresh, 0.0, acc) + prod
            stash[p] = acc.astype(stash.dtype)
        return acc

    lax.fori_loop(0, steps // GROUP, some, jnp.zeros(shape, F32))
    stash[steps] = jnp.zeros(shape, stash.dtype)


def add_into(dst, *terms):
    total = dst[...].astype(F32)
    for t in terms:
        total = total + t[...].astype(F32)
    dst[...] = total.astype(dst.dtype)


def cut_of(rows):
    return (rows * 7 // 16) // 16 * 16


def gather_row(s, p, tag, tab):
    rows = tab.shape[2]
    cut = cut_of(rows)
    top = NZ // 2
    mine, other = p.yl, 1 - p.yl
    ways = ((1, p.right), (-1, p.left))
    a_, b_ = pl.ds(0, cut), pl.ds(cut, rows - cut)
    a_last = {1: pl.ds(0, cut // 2 // 16 * 16 + 16), -1: pl.ds(cut // 2 // 16 * 16 + 16, cut - cut // 2 // 16 * 16 - 16)}
    b_half = (rows - cut) // 2 // 16 * 16
    b_last = {1: pl.ds(cut, b_half), -1: pl.ds(cut + b_half, rows - cut - b_half)}

    def blk(yl, h, ds):
        return tab.at[yl, p.zat(h), ds]

    def pair(h, ds):
        return tab.at[:, p.zat(h), ds]

    def push(key, b, to):
        s.send((tag,) + key, b, b, to)

    push(("ya",), blk(mine, 0, a_), p.across)
    for d, to in ways:
        push(("b", d, 1), blk(mine, 0, b_), to)
    push(("yb", 0), blk(mine, 0, b_), p.across)
    yield
    s.wait((tag, "ya"), blk(other, 0, a_), p.across)
    for d, to in ways:
        push(("a", d, 1), pair(0, a_), to)
    for h in range(1, top + 1):
        yield
        for d, to in ways:
            s.wait((tag, "b", d, h), blk(mine, -d * h, b_last[d] if h == top else b_), to)
            if h < top:
                push(("b", d, h + 1), blk(mine, -d * h, b_last[d] if h == top - 1 else b_), to)
                push(("yb", -d * h), blk(mine, -d * h, b_), p.across)
        if h == top:
            push(("yb", top), blk(mine, top, b_), p.across)
        yield
        for d, to in ways:
            s.wait((tag, "a", d, h), pair(-d * h, a_last[d] if h == top else a_), to)
            if h < top:
                push(("a", d, h + 1), pair(-d * h, a_last[d] if h == top - 1 else a_), to)
    yield
    for h in [0] + [d * h for h in range(1, top) for d in (1, -1)] + [top]:
        s.wait((tag, "yb", h), blk(other, h, b_), p.across)


def reduce_row(s, p, tag, part, ybuf, abuf, bbuf, fbuf):
    rows = part.shape[2]
    cut = cut_of(rows)
    top = NZ // 2
    mine, other = p.yl, 1 - p.yl
    ways = ((1, p.right, 0), (-1, p.left, 1))
    a_, b_ = pl.ds(0, cut), pl.ds(cut, rows - cut)
    a_mid = cut // 2 // 16 * 16 + 16
    b_mid = (rows - cut) // 2 // 16 * 16
    a_last = {1: (0, a_mid), -1: (a_mid, cut)}
    b_last = {1: (0, b_mid), -1: (b_mid, rows - cut)}

    def a_cut(d, h):
        lo, hi = a_last[d] if h == top else (0, cut)
        return pl.ds(lo, hi - lo)

    def b_cut(d, h, base=0):
        lo, hi = b_last[d] if h == top else (0, rows - cut)
        return pl.ds(base + lo, hi - lo)

    for h in [top] + [d * h for h in range(top - 1, 0, -1) for d in (1, -1)] + [0]:
        s.send((tag, "yb", h), part.at[other, p.zat(h), b_], ybuf.at[h + top - 1], p.across)
        if h == top:
            for d, to, n in ways:
                ds = a_cut(d, top)
                s.send((tag, "a", d, top), part.at[:, p.zat(top), ds], abuf.at[top - 1, n, :, ds], to)
    for h in range(top, 0, -1):
        yield
        for d, to, n in ways:
            if h < top:
                ds = a_cut(d, h + 1)
                got = abuf.at[h, n, :, ds]
                s.wait((tag, "a", d, h + 1), got, to)
                add_into(part.at[:, p.zat(d * h), ds], got)
                s.send((tag, "a", d, h), part.at[:, p.zat(d * h), a_], abuf.at[h - 1, n], to)
        yield
        for d, to, n in ways:
            if h < top or d == 1:
                s.wait((tag, "yb", d * h), ybuf.at[d * h + top - 1], p.across)
                add_into(part.at[mine, p.zat(d * h), b_], ybuf.at[d * h + top - 1])
            if h < top:
                got = bbuf.at[h, n, b_cut(d, h + 1)]
                s.wait((tag, "b", d, h + 1), got, to)
                add_into(part.at[mine, p.zat(d * h), b_cut(d, h + 1, cut)], got)
            ds = b_cut(d, h)
            s.send((tag, "b", d, h), part.at[mine, p.zat(d * h), b_cut(d, h, cut)], bbuf.at[h - 1, n, ds], to)
    yield
    for d, to, n in ways:
        s.wait((tag, "a", d, 1), abuf.at[0, n], to)
    add_into(part.at[:, p.z, a_], abuf.at[0, 0], abuf.at[0, 1])
    s.send((tag, "f"), part.at[other, p.z, a_], fbuf, p.across)
    s.wait((tag, "yb", 0), ybuf.at[top - 1], p.across)
    yield
    for d, to, n in ways:
        s.wait((tag, "b", d, 1), bbuf.at[0, n], to)
    add_into(part.at[mine, p.z, b_], ybuf.at[top - 1], bbuf.at[0, 0], bbuf.at[0, 1])
    yield
    s.wait((tag, "f"), fbuf, p.across)
    add_into(part.at[mine, p.z, a_], fbuf)


def reduce_row_scratch(rows, feats):
    cut, top = cut_of(rows), NZ // 2
    return [
        pltpu.VMEM((NZ, rows - cut, feats), BF16),
        pltpu.VMEM((top, 2, 2, cut, feats), BF16),
        pltpu.VMEM((top, 2, rows - cut, feats), BF16),
        pltpu.VMEM((cut, feats), BF16),
    ]


def reduce_col(s, p, tag, part, cbuf, xa2, xa1, xb2, xb1, yb, ya):
    rows = part.shape[3]
    half = rows // 2
    qr = half // 2
    a_, b_ = pl.ds(0, half), pl.ds(half, half)
    mine, other, core, sib = p.yh, 1 - p.yh, p.core, 1 - p.core
    ways = ((1, p.right, 0), (-1, p.left, 1))

    def cuts(n, base):
        return pl.ds(base + n * qr, qr)

    def whole(h):
        return cbuf.at[:, p.xat(h)]

    for h in (2, 1, -1, 0):
        s.send((tag, "c", h), part.at[:, p.xat(h), sib], whole(h), p.sibling)
    yield
    for h in (2, 1, -1):
        s.wait((tag, "c", h), whole(h), p.sibling)
        add_into(part.at[:, p.xat(h), core], whole(h))
        s.send((tag, "yb", h), part.at[other, p.xat(h), core, b_], yb.at[h % NX], p.across)
        if h == 2:
            for d, to, n in ways:
                s.send((tag, "xa2", d), part.at[:, p.xat(2), core, cuts(n, 0)], xa2.at[:, cuts(n, 0)], to)
    s.wait((tag, "c", 0), whole(0), p.sibling)
    add_into(part.at[:, p.x, core], whole(0))
    s.send((tag, "yb", 0), part.at[other, p.x, core, b_], yb.at[0], p.across)
    yield
    s.wait((tag, "yb", 2), yb.at[2], p.across)
    add_into(part.at[mine, p.xat(2), core, b_], yb.at[2])
    for d, to, n in ways:
        s.send((tag, "xb2", d), part.at[mine, p.xat(2), core, cuts(n, half)], xb2.at[cuts(n, 0)], to)
    yield
    for d, to, n in ways:
        s.wait((tag, "xa2", d), xa2.at[:, cuts(n, 0)], to)
        add_into(part.at[:, p.xat(d), core, cuts(n, 0)], xa2.at[:, cuts(n, 0)])
        s.send((tag, "xa1", d), part.at[:, p.xat(d), core, a_], xa1.at[n], to)
    yield
    for d, to, n in ways:
        s.wait((tag, "yb", d), yb.at[d % NX], p.across)
        add_into(part.at[mine, p.xat(d), core, b_], yb.at[d % NX])
        s.wait((tag, "xb2", d), xb2.at[cuts(n, 0)], to)
        add_into(part.at[mine, p.xat(d), core, cuts(n, half)], xb2.at[cuts(n, 0)])
        s.send((tag, "xb1", d), part.at[mine, p.xat(d), core, b_], xb1.at[n], to)
    yield
    for d, to, n in ways:
        s.wait((tag, "xa1", d), xa1.at[n], to)
    add_into(part.at[:, p.x, core, a_], xa1.at[0], xa1.at[1])
    s.send((tag, "ya"), part.at[other, p.x, core, a_], ya, p.across)
    s.wait((tag, "yb", 0), yb.at[0], p.across)
    yield
    for d, to, n in ways:
        s.wait((tag, "xb1", d), xb1.at[n], to)
    add_into(part.at[mine, p.x, core, b_], yb.at[0], xb1.at[0], xb1.at[1])
    yield
    s.wait((tag, "ya"), ya, p.across)
    add_into(part.at[mine, p.x, core, a_], ya)


def reduce_col_scratch(n_yh, n_x, rows, feats):
    half = rows // 2
    return [
        pltpu.VMEM((n_yh, n_x, rows, feats), BF16),
        pltpu.VMEM((n_yh, half, feats), BF16),
        pltpu.VMEM((2, n_yh, half, feats), BF16),
        pltpu.VMEM((half, feats), BF16),
        pltpu.VMEM((2, half, feats), BF16),
        pltpu.VMEM((n_x, half, feats), BF16),
        pltpu.VMEM((half, feats), BF16),
    ]


def gather_col(s, p, tag, tab):
    rows = tab.shape[3]
    half = rows // 2
    qr = half // 2
    a_, b_ = pl.ds(0, half), pl.ds(half, half)
    mine, other, core = p.yh, 1 - p.yh, p.core
    ways = ((1, p.right, 0), (-1, p.left, 1))

    def blk(yh, h, ds):
        return tab.at[yh, p.xat(h), core, ds]

    def pair(h, ds):
        return tab.at[:, p.xat(h), core, ds]

    def push(key, b, to):
        s.send((tag,) + key, b, b, to)

    def took(key, b):
        s.wait((tag,) + key, b, p.sibling)

    push(("ya",), blk(mine, 0, a_), p.across)
    for d, to, n in ways:
        push(("b", d), blk(mine, 0, b_), to)
    push(("yb", 0), blk(mine, 0, b_), p.across)
    yield
    took(("ya",), blk(other, 0, a_))
    for d, to, n in ways:
        push(("a", d), pair(0, a_), to)
    push(("c", 0, "a"), pair(0, a_), p.sibling)
    yield
    for d, to, n in ways:
        took(("b", d), blk(mine, -d, b_))
        push(("b2", d), blk(mine, -d, pl.ds(half + n * qr, qr)), to)
        push(("yb", -d), blk(mine, -d, b_), p.across)
    yield
    for d, to, n in ways:
        took(("a", d), pair(-d, a_))
        push(("a2", d), pair(-d, pl.ds(n * qr, qr)), to)
        push(("c", -d, "a"), pair(-d, a_), p.sibling)
    took(("yb", 0), blk(other, 0, b_))
    push(("c", 0, "b"), pair(0, b_), p.sibling)
    yield
    for d, to, n in ways:
        took(("b2", d), blk(mine, 2, pl.ds(half + n * qr, qr)))
    push(("yb", 2), blk(mine, 2, b_), p.across)
    yield
    for d in (1, -1):
        took(("yb", d), blk(other, d, b_))
        push(("c", d, "b"), pair(d, b_), p.sibling)
    yield
    for d, to, n in ways:
        took(("a2", d), pair(2, pl.ds(n * qr, qr)))
    push(("c", 2, "a"), pair(2, a_), p.sibling)
    took(("yb", 2), blk(other, 2, b_))
    push(("c", 2, "b"), pair(2, b_), p.sibling)
    yield
    for h in (0, 1, -1, 2):
        for name, ds in (("a", a_), ("b", b_)):
            s.wait((tag, "c", h, name), tab.at[:, p.xat(h), 1 - core, ds], p.sibling)


def sum_weight(s, p, q, wpart, wc, wd, wy, wz, wtab, scale):
    core, sib = p.core, 1 - p.core
    s.send("wc", wpart.at[:, :, sib], wc, p.sibling)
    yield
    s.wait("wc", wc, p.sibling)
    mine = wpart.at[:, :, core]
    mine[...] = mine[...] + wc[...]
    for dy, h in p.mates:
        yh = p.yh + dy - 2 * p.yh * dy
        s.send(("wd", dy, h), wpart.at[yh, p.xat(h), core], wd.at[dy * NX + h], p.mate(dy, h))
    yield
    total = wpart[p.yh, p.x, core]
    for dy, h in p.mates:
        s.wait(("wd", dy, h), wd.at[dy * NX + h], p.mate(dy, h))
        total = total + wd[dy * NX + h]
    wy[0] = total
    s.send("wy", wy.at[0], wy.at[1], q.across)
    yield
    s.wait("wy", wy.at[1], q.across)
    wz[q.z] = wy[0] + wy[1]
    for h in range(1, NZ):
        s.send(("wz", h), wz.at[q.z], wz.at[q.z], {"row": q.at(q.yl, h)})
    yield
    for h in range(1, NZ):
        s.wait(("wz", h), wz.at[q.zat(-h)], q.across)
    total = wz[0]
    for z in range(1, NZ):
        total = total + wz[z]
    own = wtab.at[p.yh, p.x, core]
    own[...] = total * scale
    for dy, h in p.mates:
        s.send(("w", dy, h), own, own, p.mate(dy, h))
    yield
    for dy, h in p.mates:
        yh = p.yh + dy - 2 * p.yh * dy
        s.wait(("w", dy, h), wtab.at[yh, p.xat(-h), core], p.sibling)
    s.send("ws", wtab.at[:, :, core], wtab.at[:, :, core], p.sibling)
    yield
    s.wait("ws", wtab.at[:, :, sib], p.sibling)


def drain(steps):
    for _ in steps:
        pass


def layer_kernel(
    scale, x_ref, tiles_ref, tr_ref, tc_ref, cnt_ref, w_ref, g_ref, act_ref, grad_ref, wg_ref,
    xtab, etab, tiles, stash, part, back, plan, splan, tr, tc, cnt, w, g, act, wpart, wc, wd, wy, wz, wtab, *rest,
):
    n_col, n_row = 7, 4
    for_col, for_row, (send_sem, recv_sem, sems) = rest[:n_col], rest[n_col : n_col + n_row], rest[n_col + n_row :]
    slots, edge, _ = tiles_ref.shape
    rows, feats = x_ref.shape
    per = rows // edge
    p, q = ColPlace(), RowPlace()
    mr, mc = lax.axis_index("row"), lax.axis_index("col")

    barrier = pltpu.get_barrier_semaphore()
    peers = [p.sibling, q.across] + [p.mate(dy, h) for dy, h in p.mates]
    peers += [{"row": q.at(q.yl, h)} for h in range(1, NZ)]
    for peer in peers:
        pl.semaphore_signal(barrier, inc=1, device_id=peer, device_id_type=MESH)
    loads = [
        pltpu.make_async_copy(tr_ref.at[mr], tr, sems.at[0]),
        pltpu.make_async_copy(tc_ref.at[mr], tc, sems.at[1]),
        pltpu.make_async_copy(cnt_ref, cnt, sems.at[2]),
        pltpu.make_async_copy(x_ref, xtab.at[q.yl, q.z], sems.at[3]),
        pltpu.make_async_copy(tiles_ref, tiles.at[pl.ds(0, slots)], sems.at[4]),
        pltpu.make_async_copy(w_ref, w, sems.at[5]),
        pltpu.make_async_copy(g_ref, g, sems.at[6]),
    ]
    for c in loads:
        c.start()
    tiles[slots] = jnp.zeros((edge, edge), tiles.dtype)
    loads[3].wait()
    pl.semaphore_wait(barrier, len(peers))

    s = Sender(send_sem, recv_sem)
    gather = gather_row(s, q, "gr", xtab)
    next(gather)
    for c in loads[:3]:
        c.wait()
    n_tiles = stash.shape[0] * 2 - 2 - slots
    order_slots(tr[pl.ds(mc, 1)], tc[pl.ds(mc, 1)], cnt[mr, mc], n_tiles, plan)
    to_scalars = pltpu.make_async_copy(plan, splan, sems.at[7])
    to_scalars.start()
    drain(gather)
    to_scalars.wait()
    for c in loads[4:]:
        c.wait()

    multiply(False, splan, tiles, xtab.reshape(n_tiles, edge, feats), stash)
    for t in range(n_tiles):
        b = t // per
        part[b // (2 * NX), b // 2 % NX, b % 2, pl.ds(t % per * edge, edge)] = stash[splan[3, t]]
    drain(reduce_col(s, p, "rc", part, *for_col))

    agg = part[p.yh, p.x, p.core]
    pre = jnp.dot(agg, w[...], preferred_element_type=F32)
    logistic = jax.nn.sigmoid(pre)
    upstream = g[...].astype(F32)
    d_pre = (upstream * logistic * (1.0 + pre * (1.0 - logistic))).astype(BF16)
    e = lax.dot_general(d_pre, w[...], (((1,), (1,)), ((), ())), preferred_element_type=F32)
    etab[p.yh, p.x, p.core] = e.astype(BF16)
    gather = gather_col(s, p, "gc", etab)
    next(gather)
    act[...] = (pre * logistic).astype(BF16)
    act_out = pltpu.make_async_copy(act, act_ref, sems.at[8])
    act_out.start()
    wg = lax.dot_general(agg, d_pre, (((0,), (0,)), ((), ())), preferred_element_type=F32)
    wpart[...] = wg.reshape(wpart.shape)
    weights = sum_weight(s, p, q, wpart, wc, wd, wy, wz, wtab, scale)
    next(weights)
    next(gather)
    next(gather)
    next(weights)
    drain(gather)
    next(weights)

    multiply(True, splan, tiles, etab.reshape(n_tiles, edge, feats), stash)
    next(weights)
    for t in range(n_tiles):
        b = t // per
        back[b // NZ, b % NZ, pl.ds(t % per * edge, edge)] = stash[splan[7, t]]
    reduce = reduce_row(s, q, "rr", back, *for_row)
    for _ in range(4):
        next(reduce)
    next(weights)
    for _ in range(3):
        next(reduce)
    next(weights)
    drain(reduce)
    grad_out = pltpu.make_async_copy(back.at[q.yl, q.z], grad_ref, sems.at[9])
    grad_out.start()
    drain(weights)
    wg_out = pltpu.make_async_copy(wtab, wg_ref, sems.at[10])
    wg_out.start()
    s.finish()
    for c in (act_out, grad_out, wg_out):
        c.wait()


def layer(x, tiles, tile_rows, tile_cols, tile_count, weight, cot):
    rows, feats = x.shape
    slots, edge, _ = tiles.shape
    n_row, n_col, _ = tile_rows.shape
    n_yh = n_col // (2 * NX)
    n_tiles = n_col * rows // edge
    steps = (slots + n_tiles) // 2
    n_w = feats // n_col
    hbm = pl.BlockSpec(memory_space=pl.ANY)
    vmem = pltpu.VMEM
    return pl.pallas_call(
        functools.partial(layer_kernel, 1.0 / math.sqrt(rows * n_row * n_col)),
        out_shape=(
            jax.ShapeDtypeStruct((rows, feats), BF16),
            jax.ShapeDtypeStruct((rows, feats), BF16),
            jax.ShapeDtypeStruct((n_yh, NX, 2, n_w, feats), F32),
        ),
        in_specs=[hbm] * 7,
        out_specs=(hbm, hbm, hbm),
        scratch_shapes=[
            vmem((n_row // NZ, NZ, rows, feats), BF16),
            vmem((n_yh, NX, 2, rows, feats), BF16),
            vmem((slots + 1, edge, edge), BF16),
            vmem((steps + 1, edge, feats), BF16),
            vmem((n_yh, NX, 2, rows, feats), BF16),
            vmem((n_row // NZ, NZ, rows, feats), BF16),
            vmem((8, PLACES), jnp.int32),
            pltpu.SMEM((8, PLACES), jnp.int32),
            vmem((n_col, slots), jnp.int32),
            vmem((n_col, slots), jnp.int32),
            pltpu.SMEM((n_row, n_col), jnp.int32),
            vmem((feats, feats), BF16),
            vmem((rows, feats), BF16),
            vmem((rows, feats), BF16),
            vmem((n_yh, NX, 2, n_w, feats), F32),
            vmem((n_yh, NX, n_w, feats), F32),
            vmem((n_yh * NX, n_w, feats), F32),
            vmem((2, n_w, feats), F32),
            vmem((NZ, n_w, feats), F32),
            vmem((n_yh, NX, 2, n_w, feats), F32),
        ]
        + reduce_col_scratch(n_yh, NX, rows, feats)
        + reduce_row_scratch(rows, feats)
        + [
            pltpu.SemaphoreType.DMA((200,)),
            pltpu.SemaphoreType.DMA((200,)),
            pltpu.SemaphoreType.DMA((11,)),
        ],
        compiler_params=pltpu.CompilerParams(
            collective_id=1, has_side_effects=True, vmem_limit_bytes=56 << 20
        ),
        name="layer",
    )(x, tiles, tile_rows, tile_cols, tile_count, weight, cot)


def per_device(node_features, tile_values, tile_rows, tile_cols, tile_count, weight, cotangent):
    act, grad, wgrad = layer(
        node_features[0, 0], tile_values[0, 0], tile_rows, tile_cols, tile_count, weight, cotangent[0, 0]
    )
    return act[None, None], grad[None, None], wgrad.reshape(weight.shape)


def solution(mesh):
    in_specs = (
        P("col", "row", None, None),
        P("row", "col", None, None, None),
        P(),
        P(),
        P(),
        P(),
        P("row", "col", None, None),
    )
    out_specs = (P("row", "col", None, None), P("col", "row", None, None), P())
    return jax.shard_map(
        per_device, mesh=mesh, in_specs=in_specs, out_specs=out_specs, check_vma=False
    )
```

```python
import functools
import math

import jax
import jax.numpy as jnp
from jax import lax
from jax.experimental import pallas as pl
from jax.experimental.pallas import tpu as pltpu
from jax.sharding import PartitionSpec as P

MESH = pl.DeviceIdType.MESH
F32 = jnp.float32
BF16 = jnp.bfloat16

NZ = 8
NX = 4
TILE = 128
PLACES = 256


class Sender:
    def __init__(self, send_sem, recv_sem):
        self.send_sem = send_sem
        self.recv_sem = recv_sem
        self.ids = {}
        self.sent = []

    def slot(self, key):
        if key not in self.ids:
            self.ids[key] = len(self.ids)
        return self.ids[key]

    def copy(self, key, src, dst, device_id):
        n = self.slot(key)
        return pltpu.make_async_remote_copy(
            src_ref=src,
            dst_ref=dst,
            send_sem=self.send_sem.at[n],
            recv_sem=self.recv_sem.at[n],
            device_id=device_id,
            device_id_type=MESH,
        )

    def send(self, key, src, dst, device_id):
        c = self.copy(key, src, dst, device_id)
        c.start()
        self.sent.append(c)

    def wait(self, key, dst, device_id):
        self.copy(key, dst, dst, device_id).wait_recv()

    def finish(self):
        for c in self.sent:
            c.wait_send()
        self.sent = []


class RowPlace:
    def __init__(self):
        me = lax.axis_index("row")
        self.yl = me // NZ
        self.z = lax.rem(me, NZ)
        self.right = {"row": self.at(self.yl, 1)}
        self.left = {"row": self.at(self.yl, NZ - 1)}
        self.across = {"row": self.at(1 - self.yl, 0)}

    def zat(self, hops):
        return lax.rem(self.z + hops + NZ, NZ)

    def at(self, yl, hops):
        return yl * NZ + self.zat(hops)


class ColPlace:
    def __init__(self):
        me = lax.axis_index("col")
        self.yh = me // (2 * NX)
        self.x = lax.rem(me // 2, NX)
        self.core = lax.rem(me, 2)
        self.right = {"col": self.at(self.yh, 1, self.core)}
        self.left = {"col": self.at(self.yh, NX - 1, self.core)}
        self.across = {"col": self.at(1 - self.yh, 0, self.core)}
        self.sibling = {"col": self.at(self.yh, 0, 1 - self.core)}
        self.mates = [(dy, h) for dy in (0, 1) for h in range(NX) if (dy, h) != (0, 0)]

    def mate(self, dy, h):
        return {"col": self.at(self.yh + dy - 2 * self.yh * dy, h, self.core)}

    def xat(self, hops):
        return lax.rem(self.x + hops + NX, NX)

    def at(self, yh, hops, core):
        return (yh * NX + self.xat(hops)) * 2 + core


def order_slots(rows, cols, live, n_tiles, plan):
    slots = rows.shape[1]
    places = plan.shape[1]
    steps = (slots + n_tiles) // 2
    sub = lax.broadcasted_iota(jnp.int32, (slots, slots), 0)
    lane = lax.broadcasted_iota(jnp.int32, (slots, slots), 1)
    k_col = sub[:, :1]
    live_row, live_col = lane[:1] < live, sub[:, :1] < live
    tile = lax.broadcasted_iota(jnp.int32, (n_tiles, slots), 0)
    place = lax.broadcasted_iota(jnp.int32, (slots, places), 1)
    tile_sub = lax.broadcasted_iota(jnp.int32, (n_tiles, places), 0)
    tile_lane = lax.broadcasted_iota(jnp.int32, (n_tiles, places), 1)

    def turn(row):
        return jnp.sum(jnp.where(sub == lane, row, 0), axis=1, keepdims=True)

    out = []
    for key, source in ((rows, cols), (cols, rows)):
        same = (turn(key) == key) & (sub < lane) & live_col
        rank = jnp.sum(jnp.where(same, 1, 0), axis=0, keepdims=True)
        number = jnp.sum(jnp.where((tile == key) & live_row, 1, 0), axis=1, keepdims=True)
        pairs = (number + 1) >> 1
        base = 2 * jnp.sum(jnp.where(tile < key, pairs, 0), axis=0, keepdims=True)
        at = turn(jnp.where(live_row, base + rank, -1))
        hit = at == place
        slot = slots + jnp.sum(jnp.where(hit, k_col - slots, 0), axis=0, keepdims=True)
        read = jnp.sum(jnp.where(hit, turn(source), 0), axis=0, keepdims=True)
        fresh = jnp.sum(jnp.where(hit & (turn(rank) == 0), 1, 0), axis=0, keepdims=True)
        upto = jnp.sum(jnp.where(tile_sub <= tile_lane, pairs, 0), axis=0, keepdims=True)
        some = jnp.sum(jnp.where(tile_sub == tile_lane, number, 0), axis=0, keepdims=True)
        final = jnp.where(some > 0, upto - 1, steps)
        out += [slot, read, fresh, final]
    for n, x in enumerate(out):
        plan[pl.ds(n, 1)] = x


GROUP = 28


def multiply(flip, plan, tiles, tab, stash):
    steps = stash.shape[0] - 1
    first = 4 if flip else 0
    side = 0 if flip else 1
    shape = stash.shape[1:]

    def some(g, acc):
        for u in range(GROUP):
            p = g * GROUP + u
            k = [plan[first, 2 * p + i] for i in (0, 1)]
            q = [plan[first + 1, 2 * p + i] for i in (0, 1)]
            left = jnp.concatenate([tiles[i] for i in k], axis=side)
            right = jnp.concatenate([tab[i] for i in q], axis=0)
            prod = lax.dot_general(left, right, (((side,), (0,)), ((), ())), preferred_element_type=F32)
            fresh = plan[first + 2, 2 * p] == 1
            acc = jnp.where(fresh, 0.0, acc) + prod
            stash[p] = acc.astype(stash.dtype)
        return acc

    lax.fori_loop(0, steps // GROUP, some, jnp.zeros(shape, F32))
    stash[steps] = jnp.zeros(shape, stash.dtype)


def add_into(dst, *terms):
    total = dst[...].astype(F32)
    for t in terms:
        total = total + t[...].astype(F32)
    dst[...] = total.astype(dst.dtype)


def row_parts(rows):
    cut = (rows * 7 // 16) // 16 * 16
    rest = rows - cut
    return (0, cut, cut // 2 // 16 * 16), (cut, rest, -(-rest // 2 // 16) * 16)


def hop_rows(part, d, h):
    base, n, half = part
    if h < NZ // 2:
        return base, n
    return (base, half) if d == 1 else (base + half, n - half)


def gather_row(s, p, tag, tab):
    first, rest = row_parts(tab.shape[2])
    top = NZ // 2
    mine, other = p.yl, 1 - p.yl
    ways = ((1, p.right), (-1, p.left))

    def blk(yl, h, ds):
        return tab.at[yl, p.zat(h), pl.ds(*ds)]

    def push(key, b, to):
        s.send((tag,) + key, b, b, to)

    streams = (("b", mine, rest), ("a", mine, first), ("c", other, first))

    def hop(name, yl, part, h):
        for d, to in ways:
            push((name, d, h), blk(yl, d * (1 - h), hop_rows(part, d, h)), to)

    push(("ya",), blk(mine, 0, first[:2]), p.across)
    for name, yl, part in streams[:2]:
        hop(name, yl, part, 1)
    push(("yb", 0), blk(mine, 0, rest[:2]), p.across)
    yield
    s.wait((tag, "ya"), blk(other, 0, first[:2]), p.across)
    hop(*streams[2], 1)
    for h in range(1, top + 1):
        for name, yl, part in streams:
            yield
            for d, to in ways:
                s.wait((tag, name, d, h), blk(yl, -d * h, hop_rows(part, d, h)), to)
                if h < top:
                    push((name, d, h + 1), blk(yl, -d * h, hop_rows(part, d, h + 1)), to)
                if name == "b" and (h < top or d == -1):
                    push(("yb", -d * h), blk(mine, -d * h, rest[:2]), p.across)
    yield
    for h in [0] + [d * h for h in range(1, top) for d in (1, -1)] + [top]:
        s.wait((tag, "yb", h), blk(other, h, rest[:2]), p.across)


def reduce_row(s, p, tag, part, ybuf, abuf, cbuf, bbuf, fbuf):
    first, rest = row_parts(part.shape[2])
    top = NZ // 2
    mine, other = p.yl, 1 - p.yl
    ways = ((1, p.right, 0), (-1, p.left, 1))
    streams = (("c", other, first, cbuf), ("a", mine, first, abuf), ("b", mine, rest, bbuf))

    def blk(yl, h, ds):
        return part.at[yl, p.zat(h), pl.ds(*ds)]

    def hop(name, yl, piece, buf, d, to, n, h):
        lo, m = hop_rows(piece, d, h)
        s.send((tag, name, d, h), blk(yl, d * h, (lo, m)), buf.at[h - 1, n, pl.ds(lo - piece[0], m)], to)

    def crossed(h):
        s.wait((tag, "yb", h), ybuf.at[h + top - 1], p.across)
        add_into(blk(mine, h, rest[:2]), ybuf.at[h + top - 1])

    s.send((tag, "yb", top), blk(other, top, rest[:2]), ybuf.at[2 * top - 1], p.across)
    for st in streams[:2]:
        for w in ways:
            hop(*st, *w, top)
    for h in [d * h for h in range(top - 1, 0, -1) for d in (1, -1)] + [0]:
        s.send((tag, "yb", h), blk(other, h, rest[:2]), ybuf.at[h + top - 1], p.across)
    yield
    crossed(top)
    for w in ways:
        hop(*streams[2], *w, top)
    for h in range(top - 1, 0, -1):
        for name, yl, piece, buf in streams:
            yield
            for d, to, n in ways:
                if name == "b":
                    crossed(d * h)
                lo, m = hop_rows(piece, d, h + 1)
                got = buf.at[h, n, pl.ds(lo - piece[0], m)]
                s.wait((tag, name, d, h + 1), got, to)
                add_into(blk(yl, d * h, (lo, m)), got)
                hop(name, yl, piece, buf, d, to, n, h)
    for name, yl, piece, buf in streams:
        yield
        for d, to, n in ways:
            s.wait((tag, name, d, 1), buf.at[0, n], to)
        if name == "b":
            crossed(0)
        add_into(blk(yl, 0, piece[:2]), buf.at[0, 0], buf.at[0, 1])
        if name == "c":
            s.send((tag, "f"), blk(other, 0, first[:2]), fbuf, p.across)
    yield
    s.wait((tag, "f"), fbuf, p.across)
    add_into(blk(mine, 0, first[:2]), fbuf)


def reduce_row_scratch(rows, feats):
    (_, m, _), (_, n, _) = row_parts(rows)
    top = NZ // 2
    return [
        pltpu.VMEM((NZ, n, feats), BF16),
        pltpu.VMEM((top, 2, m, feats), BF16),
        pltpu.VMEM((top, 2, m, feats), BF16),
        pltpu.VMEM((top, 2, n, feats), BF16),
        pltpu.VMEM((m, feats), BF16),
    ]


def col_parts(rows):
    na = rows * 3 // 8 // 32 * 32
    return na, rows - na


def reduce_col(s, p, tag, part, cbuf, xa2, xa1, xb2, xb1, yb, ya):
    na, nb = col_parts(part.shape[3])
    a_, b_ = pl.ds(0, na), pl.ds(na, nb)
    mine, other, core, sib = p.yh, 1 - p.yh, p.core, 1 - p.core
    ways = ((1, p.right, 0), (-1, p.left, 1))

    def a_cut(n):
        return pl.ds(n * (na // 2), na // 2)

    def b_cut(n, base):
        return pl.ds(base + n * (nb // 2), nb // 2)

    def whole(h):
        return cbuf.at[:, p.xat(h)]

    for h in (2, 1, -1, 0):
        s.send((tag, "c", h), part.at[:, p.xat(h), sib], whole(h), p.sibling)
    yield
    for h in (2, 1, -1):
        s.wait((tag, "c", h), whole(h), p.sibling)
        add_into(part.at[:, p.xat(h), core], whole(h))
        s.send((tag, "yb", h), part.at[other, p.xat(h), core, b_], yb.at[h % NX], p.across)
        if h == 2:
            for d, to, n in ways:
                s.send((tag, "xa2", d), part.at[:, p.xat(2), core, a_cut(n)], xa2.at[:, a_cut(n)], to)
    s.wait((tag, "c", 0), whole(0), p.sibling)
    add_into(part.at[:, p.x, core], whole(0))
    s.send((tag, "yb", 0), part.at[other, p.x, core, b_], yb.at[0], p.across)
    yield
    for d, to, n in ways:
        s.wait((tag, "xa2", d), xa2.at[:, a_cut(n)], to)
        add_into(part.at[:, p.xat(d), core, a_cut(n)], xa2.at[:, a_cut(n)])
        s.send((tag, "xa1", d), part.at[:, p.xat(d), core, a_], xa1.at[n], to)
    yield
    s.wait((tag, "yb", 2), yb.at[2], p.across)
    add_into(part.at[mine, p.xat(2), core, b_], yb.at[2])
    for d, to, n in ways:
        s.send((tag, "xb2", d), part.at[mine, p.xat(2), core, b_cut(n, na)], xb2.at[b_cut(n, 0)], to)
    yield
    for d, to, n in ways:
        s.wait((tag, "yb", d), yb.at[d % NX], p.across)
        add_into(part.at[mine, p.xat(d), core, b_], yb.at[d % NX])
        s.wait((tag, "xb2", d), xb2.at[b_cut(n, 0)], to)
        add_into(part.at[mine, p.xat(d), core, b_cut(n, na)], xb2.at[b_cut(n, 0)])
        s.send((tag, "xb1", d), part.at[mine, p.xat(d), core, b_], xb1.at[n], to)
    yield
    for d, to, n in ways:
        s.wait((tag, "xa1", d), xa1.at[n], to)
    add_into(part.at[:, p.x, core, a_], xa1.at[0], xa1.at[1])
    s.send((tag, "ya"), part.at[other, p.x, core, a_], ya, p.across)
    s.wait((tag, "yb", 0), yb.at[0], p.across)
    yield
    for d, to, n in ways:
        s.wait((tag, "xb1", d), xb1.at[n], to)
    add_into(part.at[mine, p.x, core, b_], yb.at[0], xb1.at[0], xb1.at[1])
    yield
    s.wait((tag, "ya"), ya, p.across)
    add_into(part.at[mine, p.x, core, a_], ya)


def reduce_col_scratch(n_yh, n_x, rows, feats):
    na, nb = col_parts(rows)
    return [
        pltpu.VMEM((n_yh, n_x, rows, feats), BF16),
        pltpu.VMEM((n_yh, na, feats), BF16),
        pltpu.VMEM((2, n_yh, na, feats), BF16),
        pltpu.VMEM((nb, feats), BF16),
        pltpu.VMEM((2, nb, feats), BF16),
        pltpu.VMEM((n_x, nb, feats), BF16),
        pltpu.VMEM((na, feats), BF16),
    ]


def gather_col(s, p, tag, tab):
    na, nb = col_parts(tab.shape[3])
    a_, b_ = pl.ds(0, na), pl.ds(na, nb)
    mine, other, core = p.yh, 1 - p.yh, p.core
    ways = ((1, p.right, 0), (-1, p.left, 1))

    def blk(yh, h, ds):
        return tab.at[yh, p.xat(h), core, ds]

    def pair(h, ds):
        return tab.at[:, p.xat(h), core, ds]

    def push(key, b, to):
        s.send((tag,) + key, b, b, to)

    def took(key, b):
        s.wait((tag,) + key, b, p.sibling)

    push(("ya",), blk(mine, 0, a_), p.across)
    for d, to, n in ways:
        push(("b", d), blk(mine, 0, b_), to)
    push(("yb", 0), blk(mine, 0, b_), p.across)
    yield
    took(("ya",), blk(other, 0, a_))
    for d, to, n in ways:
        push(("a", d), pair(0, a_), to)
    push(("c", 0, "a"), pair(0, a_), p.sibling)
    yield
    for d, to, n in ways:
        took(("b", d), blk(mine, -d, b_))
        push(("b2", d), blk(mine, -d, pl.ds(na + n * (nb // 2), nb // 2)), to)
        push(("yb", -d), blk(mine, -d, b_), p.across)
    yield
    for d, to, n in ways:
        took(("a", d), pair(-d, a_))
        push(("a2", d), pair(-d, pl.ds(n * (na // 2), na // 2)), to)
        push(("c", -d, "a"), pair(-d, a_), p.sibling)
    took(("yb", 0), blk(other, 0, b_))
    push(("c", 0, "b"), pair(0, b_), p.sibling)
    yield
    for d, to, n in ways:
        took(("b2", d), blk(mine, 2, pl.ds(na + n * (nb // 2), nb // 2)))
    push(("yb", 2), blk(mine, 2, b_), p.across)
    yield
    for d in (1, -1):
        took(("yb", d), blk(other, d, b_))
        push(("c", d, "b"), pair(d, b_), p.sibling)
    yield
    for d, to, n in ways:
        took(("a2", d), pair(2, pl.ds(n * (na // 2), na // 2)))
    push(("c", 2, "a"), pair(2, a_), p.sibling)
    took(("yb", 2), blk(other, 2, b_))
    push(("c", 2, "b"), pair(2, b_), p.sibling)
    yield
    for h in (0, 1, -1, 2):
        for name, ds in (("a", a_), ("b", b_)):
            s.wait((tag, "c", h, name), tab.at[:, p.xat(h), 1 - core, ds], p.sibling)


def sum_weight(s, p, q, wpart, wc, wd, wy, wz, wtab, scale):
    core, sib = p.core, 1 - p.core
    s.send("wc", wpart.at[:, :, sib], wc, p.sibling)
    yield
    s.wait("wc", wc, p.sibling)
    mine = wpart.at[:, :, core]
    mine[...] = mine[...] + wc[...]
    for dy, h in p.mates:
        yh = p.yh + dy - 2 * p.yh * dy
        s.send(("wd", dy, h), wpart.at[yh, p.xat(h), core], wd.at[dy * NX + h], p.mate(dy, h))
    yield
    total = wpart[p.yh, p.x, core]
    for dy, h in p.mates:
        s.wait(("wd", dy, h), wd.at[dy * NX + h], p.mate(dy, h))
        total = total + wd[dy * NX + h]
    wy[0] = total
    s.send("wy", wy.at[0], wy.at[1], q.across)
    yield
    s.wait("wy", wy.at[1], q.across)
    wz[q.z] = wy[0] + wy[1]
    for h in range(1, NZ):
        s.send(("wz", h), wz.at[q.z], wz.at[q.z], {"row": q.at(q.yl, h)})
    yield
    for h in range(1, NZ):
        s.wait(("wz", h), wz.at[q.zat(-h)], q.across)
    total = wz[0]
    for z in range(1, NZ):
        total = total + wz[z]
    own = wtab.at[p.yh, p.x, core]
    own[...] = total * scale
    for dy, h in p.mates:
        s.send(("w", dy, h), own, own, p.mate(dy, h))
    yield
    for dy, h in p.mates:
        yh = p.yh + dy - 2 * p.yh * dy
        s.wait(("w", dy, h), wtab.at[yh, p.xat(-h), core], p.sibling)
    s.send("ws", wtab.at[:, :, core], wtab.at[:, :, core], p.sibling)
    yield
    s.wait("ws", wtab.at[:, :, sib], p.sibling)


def drain(steps):
    for _ in steps:
        pass


def drain_after(s, steps):
    before, s.sent = s.sent, []
    next(steps)
    for c in before:
        c.wait_send()
    drain(steps)


def layer_kernel(
    scale, x_ref, tiles_ref, tr_ref, tc_ref, cnt_ref, w_ref, g_ref, act_ref, grad_ref, wg_ref,
    xtab, etab, tiles, stash, part, back, plan, splan, tr, tc, cnt, w, g, wpart, wc, wd, wy, wz, *rest,
):
    n_col, n_row = 7, 5
    for_col, for_row, (send_sem, recv_sem, sems) = rest[:n_col], rest[n_col : n_col + n_row], rest[n_col + n_row :]
    slots, edge, _ = tiles_ref.shape
    rows, feats = x_ref.shape
    per = rows // edge
    p, q = ColPlace(), RowPlace()
    mr, mc = lax.axis_index("row"), lax.axis_index("col")

    barrier = pltpu.get_barrier_semaphore()
    peers = [p.sibling, q.across] + [p.mate(dy, h) for dy, h in p.mates]
    peers += [{"row": q.at(q.yl, h)} for h in range(1, NZ)]
    for peer in peers:
        pl.semaphore_signal(barrier, inc=1, device_id=peer, device_id_type=MESH)
    loads = [
        pltpu.make_async_copy(tr_ref.at[mr], tr, sems.at[0]),
        pltpu.make_async_copy(tc_ref.at[mr], tc, sems.at[1]),
        pltpu.make_async_copy(cnt_ref, cnt, sems.at[2]),
        pltpu.make_async_copy(x_ref, xtab.at[q.yl, q.z], sems.at[3]),
        pltpu.make_async_copy(tiles_ref, tiles.at[pl.ds(0, slots)], sems.at[4]),
        pltpu.make_async_copy(w_ref, w, sems.at[5]),
        pltpu.make_async_copy(g_ref, g, sems.at[6]),
    ]
    for c in loads:
        c.start()
    tiles[slots] = jnp.zeros((edge, edge), tiles.dtype)
    n_tiles = stash.shape[0] * 2 - 2 - slots
    for c in loads[:3]:
        c.wait()
    order_slots(tr[pl.ds(mc, 1)], tc[pl.ds(mc, 1)], cnt[mr, mc], n_tiles, plan)
    to_scalars = pltpu.make_async_copy(plan, splan, sems.at[7])
    to_scalars.start()
    loads[3].wait()
    pl.semaphore_wait(barrier, len(peers))

    s = Sender(send_sem, recv_sem)
    gather = gather_row(s, q, "gr", xtab)
    drain(gather)
    to_scalars.wait()
    for c in loads[4:]:
        c.wait()

    multiply(False, splan, tiles, xtab.reshape(n_tiles, edge, feats), stash)
    for t in range(n_tiles):
        b = t // per
        part[b // (2 * NX), b // 2 % NX, b % 2, pl.ds(t % per * edge, edge)] = stash[splan[3, t]]
    reduce = reduce_col(s, p, "rc", part, *for_col)
    drain_after(s, reduce)

    agg = part[p.yh, p.x, p.core]
    pre = jnp.dot(agg, w[...], preferred_element_type=F32)
    logistic = jax.nn.sigmoid(pre)
    upstream = g[...].astype(F32)
    d_pre = (upstream * logistic * (1.0 + pre * (1.0 - logistic))).astype(BF16)
    e = lax.dot_general(d_pre, w[...], (((1,), (1,)), ((), ())), preferred_element_type=F32)
    etab[p.yh, p.x, p.core] = e.astype(BF16)
    before, s.sent = s.sent, []
    gather = gather_col(s, p, "gc", etab)
    next(gather)
    act_ref[...] = (pre * logistic).astype(BF16)
    wg = lax.dot_general(agg, d_pre, (((0,), (0,)), ((), ())), preferred_element_type=F32)
    wpart[...] = wg.reshape(wpart.shape)
    weights = sum_weight(s, p, q, wpart, wc, wd, wy, wz, wg_ref, scale)
    next(weights)
    for c in before:
        c.wait_send()
    next(gather)
    next(gather)
    next(weights)
    drain(gather)
    next(weights)

    multiply(True, splan, tiles, etab.reshape(n_tiles, edge, feats), stash)
    next(weights)
    for t in range(n_tiles):
        b = t // per
        back[b // NZ, b % NZ, pl.ds(t % per * edge, edge)] = stash[splan[7, t]]
    before, s.sent = s.sent, []
    reduce = reduce_row(s, q, "rr", back, *for_row)
    next(reduce)
    for c in before:
        c.wait_send()
    for _ in range(3):
        next(reduce)
    next(weights)
    for _ in range(5):
        next(reduce)
    next(weights)
    drain(reduce)
    grad_ref[...] = back[q.yl, q.z]
    drain(weights)
    s.finish()


def layer(*args):
    x, tiles, tile_rows = args[:3]
    rows, feats = x.shape
    slots, edge, _ = tiles.shape
    n_row, n_col, _ = tile_rows.shape
    n_yh = n_col // (2 * NX)
    n_tiles = n_col * rows // edge
    steps = (slots + n_tiles) // 2
    n_w = feats // n_col
    hbm = pl.BlockSpec(memory_space=pltpu.HBM)
    vmem = pltpu.VMEM
    return pl.pallas_call(
        functools.partial(layer_kernel, 1.0 / math.sqrt(rows * n_row * n_col)),
        out_shape=(
            vmem((rows, feats), BF16),
            vmem((rows, feats), BF16),
            vmem((n_yh, NX, 2, n_w, feats), F32),
        ),
        in_specs=[hbm] * 7,
        out_specs=[pl.BlockSpec(memory_space=vmem)] * 3,
        scratch_shapes=[
            vmem((n_row // NZ, NZ, rows, feats), BF16),
            vmem((n_yh, NX, 2, rows, feats), BF16),
            vmem((slots + 1, edge, edge), BF16),
            vmem((steps + 1, edge, feats), BF16),
            vmem((n_yh, NX, 2, rows, feats), BF16),
            vmem((n_row // NZ, NZ, rows, feats), BF16),
            vmem((8, PLACES), jnp.int32),
            pltpu.SMEM((8, PLACES), jnp.int32),
            vmem((n_col, slots), jnp.int32),
            vmem((n_col, slots), jnp.int32),
            pltpu.SMEM((n_row, n_col), jnp.int32),
            vmem((feats, feats), BF16),
            vmem((rows, feats), BF16),
            vmem((n_yh, NX, 2, n_w, feats), F32),
            vmem((n_yh, NX, n_w, feats), F32),
            vmem((n_yh * NX, n_w, feats), F32),
            vmem((2, n_w, feats), F32),
            vmem((NZ, n_w, feats), F32),
        ]
        + reduce_col_scratch(n_yh, NX, rows, feats)
        + reduce_row_scratch(rows, feats)
        + [
            pltpu.SemaphoreType.DMA((200,)),
            pltpu.SemaphoreType.DMA((200,)),
            pltpu.SemaphoreType.DMA((8,)),
        ],
        compiler_params=pltpu.CompilerParams(
            collective_id=1, has_side_effects=True, vmem_limit_bytes=48 << 20
        ),
        name="layer",
    )(*[pltpu.with_memory_space_constraint(a, pltpu.HBM) for a in args])


def per_device(node_features, tile_values, tile_rows, tile_cols, tile_count, weight, cotangent):
    act, grad, wgrad = layer(
        node_features[0, 0], tile_values[0, 0], tile_rows, tile_cols, tile_count, weight, cotangent[0, 0]
    )
    return act[None, None], grad[None, None], wgrad.reshape(weight.shape)


def solution(mesh):
    in_specs = (
        P("col", "row", None, None),
        P("row", "col", None, None, None),
        P(),
        P(),
        P(),
        P(),
        P("row", "col", None, None),
    )
    out_specs = (P("row", "col", None, None), P("col", "row", None, None), P())
    return jax.shard_map(
        per_device, mesh=mesh, in_specs=in_specs, out_specs=out_specs, check_vma=False
    )
```

```python
import functools
import math

import jax
import jax.numpy as jnp
from jax import lax
from jax.experimental import pallas as pl
from jax.experimental.pallas import tpu as pltpu
from jax.sharding import PartitionSpec as P

MESH = pl.DeviceIdType.MESH
F32 = jnp.float32
BF16 = jnp.bfloat16

NZ = 8
NX = 4
TILE = 128
PLACES = 256


class Sender:
    def __init__(self, send_sem, recv_sem):
        self.send_sem = send_sem
        self.recv_sem = recv_sem
        self.ids = {}
        self.sent = []

    def slot(self, key):
        if key not in self.ids:
            self.ids[key] = len(self.ids)
        return self.ids[key]

    def copy(self, key, src, dst, device_id):
        n = self.slot(key)
        return pltpu.make_async_remote_copy(
            src_ref=src,
            dst_ref=dst,
            send_sem=self.send_sem.at[n],
            recv_sem=self.recv_sem.at[n],
            device_id=device_id,
            device_id_type=MESH,
        )

    def send(self, key, src, dst, device_id):
        c = self.copy(key, src, dst, device_id)
        c.start()
        self.sent.append(c)

    def wait(self, key, dst, device_id):
        self.copy(key, dst, dst, device_id).wait_recv()

    def finish(self):
        for c in self.sent:
            c.wait_send()
        self.sent = []


class RowPlace:
    def __init__(self):
        me = lax.axis_index("row")
        self.yl = me // NZ
        self.z = lax.rem(me, NZ)
        self.right = {"row": self.at(self.yl, 1)}
        self.left = {"row": self.at(self.yl, NZ - 1)}
        self.across = {"row": self.at(1 - self.yl, 0)}

    def zat(self, hops):
        return lax.rem(self.z + hops + NZ, NZ)

    def at(self, yl, hops):
        return yl * NZ + self.zat(hops)


class ColPlace:
    def __init__(self):
        me = lax.axis_index("col")
        self.yh = me // (2 * NX)
        self.x = lax.rem(me // 2, NX)
        self.core = lax.rem(me, 2)
        self.right = {"col": self.at(self.yh, 1, self.core)}
        self.left = {"col": self.at(self.yh, NX - 1, self.core)}
        self.across = {"col": self.at(1 - self.yh, 0, self.core)}
        self.sibling = {"col": self.at(self.yh, 0, 1 - self.core)}
        self.mates = [(dy, h) for dy in (0, 1) for h in range(NX) if (dy, h) != (0, 0)]

    def mate(self, dy, h):
        return {"col": self.at(self.yh + dy - 2 * self.yh * dy, h, self.core)}

    def xat(self, hops):
        return lax.rem(self.x + hops + NX, NX)

    def at(self, yh, hops, core):
        return (yh * NX + self.xat(hops)) * 2 + core


def order_slots(rows, cols, live, n_tiles, plan):
    slots = rows.shape[1]
    places = plan.shape[1]
    steps = (slots + n_tiles) // 2
    sub = lax.broadcasted_iota(jnp.int32, (slots, slots), 0)
    lane = lax.broadcasted_iota(jnp.int32, (slots, slots), 1)
    k_col = sub[:, :1]
    live_row, live_col = lane[:1] < live, sub[:, :1] < live
    tile = lax.broadcasted_iota(jnp.int32, (n_tiles, slots), 0)
    place = lax.broadcasted_iota(jnp.int32, (slots, places), 1)
    tile_sub = lax.broadcasted_iota(jnp.int32, (n_tiles, places), 0)
    tile_lane = lax.broadcasted_iota(jnp.int32, (n_tiles, places), 1)

    def turn(row):
        return jnp.sum(jnp.where(sub == lane, row, 0), axis=1, keepdims=True)

    out = []
    for key, source in ((rows, cols), (cols, rows)):
        same = (turn(key) == key) & (sub < lane) & live_col
        rank = jnp.sum(jnp.where(same, 1, 0), axis=0, keepdims=True)
        number = jnp.sum(jnp.where((tile == key) & live_row, 1, 0), axis=1, keepdims=True)
        pairs = (number + 1) >> 1
        base = 2 * jnp.sum(jnp.where(tile < key, pairs, 0), axis=0, keepdims=True)
        at = turn(jnp.where(live_row, base + rank, -1))
        hit = at == place
        slot = slots + jnp.sum(jnp.where(hit, k_col - slots, 0), axis=0, keepdims=True)
        read = jnp.sum(jnp.where(hit, turn(source), 0), axis=0, keepdims=True)
        fresh = jnp.sum(jnp.where(hit & (turn(rank) == 0), 1, 0), axis=0, keepdims=True)
        upto = jnp.sum(jnp.where(tile_sub <= tile_lane, pairs, 0), axis=0, keepdims=True)
        some = jnp.sum(jnp.where(tile_sub == tile_lane, number, 0), axis=0, keepdims=True)
        final = jnp.where(some > 0, upto - 1, steps)
        out += [slot, read, fresh, final]
    for n, x in enumerate(out):
        plan[pl.ds(n, 1)] = x


GROUP = 28


def multiply(flip, plan, tiles, tab, stash):
    steps = stash.shape[0] - 1
    first = 4 if flip else 0
    side = 0 if flip else 1
    shape = stash.shape[1:]

    def some(g, acc):
        for u in range(GROUP):
            p = g * GROUP + u
            k = [plan[first, 2 * p + i] for i in (0, 1)]
            q = [plan[first + 1, 2 * p + i] for i in (0, 1)]
            left = jnp.concatenate([tiles[i] for i in k], axis=side)
            right = jnp.concatenate([tab[i] for i in q], axis=0)
            prod = lax.dot_general(left, right, (((side,), (0,)), ((), ())), preferred_element_type=F32)
            fresh = plan[first + 2, 2 * p] == 1
            acc = jnp.where(fresh, 0.0, acc) + prod
            stash[p] = acc.astype(stash.dtype)
        return acc

    lax.fori_loop(0, steps // GROUP, some, jnp.zeros(shape, F32))
    stash[steps] = jnp.zeros(shape, stash.dtype)


def add_into(dst, *terms):
    total = dst[...].astype(F32)
    for t in terms:
        total = total + t[...].astype(F32)
    dst[...] = total.astype(dst.dtype)


def row_parts(rows):
    cut = (rows * 7 // 16) // 16 * 16
    rest = rows - cut
    return (0, cut, cut // 2 // 16 * 16), (cut, rest, -(-rest // 2 // 16) * 16)


def hop_rows(part, d, h):
    base, n, half = part
    if h < NZ // 2:
        return base, n
    return (base, half) if d == 1 else (base + half, n - half)


def gather_row(s, p, tag, own, tab):
    first, rest = row_parts(tab.shape[2])
    top = NZ // 2
    mine, other = p.yl, 1 - p.yl
    ways = ((1, p.right), (-1, p.left))

    def blk(yl, h, ds):
        return tab.at[yl, p.zat(h), pl.ds(*ds)]

    def push(key, b, to):
        s.send((tag,) + key, b, b, to)

    streams = (("b", mine, rest), ("a", mine, first), ("c", other, first))

    def begin(key, ds, to):
        s.send((tag,) + key, own.at[pl.ds(*ds)], blk(mine, 0, ds), to)

    begin(("ya",), first[:2], p.across)
    for name, yl, part in streams[:2]:
        for d, to in ways:
            begin((name, d, 1), part[:2], to)
    begin(("yb", 0), rest[:2], p.across)
    yield
    s.wait((tag, "ya"), blk(other, 0, first[:2]), p.across)
    for d, to in ways:
        push(("c", d, 1), blk(other, 0, first[:2]), to)
    for h in range(1, top + 1):
        for name, yl, part in streams:
            yield
            for d, to in ways:
                s.wait((tag, name, d, h), blk(yl, -d * h, hop_rows(part, d, h)), to)
                if h < top:
                    push((name, d, h + 1), blk(yl, -d * h, hop_rows(part, d, h + 1)), to)
                if name == "b" and (h < top or d == -1):
                    push(("yb", -d * h), blk(mine, -d * h, rest[:2]), p.across)
    yield
    for h in [0] + [d * h for h in range(1, top) for d in (1, -1)] + [top]:
        s.wait((tag, "yb", h), blk(other, h, rest[:2]), p.across)


def reduce_row(s, p, tag, part, ybuf, abuf, cbuf, bbuf, fbuf):
    first, rest = row_parts(part.shape[2])
    top = NZ // 2
    mine, other = p.yl, 1 - p.yl
    ways = ((1, p.right, 0), (-1, p.left, 1))
    streams = (("c", other, first, cbuf), ("a", mine, first, abuf), ("b", mine, rest, bbuf))

    def blk(yl, h, ds):
        return part.at[yl, p.zat(h), pl.ds(*ds)]

    def hop(name, yl, piece, buf, d, to, n, h):
        lo, m = hop_rows(piece, d, h)
        s.send((tag, name, d, h), blk(yl, d * h, (lo, m)), buf.at[h - 1, n, pl.ds(lo - piece[0], m)], to)

    def crossed(h):
        s.wait((tag, "yb", h), ybuf.at[h + top - 1], p.across)
        add_into(blk(mine, h, rest[:2]), ybuf.at[h + top - 1])

    s.send((tag, "yb", top), blk(other, top, rest[:2]), ybuf.at[2 * top - 1], p.across)
    for st in streams[:2]:
        for w in ways:
            hop(*st, *w, top)
    for h in [d * h for h in range(top - 1, 0, -1) for d in (1, -1)] + [0]:
        s.send((tag, "yb", h), blk(other, h, rest[:2]), ybuf.at[h + top - 1], p.across)
    yield
    crossed(top)
    for w in ways:
        hop(*streams[2], *w, top)
    for h in range(top - 1, 0, -1):
        for name, yl, piece, buf in streams:
            yield
            for d, to, n in ways:
                if name == "b":
                    crossed(d * h)
                lo, m = hop_rows(piece, d, h + 1)
                got = buf.at[h, n, pl.ds(lo - piece[0], m)]
                s.wait((tag, name, d, h + 1), got, to)
                add_into(blk(yl, d * h, (lo, m)), got)
                hop(name, yl, piece, buf, d, to, n, h)
    for name, yl, piece, buf in streams:
        yield
        for d, to, n in ways:
            s.wait((tag, name, d, 1), buf.at[0, n], to)
        if name == "b":
            crossed(0)
        add_into(blk(yl, 0, piece[:2]), buf.at[0, 0], buf.at[0, 1])
        if name == "c":
            s.send((tag, "f"), blk(other, 0, first[:2]), fbuf, p.across)
    yield
    s.wait((tag, "f"), fbuf, p.across)
    add_into(blk(mine, 0, first[:2]), fbuf)


def reduce_row_scratch(rows, feats):
    (_, m, _), (_, n, _) = row_parts(rows)
    top = NZ // 2
    return [
        pltpu.VMEM((NZ, n, feats), BF16),
        pltpu.VMEM((top, 2, m, feats), BF16),
        pltpu.VMEM((top, 2, m, feats), BF16),
        pltpu.VMEM((top, 2, n, feats), BF16),
        pltpu.VMEM((m, feats), BF16),
    ]


def col_parts(rows):
    na = rows // 2
    return na, rows - na


def reduce_col(s, p, tag, part, cbuf, xa2, xa1, xb2, xb1, yb, ya):
    na, nb = col_parts(part.shape[3])
    a_, b_ = pl.ds(0, na), pl.ds(na, nb)
    mine, other, core, sib = p.yh, 1 - p.yh, p.core, 1 - p.core
    ways = ((1, p.right, 0), (-1, p.left, 1))
    groups = (("o", other, 1), ("m", mine, 0))

    def a_cut(n):
        return pl.ds(n * (na // 2), na // 2)

    def b_cut(n, base):
        return pl.ds(base + n * (nb // 2), nb // 2)

    def whole(h):
        return cbuf.at[:, p.xat(h)]

    def crossed(h):
        s.wait((tag, "yb", h), yb.at[h % NX], p.across)
        add_into(part.at[mine, p.xat(h), core, b_], yb.at[h % NX])

    for h in (2, 1, -1, 0):
        s.send((tag, "c", h), part.at[:, p.xat(h), sib], whole(h), p.sibling)
    yield
    for h in (2, 1, -1, 0):
        s.wait((tag, "c", h), whole(h), p.sibling)
        add_into(part.at[:, p.xat(h), core], whole(h))
        if h == 2:
            for name, yh, i in groups:
                for d, to, n in ways:
                    s.send((tag, "xa2", name, d), part.at[yh, p.xat(2), core, a_cut(n)], xa2.at[i, a_cut(n)], to)
        s.send((tag, "yb", h), part.at[other, p.xat(h), core, b_], yb.at[h % NX], p.across)
    for name, yh, i in groups:
        yield
        for d, to, n in ways:
            s.wait((tag, "xa2", name, d), xa2.at[i, a_cut(n)], to)
            add_into(part.at[yh, p.xat(d), core, a_cut(n)], xa2.at[i, a_cut(n)])
            s.send((tag, "xa1", name, d), part.at[yh, p.xat(d), core, a_], xa1.at[n, i], to)
        if name == "o":
            yield
            crossed(2)
            for d, to, n in ways:
                s.send((tag, "xb2", d), part.at[mine, p.xat(2), core, b_cut(n, na)], xb2.at[b_cut(n, 0)], to)
    yield
    name, yh, i = groups[0]
    for d, to, n in ways:
        s.wait((tag, "xa1", name, d), xa1.at[n, i], to)
    add_into(part.at[yh, p.x, core, a_], xa1.at[0, i], xa1.at[1, i])
    s.send((tag, "ya"), part.at[other, p.x, core, a_], ya, p.across)
    yield
    for d, to, n in ways:
        crossed(d)
        s.wait((tag, "xb2", d), xb2.at[b_cut(n, 0)], to)
        add_into(part.at[mine, p.xat(d), core, b_cut(n, na)], xb2.at[b_cut(n, 0)])
        s.send((tag, "xb1", d), part.at[mine, p.xat(d), core, b_], xb1.at[n], to)
    yield
    name, yh, i = groups[1]
    for d, to, n in ways:
        s.wait((tag, "xa1", name, d), xa1.at[n, i], to)
    add_into(part.at[yh, p.x, core, a_], xa1.at[0, i], xa1.at[1, i])
    s.wait((tag, "yb", 0), yb.at[0], p.across)
    yield
    for d, to, n in ways:
        s.wait((tag, "xb1", d), xb1.at[n], to)
    add_into(part.at[mine, p.x, core, b_], yb.at[0], xb1.at[0], xb1.at[1])
    yield
    s.wait((tag, "ya"), ya, p.across)
    add_into(part.at[mine, p.x, core, a_], ya)


def reduce_col_scratch(n_yh, n_x, rows, feats):
    na, nb = col_parts(rows)
    return [
        pltpu.VMEM((n_yh, n_x, rows, feats), BF16),
        pltpu.VMEM((n_yh, na, feats), BF16),
        pltpu.VMEM((2, n_yh, na, feats), BF16),
        pltpu.VMEM((nb, feats), BF16),
        pltpu.VMEM((2, nb, feats), BF16),
        pltpu.VMEM((n_x, nb, feats), BF16),
        pltpu.VMEM((na, feats), BF16),
    ]


def gather_col(s, p, tag, tab):
    na, nb = col_parts(tab.shape[3])
    a_, b_ = pl.ds(0, na), pl.ds(na, nb)
    mine, other, core = p.yh, 1 - p.yh, p.core
    ways = ((1, p.right, 0), (-1, p.left, 1))

    def a_cut(n):
        return pl.ds(n * (na // 2), na // 2)

    def b_cut(n):
        return pl.ds(na + n * (nb // 2), nb // 2)

    def blk(yh, h, ds):
        return tab.at[yh, p.xat(h), core, ds]

    def push(key, b, to):
        s.send((tag,) + key, b, b, to)

    def took(key, b):
        s.wait((tag,) + key, b, p.sibling)

    def share(h, name, ds):
        push(("c", h, name), tab.at[:, p.xat(h), core, ds], p.sibling)

    push(("ya",), blk(mine, 0, a_), p.across)
    for d, to, n in ways:
        push(("b", d), blk(mine, 0, b_), to)
    push(("yb", 0), blk(mine, 0, b_), p.across)
    for d, to, n in ways:
        push(("m", d), blk(mine, 0, a_), to)
    yield
    for d, to, n in ways:
        took(("b", d), blk(mine, -d, b_))
        push(("b2", d), blk(mine, -d, b_cut(n)), to)
        push(("yb", -d), blk(mine, -d, b_), p.across)
    yield
    took(("ya",), blk(other, 0, a_))
    for d, to, n in ways:
        push(("o", d), blk(other, 0, a_), to)
    share(0, "a", a_)
    yield
    for d, to, n in ways:
        took(("m", d), blk(mine, -d, a_))
        push(("m2", d), blk(mine, -d, a_cut(n)), to)
    took(("yb", 0), blk(other, 0, b_))
    share(0, "b", b_)
    yield
    for d, to, n in ways:
        took(("b2", d), blk(mine, 2, b_cut(n)))
    push(("yb", 2), blk(mine, 2, b_), p.across)
    yield
    for d, to, n in ways:
        took(("o", d), blk(other, -d, a_))
        push(("o2", d), blk(other, -d, a_cut(n)), to)
        share(-d, "a", a_)
    yield
    for d in (1, -1):
        took(("yb", d), blk(other, d, b_))
        share(d, "b", b_)
    yield
    for name, yh in (("m2", mine), ("o2", other)):
        for d, to, n in ways:
            took((name, d), blk(yh, 2, a_cut(n)))
    share(2, "a", a_)
    took(("yb", 2), blk(other, 2, b_))
    share(2, "b", b_)
    yield
    for h in (0, 1, -1, 2):
        for name, ds in (("a", a_), ("b", b_)):
            s.wait((tag, "c", h, name), tab.at[:, p.xat(h), 1 - core, ds], p.sibling)


def sum_weight(s, p, q, wpart, wc, wd, wy, wz, wtab, scale):
    core, sib = p.core, 1 - p.core
    s.send("wc", wpart.at[:, :, sib], wc, p.sibling)
    yield
    s.wait("wc", wc, p.sibling)
    mine = wpart.at[:, :, core]
    mine[...] = mine[...] + wc[...]
    for dy, h in p.mates:
        yh = p.yh + dy - 2 * p.yh * dy
        s.send(("wd", dy, h), wpart.at[yh, p.xat(h), core], wd.at[dy * NX + h], p.mate(dy, h))
    yield
    total = wpart[p.yh, p.x, core]
    for dy, h in p.mates:
        s.wait(("wd", dy, h), wd.at[dy * NX + h], p.mate(dy, h))
        total = total + wd[dy * NX + h]
    wy[0] = total
    s.send("wy", wy.at[0], wy.at[1], q.across)
    yield
    s.wait("wy", wy.at[1], q.across)
    wz[q.z] = wy[0] + wy[1]
    for h in range(1, NZ):
        s.send(("wz", h), wz.at[q.z], wz.at[q.z], {"row": q.at(q.yl, h)})
    yield
    for h in range(1, NZ):
        s.wait(("wz", h), wz.at[q.zat(-h)], q.across)
    total = wz[0]
    for z in range(1, NZ):
        total = total + wz[z]
    own = wtab.at[p.yh, p.x, core]
    own[...] = total * scale
    for dy, h in p.mates:
        s.send(("w", dy, h), own, own, p.mate(dy, h))
    yield
    for dy, h in p.mates:
        yh = p.yh + dy - 2 * p.yh * dy
        s.wait(("w", dy, h), wtab.at[yh, p.xat(-h), core], p.sibling)
    s.send("ws", wtab.at[:, :, core], wtab.at[:, :, core], p.sibling)
    yield
    s.wait("ws", wtab.at[:, :, sib], p.sibling)


def drain(steps):
    for _ in steps:
        pass


def drain_after(s, steps):
    before, s.sent = s.sent, []
    next(steps)
    for c in before:
        c.wait_send()
    drain(steps)


def layer_kernel(
    scale, x_ref, tiles_ref, tr_ref, tc_ref, cnt_ref, w_ref, g_ref, act_ref, grad_ref, wg_ref,
    xtab, etab, tiles, stash, part, back, plan, splan, tr, tc, cnt, w, g, wpart, wc, wd, wy, wz, *rest,
):
    n_col, n_row = 7, 5
    for_col, for_row, (send_sem, recv_sem, sems) = rest[:n_col], rest[n_col : n_col + n_row], rest[n_col + n_row :]
    slots, edge, _ = tiles_ref.shape
    rows, feats = x_ref.shape
    per = rows // edge
    p, q = ColPlace(), RowPlace()
    mr, mc = lax.axis_index("row"), lax.axis_index("col")

    barrier = pltpu.get_barrier_semaphore()
    peers = [p.sibling, q.across] + [p.mate(dy, h) for dy, h in p.mates]
    peers += [{"row": q.at(q.yl, h)} for h in range(1, NZ)]
    for peer in peers:
        pl.semaphore_signal(barrier, inc=1, device_id=peer, device_id_type=MESH)
    loads = [
        pltpu.make_async_copy(tr_ref.at[mr], tr, sems.at[0]),
        pltpu.make_async_copy(tc_ref.at[mr], tc, sems.at[1]),
        pltpu.make_async_copy(cnt_ref, cnt, sems.at[2]),
        pltpu.make_async_copy(x_ref, xtab.at[q.yl, q.z], sems.at[3]),
        pltpu.make_async_copy(tiles_ref, tiles.at[pl.ds(0, slots)], sems.at[4]),
        pltpu.make_async_copy(w_ref, w, sems.at[5]),
        pltpu.make_async_copy(g_ref, g, sems.at[6]),
    ]
    for c in loads:
        c.start()
    tiles[slots] = jnp.zeros((edge, edge), tiles.dtype)
    pl.semaphore_wait(barrier, len(peers))

    s = Sender(send_sem, recv_sem)
    gather = gather_row(s, q, "gr", x_ref, xtab)
    next(gather)
    n_tiles = stash.shape[0] * 2 - 2 - slots
    for c in loads[:3]:
        c.wait()
    order_slots(tr[pl.ds(mc, 1)], tc[pl.ds(mc, 1)], cnt[mr, mc], n_tiles, plan)
    to_scalars = pltpu.make_async_copy(plan, splan, sems.at[7])
    to_scalars.start()
    drain(gather)
    to_scalars.wait()
    for c in loads[3:]:
        c.wait()

    multiply(False, splan, tiles, xtab.reshape(n_tiles, edge, feats), stash)
    for t in range(n_tiles):
        b = t // per
        part[b // (2 * NX), b // 2 % NX, b % 2, pl.ds(t % per * edge, edge)] = stash[splan[3, t]]
    reduce = reduce_col(s, p, "rc", part, *for_col)
    drain_after(s, reduce)

    agg = part[p.yh, p.x, p.core]
    pre = jnp.dot(agg, w[...], preferred_element_type=F32)
    logistic = jax.nn.sigmoid(pre)
    upstream = g[...].astype(F32)
    d_pre = (upstream * logistic * (1.0 + pre * (1.0 - logistic))).astype(BF16)
    e = lax.dot_general(d_pre, w[...], (((1,), (1,)), ((), ())), preferred_element_type=F32)
    etab[p.yh, p.x, p.core] = e.astype(BF16)
    before, s.sent = s.sent, []
    gather = gather_col(s, p, "gc", etab)
    next(gather)
    act_ref[...] = (pre * logistic).astype(BF16)
    wg = lax.dot_general(agg, d_pre, (((0,), (0,)), ((), ())), preferred_element_type=F32)
    wpart[...] = wg.reshape(wpart.shape)
    weights = sum_weight(s, p, q, wpart, wc, wd, wy, wz, wg_ref, scale)
    next(weights)
    for c in before:
        c.wait_send()
    for _ in range(2):
        next(gather)
    next(weights)
    for _ in range(4):
        next(gather)
    next(weights)
    drain(gather)
    next(weights)

    multiply(True, splan, tiles, etab.reshape(n_tiles, edge, feats), stash)
    for t in range(n_tiles):
        b = t // per
        back[b // NZ, b % NZ, pl.ds(t % per * edge, edge)] = stash[splan[7, t]]
    before, s.sent = s.sent, []
    reduce = reduce_row(s, q, "rr", back, *for_row)
    next(reduce)
    for c in before:
        c.wait_send()
    for _ in range(7):
        next(reduce)
    next(weights)
    for _ in range(5):
        next(reduce)
    next(weights)
    drain(reduce)
    grad_ref[...] = back[q.yl, q.z]
    drain(weights)
    s.finish()


def layer(*args):
    x, tiles, tile_rows = args[:3]
    rows, feats = x.shape
    slots, edge, _ = tiles.shape
    n_row, n_col, _ = tile_rows.shape
    n_yh = n_col // (2 * NX)
    n_tiles = n_col * rows // edge
    steps = (slots + n_tiles) // 2
    n_w = feats // n_col
    hbm = pl.BlockSpec(memory_space=pltpu.HBM)
    vmem = pltpu.VMEM
    return pl.pallas_call(
        functools.partial(layer_kernel, 1.0 / math.sqrt(rows * n_row * n_col)),
        out_shape=(
            vmem((rows, feats), BF16),
            vmem((rows, feats), BF16),
            vmem((n_yh, NX, 2, n_w, feats), F32),
        ),
        in_specs=[hbm] * 7,
        out_specs=[pl.BlockSpec(memory_space=vmem)] * 3,
        scratch_shapes=[
            vmem((n_row // NZ, NZ, rows, feats), BF16),
            vmem((n_yh, NX, 2, rows, feats), BF16),
            vmem((slots + 1, edge, edge), BF16),
            vmem((steps + 1, edge, feats), BF16),
            vmem((n_yh, NX, 2, rows, feats), BF16),
            vmem((n_row // NZ, NZ, rows, feats), BF16),
            vmem((8, PLACES), jnp.int32),
            pltpu.SMEM((8, PLACES), jnp.int32),
            vmem((n_col, slots), jnp.int32),
            vmem((n_col, slots), jnp.int32),
            pltpu.SMEM((n_row, n_col), jnp.int32),
            vmem((feats, feats), BF16),
            vmem((rows, feats), BF16),
            vmem((n_yh, NX, 2, n_w, feats), F32),
            vmem((n_yh, NX, n_w, feats), F32),
            vmem((n_yh * NX, n_w, feats), F32),
            vmem((2, n_w, feats), F32),
            vmem((NZ, n_w, feats), F32),
        ]
        + reduce_col_scratch(n_yh, NX, rows, feats)
        + reduce_row_scratch(rows, feats)
        + [
            pltpu.SemaphoreType.DMA((256,)),
            pltpu.SemaphoreType.DMA((256,)),
            pltpu.SemaphoreType.DMA((8,)),
        ],
        compiler_params=pltpu.CompilerParams(
            collective_id=1, has_side_effects=True, vmem_limit_bytes=48 << 20
        ),
        name="layer",
    )(*[pltpu.with_memory_space_constraint(a, pltpu.HBM) for a in args])


def per_device(node_features, tile_values, tile_rows, tile_cols, tile_count, weight, cotangent):
    act, grad, wgrad = layer(
        node_features[0, 0], tile_values[0, 0], tile_rows, tile_cols, tile_count, weight, cotangent[0, 0]
    )
    return act[None, None], grad[None, None], wgrad.reshape(weight.shape)


def solution(mesh):
    in_specs = (
        P("col", "row", None, None),
        P("row", "col", None, None, None),
        P(),
        P(),
        P(),
        P(),
        P("row", "col", None, None),
    )
    out_specs = (P("row", "col", None, None), P("col", "row", None, None), P())
    return jax.shard_map(
        per_device, mesh=mesh, in_specs=in_specs, out_specs=out_specs, check_vma=False
    )
```

```python
import functools
import math

import jax
import jax.numpy as jnp
from jax import lax
from jax.experimental import pallas as pl
from jax.experimental.pallas import tpu as pltpu
from jax.sharding import PartitionSpec as P

MESH = pl.DeviceIdType.MESH
F32 = jnp.float32
BF16 = jnp.bfloat16

NZ = 8
NX = 4
TILE = 128
PLACES = 256


class Sender:
    def __init__(self, send_sem, recv_sem):
        self.send_sem = send_sem
        self.recv_sem = recv_sem
        self.ids = {}
        self.sent = []

    def slot(self, key):
        if key not in self.ids:
            self.ids[key] = len(self.ids)
        return self.ids[key]

    def copy(self, key, src, dst, device_id):
        n = self.slot(key)
        return pltpu.make_async_remote_copy(
            src_ref=src,
            dst_ref=dst,
            send_sem=self.send_sem.at[n],
            recv_sem=self.recv_sem.at[n],
            device_id=device_id,
            device_id_type=MESH,
        )

    def send(self, key, src, dst, device_id):
        c = self.copy(key, src, dst, device_id)
        c.start()
        self.sent.append(c)

    def wait(self, key, dst, device_id):
        self.copy(key, dst, dst, device_id).wait_recv()

    def finish(self):
        for c in self.sent:
            c.wait_send()
        self.sent = []


class RowPlace:
    def __init__(self):
        me = lax.axis_index("row")
        self.yl = me // NZ
        self.z = lax.rem(me, NZ)
        self.right = {"row": self.at(self.yl, 1)}
        self.left = {"row": self.at(self.yl, NZ - 1)}
        self.across = {"row": self.at(1 - self.yl, 0)}

    def zat(self, hops):
        return lax.rem(self.z + hops + NZ, NZ)

    ORDER = (4, 5, 3, 6, 2, 7, 1, 0)

    def place(self, tile, per):
        block = tile // per
        hops = (block % NZ - self.z + NZ) % NZ
        rank = jnp.zeros_like(tile)
        for n, h in enumerate(self.ORDER):
            rank = jnp.where(hops == h, n, rank)
        return (rank * 2 + block // NZ) * per + tile % per

    def spot(self, place, per):
        return place // per % 2, self.zat(self.ORDER[place // (2 * per)]), place % per

    def at(self, yl, hops):
        return yl * NZ + self.zat(hops)


class ColPlace:
    def __init__(self):
        me = lax.axis_index("col")
        self.yh = me // (2 * NX)
        self.x = lax.rem(me // 2, NX)
        self.core = lax.rem(me, 2)
        self.right = {"col": self.at(self.yh, 1, self.core)}
        self.left = {"col": self.at(self.yh, NX - 1, self.core)}
        self.across = {"col": self.at(1 - self.yh, 0, self.core)}
        self.sibling = {"col": self.at(self.yh, 0, 1 - self.core)}
        self.mates = [(dy, h) for dy in (0, 1) for h in range(NX) if (dy, h) != (0, 0)]

    def mate(self, dy, h):
        return {"col": self.at(self.yh + dy - 2 * self.yh * dy, h, self.core)}

    def xat(self, hops):
        return lax.rem(self.x + hops + NX, NX)

    ORDER = (2, 1, 3, 0)

    def place(self, tile, per):
        block = tile // per
        hops = (block // 2 % NX - self.x + NX) % NX
        rank = jnp.zeros_like(tile)
        for n, h in enumerate(self.ORDER):
            rank = jnp.where(hops == h, n, rank)
        rank = rank + jnp.where(block % 2 == self.core, NX, 0)
        return (rank * 2 + block // (2 * NX)) * per + tile % per

    def spot(self, place, per):
        rank = place // (2 * per)
        core = self.core if rank >= NX else 1 - self.core
        return place // per % 2, self.xat(self.ORDER[rank % NX]), core, place % per

    def at(self, yh, hops, core):
        return (yh * NX + self.xat(hops)) * 2 + core


def order_slots(rows, row_place, cols, col_place, live, n_tiles, plan):
    slots = rows.shape[1]
    places = plan.shape[1]
    steps = (slots + n_tiles) // 2
    sub = lax.broadcasted_iota(jnp.int32, (slots, slots), 0)
    lane = lax.broadcasted_iota(jnp.int32, (slots, slots), 1)
    k_col = sub[:, :1]
    live_row, live_col = lane[:1] < live, sub[:, :1] < live
    tile = lax.broadcasted_iota(jnp.int32, (n_tiles, slots), 0)
    place = lax.broadcasted_iota(jnp.int32, (slots, places), 1)
    tile_sub = lax.broadcasted_iota(jnp.int32, (n_tiles, places), 0)
    tile_lane = lax.broadcasted_iota(jnp.int32, (n_tiles, places), 1)

    def turn(row):
        return jnp.sum(jnp.where(sub == lane, row, 0), axis=1, keepdims=True)

    out = []
    for key, source in ((row_place, cols), (col_place, rows)):
        same = (turn(key) == key) & (sub < lane) & live_col
        rank = jnp.sum(jnp.where(same, 1, 0), axis=0, keepdims=True)
        number = jnp.sum(jnp.where((tile == key) & live_row, 1, 0), axis=1, keepdims=True)
        pairs = (number + 1) >> 1
        base = 2 * jnp.sum(jnp.where(tile < key, pairs, 0), axis=0, keepdims=True)
        at = turn(jnp.where(live_row, base + rank, -1))
        hit = at == place
        slot = slots + jnp.sum(jnp.where(hit, k_col - slots, 0), axis=0, keepdims=True)
        read = jnp.sum(jnp.where(hit, turn(source), 0), axis=0, keepdims=True)
        fresh = jnp.sum(jnp.where(hit & (turn(rank) == 0), 1, 0), axis=0, keepdims=True)
        upto = jnp.sum(jnp.where(tile_sub <= tile_lane, pairs, 0), axis=0, keepdims=True)
        some = jnp.sum(jnp.where(tile_sub == tile_lane, number, 0), axis=0, keepdims=True)
        final = jnp.where(some > 0, upto - 1, steps)
        out += [slot, read, fresh, final]
    for n, x in enumerate(out):
        plan[pl.ds(n, 1)] = x


EARLY = 4
LOOPS = 2


def multiply(flip, plan, tiles, tab, stash, put):
    steps = stash.shape[0] - 1
    early = EARLY * tab.shape[0] // 2
    first = 4 if flip else 0
    side = 0 if flip else 1
    shape = stash.shape[1:]

    def run_steps(start, number, acc):
        def some(g, acc):
            for u in range(number // LOOPS):
                p = start + g * (number // LOOPS) + u
                k = [plan[first, 2 * p + i] for i in (0, 1)]
                q = [plan[first + 1, 2 * p + i] for i in (0, 1)]
                left = jnp.concatenate([tiles[i] for i in k], axis=side)
                right = jnp.concatenate([tab[i] for i in q], axis=0)
                prod = lax.dot_general(left, right, (((side,), (0,)), ((), ())), preferred_element_type=F32)
                fresh = plan[first + 2, 2 * p] == 1
                acc = jnp.where(fresh, 0.0, acc) + prod
                stash[p] = acc.astype(stash.dtype)
            return acc

        return lax.fori_loop(0, LOOPS, some, acc)

    stash[steps] = jnp.zeros(shape, stash.dtype)
    acc = run_steps(0, early, jnp.zeros(shape, F32))
    for t in range(EARLY):
        put(t, stash[plan[first + 3, t]])
    yield
    run_steps(early, steps - early, acc)
    for t in range(EARLY, tab.shape[0]):
        put(t, stash[plan[first + 3, t]])


def add_into(dst, *terms):
    total = dst[...].astype(F32)
    for t in terms:
        total = total + t[...].astype(F32)
    dst[...] = total.astype(dst.dtype)


def row_parts(rows):
    cut = (rows * 7 // 16) // 16 * 16
    rest = rows - cut
    return (0, cut, cut // 2 // 16 * 16), (cut, rest, -(-rest // 2 // 16) * 16)


def hop_rows(part, d, h):
    base, n, half = part
    if h < NZ // 2:
        return base, n
    return (base, half) if d == 1 else (base + half, n - half)


def gather_row(s, p, tag, own, tab):
    first, rest = row_parts(tab.shape[2])
    top = NZ // 2
    mine, other = p.yl, 1 - p.yl
    ways = ((1, p.right), (-1, p.left))

    def blk(yl, h, ds):
        return tab.at[yl, p.zat(h), pl.ds(*ds)]

    def push(key, b, to):
        s.send((tag,) + key, b, b, to)

    streams = (("b", mine, rest), ("a", mine, first), ("c", other, first))

    def begin(key, ds, to):
        s.send((tag,) + key, own.at[pl.ds(*ds)], blk(mine, 0, ds), to)

    begin(("ya",), first[:2], p.across)
    for name, yl, part in streams[:2]:
        for d, to in ways:
            begin((name, d, 1), part[:2], to)
    begin(("yb", 0), rest[:2], p.across)
    yield
    s.wait((tag, "ya"), blk(other, 0, first[:2]), p.across)
    for d, to in ways:
        push(("c", d, 1), blk(other, 0, first[:2]), to)
    for h in range(1, top + 1):
        for name, yl, part in streams:
            yield
            for d, to in ways:
                s.wait((tag, name, d, h), blk(yl, -d * h, hop_rows(part, d, h)), to)
                if h < top:
                    push((name, d, h + 1), blk(yl, -d * h, hop_rows(part, d, h + 1)), to)
                if name == "b" and (h < top or d == -1):
                    push(("yb", -d * h), blk(mine, -d * h, rest[:2]), p.across)
    yield
    for h in [0] + [d * h for h in range(1, top) for d in (1, -1)] + [top]:
        s.wait((tag, "yb", h), blk(other, h, rest[:2]), p.across)


def reduce_row(s, p, tag, part, ybuf, abuf, cbuf, bbuf, fbuf):
    first, rest = row_parts(part.shape[2])
    top = NZ // 2
    mine, other = p.yl, 1 - p.yl
    ways = ((1, p.right, 0), (-1, p.left, 1))
    streams = (("c", other, first, cbuf), ("a", mine, first, abuf), ("b", mine, rest, bbuf))

    def blk(yl, h, ds):
        return part.at[yl, p.zat(h), pl.ds(*ds)]

    def hop(name, yl, piece, buf, d, to, n, h):
        lo, m = hop_rows(piece, d, h)
        s.send((tag, name, d, h), blk(yl, d * h, (lo, m)), buf.at[h - 1, n, pl.ds(lo - piece[0], m)], to)

    def crossed(h):
        s.wait((tag, "yb", h), ybuf.at[h + top - 1], p.across)
        add_into(blk(mine, h, rest[:2]), ybuf.at[h + top - 1])

    s.send((tag, "yb", top), blk(other, top, rest[:2]), ybuf.at[2 * top - 1], p.across)
    for st in streams[:2]:
        for w in ways:
            hop(*st, *w, top)
    yield
    for h in [d * h for h in range(top - 1, 0, -1) for d in (1, -1)] + [0]:
        s.send((tag, "yb", h), blk(other, h, rest[:2]), ybuf.at[h + top - 1], p.across)
    yield
    crossed(top)
    for w in ways:
        hop(*streams[2], *w, top)
    for h in range(top - 1, 0, -1):
        for name, yl, piece, buf in streams:
            yield
            for d, to, n in ways:
                if name == "b":
                    crossed(d * h)
                lo, m = hop_rows(piece, d, h + 1)
                got = buf.at[h, n, pl.ds(lo - piece[0], m)]
                s.wait((tag, name, d, h + 1), got, to)
                add_into(blk(yl, d * h, (lo, m)), got)
                hop(name, yl, piece, buf, d, to, n, h)
    for name, yl, piece, buf in streams:
        yield
        for d, to, n in ways:
            s.wait((tag, name, d, 1), buf.at[0, n], to)
        if name == "b":
            crossed(0)
        add_into(blk(yl, 0, piece[:2]), buf.at[0, 0], buf.at[0, 1])
        if name == "c":
            s.send((tag, "f"), blk(other, 0, first[:2]), fbuf, p.across)
    yield
    s.wait((tag, "f"), fbuf, p.across)
    add_into(blk(mine, 0, first[:2]), fbuf)


def reduce_row_scratch(rows, feats):
    (_, m, _), (_, n, _) = row_parts(rows)
    top = NZ // 2
    return [
        pltpu.VMEM((NZ, n, feats), BF16),
        pltpu.VMEM((top, 2, m, feats), BF16),
        pltpu.VMEM((top, 2, m, feats), BF16),
        pltpu.VMEM((top, 2, n, feats), BF16),
        pltpu.VMEM((m, feats), BF16),
    ]


def col_parts(rows):
    na = rows // 2
    return na, rows - na


def reduce_col(s, p, tag, part, cbuf, xa2, xa1, xb2, xb1, yb, ya):
    na, nb = col_parts(part.shape[3])
    a_, b_ = pl.ds(0, na), pl.ds(na, nb)
    mine, other, core, sib = p.yh, 1 - p.yh, p.core, 1 - p.core
    ways = ((1, p.right, 0), (-1, p.left, 1))
    groups = (("o", other, 1), ("m", mine, 0))

    def a_cut(n):
        return pl.ds(n * (na // 2), na // 2)

    def b_cut(n, base):
        return pl.ds(base + n * (nb // 2), nb // 2)

    def whole(h):
        return cbuf.at[:, p.xat(h)]

    def crossed(h):
        s.wait((tag, "yb", h), yb.at[h % NX], p.across)
        add_into(part.at[mine, p.xat(h), core, b_], yb.at[h % NX])

    for h in (2, 1, -1, 0):
        s.send((tag, "c", h), part.at[:, p.xat(h), sib], whole(h), p.sibling)
        if h == 2:
            yield
    yield
    for h in (2, 1, -1, 0):
        s.wait((tag, "c", h), whole(h), p.sibling)
        add_into(part.at[:, p.xat(h), core], whole(h))
        if h == 2:
            for name, yh, i in groups:
                for d, to, n in ways:
                    s.send((tag, "xa2", name, d), part.at[yh, p.xat(2), core, a_cut(n)], xa2.at[i, a_cut(n)], to)
        s.send((tag, "yb", h), part.at[other, p.xat(h), core, b_], yb.at[h % NX], p.across)
    for name, yh, i in groups:
        yield
        for d, to, n in ways:
            s.wait((tag, "xa2", name, d), xa2.at[i, a_cut(n)], to)
            add_into(part.at[yh, p.xat(d), core, a_cut(n)], xa2.at[i, a_cut(n)])
            s.send((tag, "xa1", name, d), part.at[yh, p.xat(d), core, a_], xa1.at[n, i], to)
        if name == "o":
            yield
            crossed(2)
            for d, to, n in ways:
                s.send((tag, "xb2", d), part.at[mine, p.xat(2), core, b_cut(n, na)], xb2.at[b_cut(n, 0)], to)
    yield
    name, yh, i = groups[0]
    for d, to, n in ways:
        s.wait((tag, "xa1", name, d), xa1.at[n, i], to)
    add_into(part.at[yh, p.x, core, a_], xa1.at[0, i], xa1.at[1, i])
    s.send((tag, "ya"), part.at[other, p.x, core, a_], ya, p.across)
    yield
    for d, to, n in ways:
        crossed(d)
        s.wait((tag, "xb2", d), xb2.at[b_cut(n, 0)], to)
        add_into(part.at[mine, p.xat(d), core, b_cut(n, na)], xb2.at[b_cut(n, 0)])
        s.send((tag, "xb1", d), part.at[mine, p.xat(d), core, b_], xb1.at[n], to)
    yield
    name, yh, i = groups[1]
    for d, to, n in ways:
        s.wait((tag, "xa1", name, d), xa1.at[n, i], to)
    add_into(part.at[yh, p.x, core, a_], xa1.at[0, i], xa1.at[1, i])
    s.wait((tag, "yb", 0), yb.at[0], p.across)
    yield
    for d, to, n in ways:
        s.wait((tag, "xb1", d), xb1.at[n], to)
    add_into(part.at[mine, p.x, core, b_], yb.at[0], xb1.at[0], xb1.at[1])
    yield
    s.wait((tag, "ya"), ya, p.across)
    add_into(part.at[mine, p.x, core, a_], ya)


def reduce_col_scratch(n_yh, n_x, rows, feats):
    na, nb = col_parts(rows)
    return [
        pltpu.VMEM((n_yh, n_x, rows, feats), BF16),
        pltpu.VMEM((n_yh, na, feats), BF16),
        pltpu.VMEM((2, n_yh, na, feats), BF16),
        pltpu.VMEM((nb, feats), BF16),
        pltpu.VMEM((2, nb, feats), BF16),
        pltpu.VMEM((n_x, nb, feats), BF16),
        pltpu.VMEM((na, feats), BF16),
    ]


def gather_col(s, p, tag, tab):
    na, nb = col_parts(tab.shape[3])
    a_, b_ = pl.ds(0, na), pl.ds(na, nb)
    mine, other, core = p.yh, 1 - p.yh, p.core
    ways = ((1, p.right, 0), (-1, p.left, 1))

    def a_cut(n):
        return pl.ds(n * (na // 2), na // 2)

    def b_cut(n):
        return pl.ds(na + n * (nb // 2), nb // 2)

    def blk(yh, h, ds):
        return tab.at[yh, p.xat(h), core, ds]

    def push(key, b, to):
        s.send((tag,) + key, b, b, to)

    def took(key, b):
        s.wait((tag,) + key, b, p.sibling)

    def share(h, name, ds):
        push(("c", h, name), tab.at[:, p.xat(h), core, ds], p.sibling)

    push(("ya",), blk(mine, 0, a_), p.across)
    for d, to, n in ways:
        push(("b", d), blk(mine, 0, b_), to)
    push(("yb", 0), blk(mine, 0, b_), p.across)
    for d, to, n in ways:
        push(("m", d), blk(mine, 0, a_), to)
    yield
    for d, to, n in ways:
        took(("b", d), blk(mine, -d, b_))
        push(("b2", d), blk(mine, -d, b_cut(n)), to)
        push(("yb", -d), blk(mine, -d, b_), p.across)
    yield
    took(("ya",), blk(other, 0, a_))
    for d, to, n in ways:
        push(("o", d), blk(other, 0, a_), to)
    share(0, "a", a_)
    yield
    for d, to, n in ways:
        took(("m", d), blk(mine, -d, a_))
        push(("m2", d), blk(mine, -d, a_cut(n)), to)
    took(("yb", 0), blk(other, 0, b_))
    share(0, "b", b_)
    yield
    for d, to, n in ways:
        took(("b2", d), blk(mine, 2, b_cut(n)))
    push(("yb", 2), blk(mine, 2, b_), p.across)
    yield
    for d, to, n in ways:
        took(("o", d), blk(other, -d, a_))
        push(("o2", d), blk(other, -d, a_cut(n)), to)
        share(-d, "a", a_)
    yield
    for d in (1, -1):
        took(("yb", d), blk(other, d, b_))
        share(d, "b", b_)
    yield
    for name, yh in (("m2", mine), ("o2", other)):
        for d, to, n in ways:
            took((name, d), blk(yh, 2, a_cut(n)))
    share(2, "a", a_)
    took(("yb", 2), blk(other, 2, b_))
    share(2, "b", b_)
    yield
    for h in (0, 1, -1, 2):
        for name, ds in (("a", a_), ("b", b_)):
            s.wait((tag, "c", h, name), tab.at[:, p.xat(h), 1 - core, ds], p.sibling)


def sum_weight(s, p, q, wpart, wc, wd, wy, wz, wtab, scale):
    core, sib = p.core, 1 - p.core
    s.send("wc", wpart.at[:, :, sib], wc, p.sibling)
    yield
    s.wait("wc", wc, p.sibling)
    mine = wpart.at[:, :, core]
    mine[...] = mine[...] + wc[...]
    for dy, h in p.mates:
        yh = p.yh + dy - 2 * p.yh * dy
        s.send(("wd", dy, h), wpart.at[yh, p.xat(h), core], wd.at[dy * NX + h], p.mate(dy, h))
    yield
    total = wpart[p.yh, p.x, core]
    for dy, h in p.mates:
        s.wait(("wd", dy, h), wd.at[dy * NX + h], p.mate(dy, h))
        total = total + wd[dy * NX + h]
    wy[0] = total
    s.send("wy", wy.at[0], wy.at[1], q.across)
    yield
    s.wait("wy", wy.at[1], q.across)
    wz[q.z] = wy[0] + wy[1]
    for h in range(1, NZ):
        s.send(("wz", h), wz.at[q.z], wz.at[q.z], {"row": q.at(q.yl, h)})
    yield
    for h in range(1, NZ):
        s.wait(("wz", h), wz.at[q.zat(-h)], q.across)
    total = wz[0]
    for z in range(1, NZ):
        total = total + wz[z]
    own = wtab.at[p.yh, p.x, core]
    own[...] = total * scale
    for dy, h in p.mates:
        s.send(("w", dy, h), own, own, p.mate(dy, h))
    yield
    for dy, h in p.mates:
        yh = p.yh + dy - 2 * p.yh * dy
        s.wait(("w", dy, h), wtab.at[yh, p.xat(-h), core], p.sibling)
    s.send("ws", wtab.at[:, :, core], wtab.at[:, :, core], p.sibling)
    yield
    s.wait("ws", wtab.at[:, :, sib], p.sibling)


def drain(steps):
    for _ in steps:
        pass


def layer_kernel(
    scale, x_ref, tiles_ref, tr_ref, tc_ref, cnt_ref, w_ref, g_ref, act_ref, grad_ref, wg_ref,
    xtab, etab, tiles, stash, part, back, plan, splan, tr, tc, cnt, w, g, wpart, wc, wd, wy, wz, *rest,
):
    n_col, n_row = 7, 5
    for_col, for_row, (send_sem, recv_sem, sems) = rest[:n_col], rest[n_col : n_col + n_row], rest[n_col + n_row :]
    slots, edge, _ = tiles_ref.shape
    rows, feats = x_ref.shape
    per = rows // edge
    p, q = ColPlace(), RowPlace()
    mr, mc = lax.axis_index("row"), lax.axis_index("col")

    barrier = pltpu.get_barrier_semaphore()
    peers = [p.sibling, q.across] + [p.mate(dy, h) for dy, h in p.mates]
    peers += [{"row": q.at(q.yl, h)} for h in range(1, NZ)]
    for peer in peers:
        pl.semaphore_signal(barrier, inc=1, device_id=peer, device_id_type=MESH)
    loads = [
        pltpu.make_async_copy(tr_ref.at[mr], tr, sems.at[0]),
        pltpu.make_async_copy(tc_ref.at[mr], tc, sems.at[1]),
        pltpu.make_async_copy(cnt_ref, cnt, sems.at[2]),
        pltpu.make_async_copy(x_ref, xtab.at[q.yl, q.z], sems.at[3]),
        pltpu.make_async_copy(tiles_ref, tiles.at[pl.ds(0, slots)], sems.at[4]),
        pltpu.make_async_copy(w_ref, w, sems.at[5]),
        pltpu.make_async_copy(g_ref, g, sems.at[6]),
    ]
    for c in loads:
        c.start()
    tiles[slots] = jnp.zeros((edge, edge), tiles.dtype)
    pl.semaphore_wait(barrier, len(peers))

    s = Sender(send_sem, recv_sem)
    gather = gather_row(s, q, "gr", x_ref, xtab)
    next(gather)
    n_tiles = stash.shape[0] * 2 - 2 - slots
    for c in loads[:3]:
        c.wait()
    t_rows, t_cols = tr[pl.ds(mc, 1)], tc[pl.ds(mc, 1)]
    order_slots(t_rows, p.place(t_rows, per), t_cols, q.place(t_cols, per), cnt[mr, mc], n_tiles, plan)
    to_scalars = pltpu.make_async_copy(plan, splan, sems.at[7])
    to_scalars.start()
    drain(gather)
    to_scalars.wait()
    for c in loads[3:]:
        c.wait()

    def put_part(place, value):
        yh, x, core, n = p.spot(place, per)
        part[yh, x, core, pl.ds(n * edge, edge)] = value

    product = multiply(False, splan, tiles, xtab.reshape(n_tiles, edge, feats), stash, put_part)
    next(product)
    reduce = reduce_col(s, p, "rc", part, *for_col)
    before, s.sent = s.sent, []
    next(reduce)
    drain(product)
    next(reduce)
    for c in before:
        c.wait_send()
    drain(reduce)

    agg = part[p.yh, p.x, p.core]
    pre = jnp.dot(agg, w[...], preferred_element_type=F32)
    logistic = jax.nn.sigmoid(pre)
    upstream = g[...].astype(F32)
    d_pre = (upstream * logistic * (1.0 + pre * (1.0 - logistic))).astype(BF16)
    e = lax.dot_general(d_pre, w[...], (((1,), (1,)), ((), ())), preferred_element_type=F32)
    etab[p.yh, p.x, p.core] = e.astype(BF16)
    before, s.sent = s.sent, []
    gather = gather_col(s, p, "gc", etab)
    next(gather)
    act_ref[...] = (pre * logistic).astype(BF16)
    wg = lax.dot_general(agg, d_pre, (((0,), (0,)), ((), ())), preferred_element_type=F32)
    wpart[...] = wg.reshape(wpart.shape)
    weights = sum_weight(s, p, q, wpart, wc, wd, wy, wz, wg_ref, scale)
    next(weights)
    for c in before:
        c.wait_send()
    for _ in range(3):
        next(gather)
    next(weights)
    drain(gather)
    next(weights)

    def put_back(place, value):
        yl, z, n = q.spot(place, per)
        back[yl, z, pl.ds(n * edge, edge)] = value

    product = multiply(True, splan, tiles, etab.reshape(n_tiles, edge, feats), stash, put_back)
    next(product)
    before, s.sent = s.sent, []
    reduce = reduce_row(s, q, "rr", back, *for_row)
    next(reduce)
    drain(product)
    next(reduce)
    next(weights)
    for c in before:
        c.wait_send()
    for _ in range(7):
        next(reduce)
    next(weights)
    for _ in range(5):
        next(reduce)
    next(weights)
    drain(reduce)
    grad_ref[...] = back[q.yl, q.z]
    drain(weights)
    s.finish()


def layer(*args):
    x, tiles, tile_rows = args[:3]
    rows, feats = x.shape
    slots, edge, _ = tiles.shape
    n_row, n_col, _ = tile_rows.shape
    n_yh = n_col // (2 * NX)
    n_tiles = n_col * rows // edge
    steps = (slots + n_tiles) // 2
    n_w = feats // n_col
    hbm = pl.BlockSpec(memory_space=pltpu.HBM)
    vmem = pltpu.VMEM
    return pl.pallas_call(
        functools.partial(layer_kernel, 1.0 / math.sqrt(rows * n_row * n_col)),
        out_shape=(
            vmem((rows, feats), BF16),
            vmem((rows, feats), BF16),
            vmem((n_yh, NX, 2, n_w, feats), F32),
        ),
        in_specs=[hbm] * 7,
        out_specs=[pl.BlockSpec(memory_space=vmem)] * 3,
        scratch_shapes=[
            vmem((n_row // NZ, NZ, rows, feats), BF16),
            vmem((n_yh, NX, 2, rows, feats), BF16),
            vmem((slots + 1, edge, edge), BF16),
            vmem((steps + 1, edge, feats), BF16),
            vmem((n_yh, NX, 2, rows, feats), BF16),
            vmem((n_row // NZ, NZ, rows, feats), BF16),
            vmem((8, PLACES), jnp.int32),
            pltpu.SMEM((8, PLACES), jnp.int32),
            vmem((n_col, slots), jnp.int32),
            vmem((n_col, slots), jnp.int32),
            pltpu.SMEM((n_row, n_col), jnp.int32),
            vmem((feats, feats), BF16),
            vmem((rows, feats), BF16),
            vmem((n_yh, NX, 2, n_w, feats), F32),
            vmem((n_yh, NX, n_w, feats), F32),
            vmem((n_yh * NX, n_w, feats), F32),
            vmem((2, n_w, feats), F32),
            vmem((NZ, n_w, feats), F32),
        ]
        + reduce_col_scratch(n_yh, NX, rows, feats)
        + reduce_row_scratch(rows, feats)
        + [
            pltpu.SemaphoreType.DMA((256,)),
            pltpu.SemaphoreType.DMA((256,)),
            pltpu.SemaphoreType.DMA((8,)),
        ],
        compiler_params=pltpu.CompilerParams(
            collective_id=1, has_side_effects=True, vmem_limit_bytes=48 << 20
        ),
        name="layer",
    )(*[pltpu.with_memory_space_constraint(a, pltpu.HBM) for a in args])


def per_device(node_features, tile_values, tile_rows, tile_cols, tile_count, weight, cotangent):
    act, grad, wgrad = layer(
        node_features[0, 0], tile_values[0, 0], tile_rows, tile_cols, tile_count, weight, cotangent[0, 0]
    )
    return act[None, None], grad[None, None], wgrad.reshape(weight.shape)


def solution(mesh):
    in_specs = (
        P("col", "row", None, None),
        P("row", "col", None, None, None),
        P(),
        P(),
        P(),
        P(),
        P("row", "col", None, None),
    )
    out_specs = (P("row", "col", None, None), P("col", "row", None, None), P())
    return jax.shard_map(
        per_device, mesh=mesh, in_specs=in_specs, out_specs=out_specs, check_vma=False
    )
```

```python
import functools
import math

import jax
import jax.numpy as jnp
from jax import lax
from jax.experimental import pallas as pl
from jax.experimental.pallas import tpu as pltpu
from jax.sharding import PartitionSpec as P

MESH = pl.DeviceIdType.MESH
F32 = jnp.float32
BF16 = jnp.bfloat16

NZ = 8
NX = 4
TILE = 128
PLACES = 256


class Sender:
    def __init__(self, send_sem, recv_sem):
        self.send_sem = send_sem
        self.recv_sem = recv_sem
        self.ids = {}
        self.sent = []

    def slot(self, key):
        if key not in self.ids:
            self.ids[key] = len(self.ids)
        return self.ids[key]

    def copy(self, key, src, dst, device_id):
        n = self.slot(key)
        return pltpu.make_async_remote_copy(
            src_ref=src,
            dst_ref=dst,
            send_sem=self.send_sem.at[n],
            recv_sem=self.recv_sem.at[n],
            device_id=device_id,
            device_id_type=MESH,
        )

    def send(self, key, src, dst, device_id):
        c = self.copy(key, src, dst, device_id)
        c.start()
        self.sent.append(c)

    def wait(self, key, dst, device_id):
        self.copy(key, dst, dst, device_id).wait_recv()

    def finish(self):
        for c in self.sent:
            c.wait_send()
        self.sent = []


class RowPlace:
    def __init__(self):
        me = lax.axis_index("row")
        self.yl = me // NZ
        self.z = lax.rem(me, NZ)
        self.right = {"row": self.at(self.yl, 1)}
        self.left = {"row": self.at(self.yl, NZ - 1)}
        self.across = {"row": self.at(1 - self.yl, 0)}

    def zat(self, hops):
        return lax.rem(self.z + hops + NZ, NZ)

    ORDER = (4, 5, 3, 6, 2, 7, 1, 0)

    def place(self, tile, per):
        block = tile // per
        hops = (block % NZ - self.z + NZ) % NZ
        rank = jnp.zeros_like(tile)
        for n, h in enumerate(self.ORDER):
            rank = jnp.where(hops == h, n, rank)
        return (rank * 2 + block // NZ) * per + tile % per

    def spot(self, place, per):
        return place // per % 2, self.zat(self.ORDER[place // (2 * per)]), place % per

    def at(self, yl, hops):
        return yl * NZ + self.zat(hops)


class ColPlace:
    def __init__(self):
        me = lax.axis_index("col")
        self.yh = me // (2 * NX)
        self.x = lax.rem(me // 2, NX)
        self.core = lax.rem(me, 2)
        self.right = {"col": self.at(self.yh, 1, self.core)}
        self.left = {"col": self.at(self.yh, NX - 1, self.core)}
        self.across = {"col": self.at(1 - self.yh, 0, self.core)}
        self.sibling = {"col": self.at(self.yh, 0, 1 - self.core)}
        self.mates = [(dy, h) for dy in (0, 1) for h in range(NX) if (dy, h) != (0, 0)]

    def mate(self, dy, h):
        return {"col": self.at(self.yh + dy - 2 * self.yh * dy, h, self.core)}

    def xat(self, hops):
        return lax.rem(self.x + hops + NX, NX)

    ORDER = (2, 1, 3, 0)

    def place(self, tile, per):
        block = tile // per
        hops = (block // 2 % NX - self.x + NX) % NX
        rank = jnp.zeros_like(tile)
        for n, h in enumerate(self.ORDER):
            rank = jnp.where(hops == h, n, rank)
        rank = rank + jnp.where(block % 2 == self.core, NX, 0)
        return (rank * 2 + block // (2 * NX)) * per + tile % per

    def spot(self, place, per):
        rank = place // (2 * per)
        core = self.core if rank >= NX else 1 - self.core
        return place // per % 2, self.xat(self.ORDER[rank % NX]), core, place % per

    def at(self, yh, hops, core):
        return (yh * NX + self.xat(hops)) * 2 + core


def order_slots(rows, row_place, cols, col_place, live, n_tiles, plan):
    slots = rows.shape[1]
    places = plan.shape[1]
    steps = (slots + n_tiles) // 2
    sub = lax.broadcasted_iota(jnp.int32, (slots, slots), 0)
    lane = lax.broadcasted_iota(jnp.int32, (slots, slots), 1)
    k_col = sub[:, :1]
    live_row, live_col = lane[:1] < live, sub[:, :1] < live
    tile = lax.broadcasted_iota(jnp.int32, (n_tiles, slots), 0)
    place = lax.broadcasted_iota(jnp.int32, (slots, places), 1)
    tile_sub = lax.broadcasted_iota(jnp.int32, (n_tiles, places), 0)
    tile_lane = lax.broadcasted_iota(jnp.int32, (n_tiles, places), 1)

    def turn(row):
        return jnp.sum(jnp.where(sub == lane, row, 0), axis=1, keepdims=True)

    out = []
    for key, source in ((row_place, cols), (col_place, rows)):
        same = (turn(key) == key) & (sub < lane) & live_col
        rank = jnp.sum(jnp.where(same, 1, 0), axis=0, keepdims=True)
        number = jnp.sum(jnp.where((tile == key) & live_row, 1, 0), axis=1, keepdims=True)
        pairs = (number + 1) >> 1
        base = 2 * jnp.sum(jnp.where(tile < key, pairs, 0), axis=0, keepdims=True)
        at = turn(jnp.where(live_row, base + rank, -1))
        hit = at == place
        slot = slots + jnp.sum(jnp.where(hit, k_col - slots, 0), axis=0, keepdims=True)
        read = jnp.sum(jnp.where(hit, turn(source), 0), axis=0, keepdims=True)
        fresh = jnp.sum(jnp.where(hit & (turn(rank) == 0), 1, 0), axis=0, keepdims=True)
        upto = jnp.sum(jnp.where(tile_sub <= tile_lane, pairs, 0), axis=0, keepdims=True)
        some = jnp.sum(jnp.where(tile_sub == tile_lane, number, 0), axis=0, keepdims=True)
        final = jnp.where(some > 0, upto - 1, steps)
        out += [slot, read, fresh, final]
    for n, x in enumerate(out):
        plan[pl.ds(n, 1)] = x


EARLY = 4
LOOPS = 2


def multiply(flip, plan, tiles, tab, stash, put):
    steps = stash.shape[0] - 1
    early = EARLY * tab.shape[0] // 2
    first = 4 if flip else 0
    side = 0 if flip else 1
    shape = stash.shape[1:]

    def run_steps(start, number, acc):
        def some(g, acc):
            for u in range(number // LOOPS):
                p = start + g * (number // LOOPS) + u
                k = [plan[first, 2 * p + i] for i in (0, 1)]
                q = [plan[first + 1, 2 * p + i] for i in (0, 1)]
                left = jnp.concatenate([tiles[i] for i in k], axis=side)
                right = jnp.concatenate([tab[i] for i in q], axis=0)
                prod = lax.dot_general(left, right, (((side,), (0,)), ((), ())), preferred_element_type=F32)
                fresh = plan[first + 2, 2 * p] == 1
                acc = jnp.where(fresh, 0.0, acc) + prod
                stash[p] = acc.astype(stash.dtype)
            return acc

        return lax.fori_loop(0, LOOPS, some, acc)

    stash[steps] = jnp.zeros(shape, stash.dtype)
    acc = run_steps(0, early, jnp.zeros(shape, F32))
    for t in range(EARLY):
        put(t, stash[plan[first + 3, t]])
    yield
    run_steps(early, steps - early, acc)
    for t in range(EARLY, tab.shape[0]):
        put(t, stash[plan[first + 3, t]])


def add_into(dst, *terms):
    total = dst[...].astype(F32)
    for t in terms:
        total = total + t[...].astype(F32)
    dst[...] = total.astype(dst.dtype)


def row_parts(rows):
    cut = (rows * 7 // 16) // 16 * 16
    rest = rows - cut
    return (0, cut, cut // 2 // 16 * 16), (cut, rest, -(-rest // 2 // 16) * 16)


def hop_rows(part, d, h):
    base, n, half = part
    if h < NZ // 2:
        return base, n
    return (base, half) if d == 1 else (base + half, n - half)


def gather_row(s, p, tag, own, tab):
    first, rest = row_parts(tab.shape[2])
    top = NZ // 2
    mine, other = p.yl, 1 - p.yl
    ways = ((1, p.right), (-1, p.left))

    def blk(yl, h, ds):
        return tab.at[yl, p.zat(h), pl.ds(*ds)]

    def push(key, b, to):
        s.send((tag,) + key, b, b, to)

    streams = (("b", mine, rest), ("a", mine, first), ("c", other, first))

    def begin(key, ds, to):
        s.send((tag,) + key, own.at[pl.ds(*ds)], blk(mine, 0, ds), to)

    begin(("ya",), first[:2], p.across)
    for name, yl, part in streams[:2]:
        for d, to in ways:
            begin((name, d, 1), part[:2], to)
    begin(("yb", 0), rest[:2], p.across)
    yield
    s.wait((tag, "ya"), blk(other, 0, first[:2]), p.across)
    for d, to in ways:
        push(("c", d, 1), blk(other, 0, first[:2]), to)
    for h in range(1, top + 1):
        for name, yl, part in streams:
            yield
            for d, to in ways:
                s.wait((tag, name, d, h), blk(yl, -d * h, hop_rows(part, d, h)), to)
                if h < top:
                    push((name, d, h + 1), blk(yl, -d * h, hop_rows(part, d, h + 1)), to)
                if name == "b" and (h < top or d == -1):
                    push(("yb", -d * h), blk(mine, -d * h, rest[:2]), p.across)
    yield
    for h in [0] + [d * h for h in range(1, top) for d in (1, -1)] + [top]:
        s.wait((tag, "yb", h), blk(other, h, rest[:2]), p.across)


def reduce_row(s, p, tag, part, ybuf, abuf, cbuf, bbuf, fbuf):
    first, rest = row_parts(part.shape[2])
    top = NZ // 2
    mine, other = p.yl, 1 - p.yl
    ways = ((1, p.right, 0), (-1, p.left, 1))
    streams = (("c", other, first, cbuf), ("a", mine, first, abuf), ("b", mine, rest, bbuf))

    def blk(yl, h, ds):
        return part.at[yl, p.zat(h), pl.ds(*ds)]

    def hop(name, yl, piece, buf, d, to, n, h):
        lo, m = hop_rows(piece, d, h)
        s.send((tag, name, d, h), blk(yl, d * h, (lo, m)), buf.at[h - 1, n, pl.ds(lo - piece[0], m)], to)

    def crossed(h):
        s.wait((tag, "yb", h), ybuf.at[h + top - 1], p.across)
        add_into(blk(mine, h, rest[:2]), ybuf.at[h + top - 1])

    s.send((tag, "yb", top), blk(other, top, rest[:2]), ybuf.at[2 * top - 1], p.across)
    for st in streams[:2]:
        for w in ways:
            hop(*st, *w, top)
    yield
    for h in [d * h for h in range(top - 1, 0, -1) for d in (1, -1)] + [0]:
        s.send((tag, "yb", h), blk(other, h, rest[:2]), ybuf.at[h + top - 1], p.across)
    yield
    crossed(top)
    for w in ways:
        hop(*streams[2], *w, top)
    for h in range(top - 1, 0, -1):
        for name, yl, piece, buf in streams:
            yield
            for d, to, n in ways:
                if name == "b":
                    crossed(d * h)
                lo, m = hop_rows(piece, d, h + 1)
                got = buf.at[h, n, pl.ds(lo - piece[0], m)]
                s.wait((tag, name, d, h + 1), got, to)
                add_into(blk(yl, d * h, (lo, m)), got)
                hop(name, yl, piece, buf, d, to, n, h)
    for name, yl, piece, buf in streams:
        yield
        for d, to, n in ways:
            s.wait((tag, name, d, 1), buf.at[0, n], to)
        if name == "b":
            crossed(0)
        add_into(blk(yl, 0, piece[:2]), buf.at[0, 0], buf.at[0, 1])
        if name == "c":
            s.send((tag, "f"), blk(other, 0, first[:2]), fbuf, p.across)
    yield
    s.wait((tag, "f"), fbuf, p.across)
    add_into(blk(mine, 0, first[:2]), fbuf)


def reduce_row_scratch(rows, feats):
    (_, m, _), (_, n, _) = row_parts(rows)
    top = NZ // 2
    return [
        pltpu.VMEM((NZ, n, feats), BF16),
        pltpu.VMEM((top, 2, m, feats), BF16),
        pltpu.VMEM((top, 2, m, feats), BF16),
        pltpu.VMEM((top, 2, n, feats), BF16),
        pltpu.VMEM((m, feats), BF16),
    ]


def col_parts(rows):
    na = rows // 2
    return na, rows - na


def reduce_col(s, p, tag, part, cbuf, xa2, xa1, xb2, xb1, yb, ya):
    na, nb = col_parts(part.shape[3])
    a_, b_ = pl.ds(0, na), pl.ds(na, nb)
    mine, other, core, sib = p.yh, 1 - p.yh, p.core, 1 - p.core
    ways = ((1, p.right, 0), (-1, p.left, 1))
    groups = (("o", other, 1), ("m", mine, 0))

    def a_cut(n):
        return pl.ds(n * (na // 2), na // 2)

    def b_cut(n, base):
        return pl.ds(base + n * (nb // 2), nb // 2)

    def whole(h):
        return cbuf.at[:, p.xat(h)]

    def crossed(h):
        s.wait((tag, "yb", h), yb.at[h % NX], p.across)
        add_into(part.at[mine, p.xat(h), core, b_], yb.at[h % NX])

    for h in (2, 1, -1, 0):
        s.send((tag, "c", h), part.at[:, p.xat(h), sib], whole(h), p.sibling)
        if h == 2:
            yield
    yield
    for h in (2, 1, -1, 0):
        s.wait((tag, "c", h), whole(h), p.sibling)
        add_into(part.at[:, p.xat(h), core], whole(h))
        if h == 2:
            for name, yh, i in groups:
                for d, to, n in ways:
                    s.send((tag, "xa2", name, d), part.at[yh, p.xat(2), core, a_cut(n)], xa2.at[i, a_cut(n)], to)
        s.send((tag, "yb", h), part.at[other, p.xat(h), core, b_], yb.at[h % NX], p.across)
    for name, yh, i in groups:
        yield
        for d, to, n in ways:
            s.wait((tag, "xa2", name, d), xa2.at[i, a_cut(n)], to)
            add_into(part.at[yh, p.xat(d), core, a_cut(n)], xa2.at[i, a_cut(n)])
            s.send((tag, "xa1", name, d), part.at[yh, p.xat(d), core, a_], xa1.at[n, i], to)
        if name == "o":
            yield
            crossed(2)
            for d, to, n in ways:
                s.send((tag, "xb2", d), part.at[mine, p.xat(2), core, b_cut(n, na)], xb2.at[b_cut(n, 0)], to)
    yield
    name, yh, i = groups[0]
    for d, to, n in ways:
        s.wait((tag, "xa1", name, d), xa1.at[n, i], to)
    add_into(part.at[yh, p.x, core, a_], xa1.at[0, i], xa1.at[1, i])
    s.send((tag, "ya"), part.at[other, p.x, core, a_], ya, p.across)
    yield
    for d, to, n in ways:
        crossed(d)
        s.wait((tag, "xb2", d), xb2.at[b_cut(n, 0)], to)
        add_into(part.at[mine, p.xat(d), core, b_cut(n, na)], xb2.at[b_cut(n, 0)])
        s.send((tag, "xb1", d), part.at[mine, p.xat(d), core, b_], xb1.at[n], to)
    yield
    name, yh, i = groups[1]
    for d, to, n in ways:
        s.wait((tag, "xa1", name, d), xa1.at[n, i], to)
    add_into(part.at[yh, p.x, core, a_], xa1.at[0, i], xa1.at[1, i])
    s.wait((tag, "yb", 0), yb.at[0], p.across)
    yield
    for d, to, n in ways:
        s.wait((tag, "xb1", d), xb1.at[n], to)
    add_into(part.at[mine, p.x, core, b_], yb.at[0], xb1.at[0], xb1.at[1])
    yield
    s.wait((tag, "ya"), ya, p.across)
    add_into(part.at[mine, p.x, core, a_], ya)


def reduce_col_scratch(n_yh, n_x, rows, feats):
    na, nb = col_parts(rows)
    return [
        pltpu.VMEM((n_yh, n_x, rows, feats), BF16),
        pltpu.VMEM((n_yh, na, feats), BF16),
        pltpu.VMEM((2, n_yh, na, feats), BF16),
        pltpu.VMEM((nb, feats), BF16),
        pltpu.VMEM((2, nb, feats), BF16),
        pltpu.VMEM((n_x, nb, feats), BF16),
        pltpu.VMEM((na, feats), BF16),
    ]


def gather_col(s, p, tag, tab):
    na, nb = col_parts(tab.shape[3])
    a_, b_ = pl.ds(0, na), pl.ds(na, nb)
    mine, other, core = p.yh, 1 - p.yh, p.core
    ways = ((1, p.right, 0), (-1, p.left, 1))

    def a_cut(n):
        return pl.ds(n * (na // 2), na // 2)

    def b_cut(n):
        return pl.ds(na + n * (nb // 2), nb // 2)

    def blk(yh, h, ds):
        return tab.at[yh, p.xat(h), core, ds]

    def push(key, b, to):
        s.send((tag,) + key, b, b, to)

    def took(key, b):
        s.wait((tag,) + key, b, p.sibling)

    def share(h, name, ds):
        push(("c", h, name), tab.at[:, p.xat(h), core, ds], p.sibling)

    push(("ya",), blk(mine, 0, a_), p.across)
    for d, to, n in ways:
        push(("b", d), blk(mine, 0, b_), to)
    for d, to, n in ways:
        push(("m", d), blk(mine, 0, a_), to)
    push(("yb", 0), blk(mine, 0, b_), p.across)
    yield
    for d, to, n in ways:
        took(("b", d), blk(mine, -d, b_))
        push(("b2", d), blk(mine, -d, b_cut(n)), to)
        push(("yb", -d), blk(mine, -d, b_), p.across)
    yield
    took(("ya",), blk(other, 0, a_))
    for d, to, n in ways:
        push(("o", d), blk(other, 0, a_), to)
    share(0, "a", a_)
    yield
    for d, to, n in ways:
        took(("m", d), blk(mine, -d, a_))
        push(("m2", d), blk(mine, -d, a_cut(n)), to)
    took(("yb", 0), blk(other, 0, b_))
    share(0, "b", b_)
    yield
    for d, to, n in ways:
        took(("b2", d), blk(mine, 2, b_cut(n)))
    push(("yb", 2), blk(mine, 2, b_), p.across)
    yield
    for d, to, n in ways:
        took(("o", d), blk(other, -d, a_))
        push(("o2", d), blk(other, -d, a_cut(n)), to)
        share(-d, "a", a_)
    yield
    for d in (1, -1):
        took(("yb", d), blk(other, d, b_))
        share(d, "b", b_)
    yield
    for name, yh in (("m2", mine), ("o2", other)):
        for d, to, n in ways:
            took((name, d), blk(yh, 2, a_cut(n)))
    share(2, "a", a_)
    took(("yb", 2), blk(other, 2, b_))
    share(2, "b", b_)
    yield
    for h in (0, 1, -1, 2):
        for name, ds in (("a", a_), ("b", b_)):
            s.wait((tag, "c", h, name), tab.at[:, p.xat(h), 1 - core, ds], p.sibling)


def sum_weight(s, p, q, wpart, wc, wd, wy, wz, wtab, scale):
    core, sib = p.core, 1 - p.core
    s.send("wc", wpart.at[:, :, sib], wc, p.sibling)
    yield
    s.wait("wc", wc, p.sibling)
    mine = wpart.at[:, :, core]
    mine[...] = mine[...] + wc[...]
    for dy, h in p.mates:
        yh = p.yh + dy - 2 * p.yh * dy
        s.send(("wd", dy, h), wpart.at[yh, p.xat(h), core], wd.at[dy * NX + h], p.mate(dy, h))
    yield
    total = wpart[p.yh, p.x, core]
    for dy, h in p.mates:
        s.wait(("wd", dy, h), wd.at[dy * NX + h], p.mate(dy, h))
        total = total + wd[dy * NX + h]
    wy[0] = total
    s.send("wy", wy.at[0], wy.at[1], q.across)
    yield
    s.wait("wy", wy.at[1], q.across)
    wz[q.z] = wy[0] + wy[1]
    for h in range(1, NZ):
        s.send(("wz", h), wz.at[q.z], wz.at[q.z], {"row": q.at(q.yl, h)})
    yield
    for h in range(1, NZ):
        s.wait(("wz", h), wz.at[q.zat(-h)], q.across)
    total = wz[0]
    for z in range(1, NZ):
        total = total + wz[z]
    own = wtab.at[p.yh, p.x, core]
    own[...] = total * scale
    for dy, h in p.mates:
        s.send(("w", dy, h), own, own, p.mate(dy, h))
    yield
    for dy, h in p.mates:
        yh = p.yh + dy - 2 * p.yh * dy
        s.wait(("w", dy, h), wtab.at[yh, p.xat(-h), core], p.sibling)
    s.send("ws", wtab.at[:, :, core], wtab.at[:, :, core], p.sibling)
    yield
    s.wait("ws", wtab.at[:, :, sib], p.sibling)


def drain(steps):
    for _ in steps:
        pass


def layer_kernel(
    scale, x_ref, tiles_ref, tr_ref, tc_ref, cnt_ref, w_ref, g_ref, out_ref, wg_ref,
    xtab, etab, tiles, stash, part, back, plan, splan, tr, tc, cnt, w, g, wpart, wc, wd, wy, wz, *rest,
):
    n_col, n_row = 7, 5
    for_col, for_row, (send_sem, recv_sem, sems) = rest[:n_col], rest[n_col : n_col + n_row], rest[n_col + n_row :]
    slots, edge, _ = tiles_ref.shape
    rows, feats = x_ref.shape
    per = rows // edge
    p, q = ColPlace(), RowPlace()
    mr, mc = lax.axis_index("row"), lax.axis_index("col")

    barrier = pltpu.get_barrier_semaphore()
    peers = [p.sibling, q.across] + [p.mate(dy, h) for dy, h in p.mates]
    peers += [{"row": q.at(q.yl, h)} for h in range(1, NZ)]
    for peer in peers:
        pl.semaphore_signal(barrier, inc=1, device_id=peer, device_id_type=MESH)
    loads = [
        pltpu.make_async_copy(tr_ref.at[mr], tr, sems.at[0]),
        pltpu.make_async_copy(tc_ref.at[mr], tc, sems.at[1]),
        pltpu.make_async_copy(cnt_ref, cnt, sems.at[2]),
        pltpu.make_async_copy(x_ref, xtab.at[q.yl, q.z], sems.at[3]),
        pltpu.make_async_copy(tiles_ref, tiles.at[pl.ds(0, slots)], sems.at[4]),
        pltpu.make_async_copy(w_ref, w, sems.at[5]),
        pltpu.make_async_copy(g_ref, g, sems.at[6]),
    ]
    for c in loads:
        c.start()
    tiles[slots] = jnp.zeros((edge, edge), tiles.dtype)
    pl.semaphore_wait(barrier, len(peers))

    s = Sender(send_sem, recv_sem)
    gather = gather_row(s, q, "gr", x_ref, xtab)
    next(gather)
    n_tiles = stash.shape[0] * 2 - 2 - slots
    for c in loads[:3]:
        c.wait()
    t_rows, t_cols = tr[pl.ds(mc, 1)], tc[pl.ds(mc, 1)]
    order_slots(t_rows, p.place(t_rows, per), t_cols, q.place(t_cols, per), cnt[mr, mc], n_tiles, plan)
    to_scalars = pltpu.make_async_copy(plan, splan, sems.at[7])
    to_scalars.start()
    drain(gather)
    to_scalars.wait()
    for c in loads[3:]:
        c.wait()

    def put_part(place, value):
        yh, x, core, n = p.spot(place, per)
        part[yh, x, core, pl.ds(n * edge, edge)] = value

    product = multiply(False, splan, tiles, xtab.reshape(n_tiles, edge, feats), stash, put_part)
    next(product)
    reduce = reduce_col(s, p, "rc", part, *for_col)
    before, s.sent = s.sent, []
    next(reduce)
    drain(product)
    next(reduce)
    for c in before:
        c.wait_send()
    drain(reduce)

    agg = part[p.yh, p.x, p.core]
    pre = jnp.dot(agg, w[...], preferred_element_type=F32)
    logistic = jax.nn.sigmoid(pre)
    upstream = g[...].astype(F32)
    d_pre = (upstream * logistic * (1.0 + pre * (1.0 - logistic))).astype(BF16)
    e = lax.dot_general(d_pre, w[...], (((1,), (1,)), ((), ())), preferred_element_type=F32)
    etab[p.yh, p.x, p.core] = e.astype(BF16)
    before, s.sent = s.sent, []
    gather = gather_col(s, p, "gc", etab)
    next(gather)
    out_ref[0] = (pre * logistic).astype(BF16)
    wg = lax.dot_general(agg, d_pre, (((0,), (0,)), ((), ())), preferred_element_type=F32)
    wpart[...] = wg.reshape(wpart.shape)
    weights = sum_weight(s, p, q, wpart, wc, wd, wy, wz, wg_ref, scale)
    next(weights)
    for c in before:
        c.wait_send()
    for _ in range(3):
        next(gather)
    next(weights)
    drain(gather)
    next(weights)

    def put_back(place, value):
        yl, z, n = q.spot(place, per)
        back[yl, z, pl.ds(n * edge, edge)] = value

    product = multiply(True, splan, tiles, etab.reshape(n_tiles, edge, feats), stash, put_back)
    next(product)
    before, s.sent = s.sent, []
    reduce = reduce_row(s, q, "rr", back, *for_row)
    next(reduce)
    drain(product)
    next(reduce)
    next(weights)
    for c in before:
        c.wait_send()
    for _ in range(7):
        next(reduce)
    next(weights)
    for _ in range(5):
        next(reduce)
    next(weights)
    drain(reduce)
    out_ref[1] = back[q.yl, q.z]
    drain(weights)
    s.finish()


def layer(*args):
    x, tiles, tile_rows = args[:3]
    rows, feats = x.shape
    slots, edge, _ = tiles.shape
    n_row, n_col, _ = tile_rows.shape
    n_yh = n_col // (2 * NX)
    n_tiles = n_col * rows // edge
    steps = (slots + n_tiles) // 2
    n_w = feats // n_col
    hbm = pl.BlockSpec(memory_space=pltpu.HBM)
    vmem = pltpu.VMEM
    return pl.pallas_call(
        functools.partial(layer_kernel, 1.0 / math.sqrt(rows * n_row * n_col)),
        out_shape=(
            vmem((2, rows, feats), BF16),
            vmem((n_yh, NX, 2, n_w, feats), F32),
        ),
        in_specs=[hbm] * 7,
        out_specs=[pl.BlockSpec(memory_space=vmem)] * 2,
        scratch_shapes=[
            vmem((n_row // NZ, NZ, rows, feats), BF16),
            vmem((n_yh, NX, 2, rows, feats), BF16),
            vmem((slots + 1, edge, edge), BF16),
            vmem((steps + 1, edge, feats), BF16),
            vmem((n_yh, NX, 2, rows, feats), BF16),
            vmem((n_row // NZ, NZ, rows, feats), BF16),
            vmem((8, PLACES), jnp.int32),
            pltpu.SMEM((8, PLACES), jnp.int32),
            vmem((n_col, slots), jnp.int32),
            vmem((n_col, slots), jnp.int32),
            pltpu.SMEM((n_row, n_col), jnp.int32),
            vmem((feats, feats), BF16),
            vmem((rows, feats), BF16),
            vmem((n_yh, NX, 2, n_w, feats), F32),
            vmem((n_yh, NX, n_w, feats), F32),
            vmem((n_yh * NX, n_w, feats), F32),
            vmem((2, n_w, feats), F32),
            vmem((NZ, n_w, feats), F32),
        ]
        + reduce_col_scratch(n_yh, NX, rows, feats)
        + reduce_row_scratch(rows, feats)
        + [
            pltpu.SemaphoreType.DMA((256,)),
            pltpu.SemaphoreType.DMA((256,)),
            pltpu.SemaphoreType.DMA((8,)),
        ],
        compiler_params=pltpu.CompilerParams(
            collective_id=1, has_side_effects=True, vmem_limit_bytes=48 << 20
        ),
        name="layer",
    )(*[pltpu.with_memory_space_constraint(a, pltpu.HBM) for a in args])


def per_device(node_features, tile_values, tile_rows, tile_cols, tile_count, weight, cotangent):
    results, wgrad = layer(
        node_features[0, 0], tile_values[0, 0], tile_rows, tile_cols, tile_count, weight, cotangent[0, 0]
    )
    return results[:1, None], results[1:, None], wgrad.reshape(weight.shape)


def solution(mesh):
    in_specs = (
        P("col", "row", None, None),
        P("row", "col", None, None, None),
        P(),
        P(),
        P(),
        P(),
        P("row", "col", None, None),
    )
    out_specs = (P("row", "col", None, None), P("col", "row", None, None), P())
    return jax.shard_map(
        per_device, mesh=mesh, in_specs=in_specs, out_specs=out_specs, check_vma=False
    )
```

```python
import functools
import math

import jax
import jax.numpy as jnp
from jax import lax
from jax.experimental import pallas as pl
from jax.experimental.pallas import tpu as pltpu
from jax.sharding import PartitionSpec as P

MESH = pl.DeviceIdType.MESH
F32 = jnp.float32
BF16 = jnp.bfloat16

NZ = 8
NX = 4
TILE = 128
PLACES = 256


class Sender:
    def __init__(self, send_sem, recv_sem):
        self.send_sem = send_sem
        self.recv_sem = recv_sem
        self.ids = {}
        self.sent = []

    def slot(self, key):
        if key not in self.ids:
            self.ids[key] = len(self.ids)
        return self.ids[key]

    def copy(self, key, src, dst, device_id):
        n = self.slot(key)
        return pltpu.make_async_remote_copy(
            src_ref=src,
            dst_ref=dst,
            send_sem=self.send_sem.at[n],
            recv_sem=self.recv_sem.at[n],
            device_id=device_id,
            device_id_type=MESH,
        )

    def send(self, key, src, dst, device_id):
        c = self.copy(key, src, dst, device_id)
        c.start()
        self.sent.append(c)

    def wait(self, key, dst, device_id):
        self.copy(key, dst, dst, device_id).wait_recv()

    def finish(self):
        for c in self.sent:
            c.wait_send()
        self.sent = []


class RowPlace:
    def __init__(self):
        me = lax.axis_index("row")
        self.yl = me // NZ
        self.z = lax.rem(me, NZ)
        self.right = {"row": self.at(self.yl, 1)}
        self.left = {"row": self.at(self.yl, NZ - 1)}
        self.across = {"row": self.at(1 - self.yl, 0)}

    def zat(self, hops):
        return lax.rem(self.z + hops + NZ, NZ)

    ORDER = (4, 3, 5, 2, 6, 1, 7, 0)

    def place(self, tile, per):
        block = tile // per
        hops = (block % NZ - self.z + NZ) % NZ
        rank = jnp.zeros_like(tile)
        for n, h in enumerate(self.ORDER):
            rank = jnp.where(hops == h, n, rank)
        return (rank * 2 + block // NZ) * per + tile % per

    def spot(self, place, per):
        return place // per % 2, self.zat(self.ORDER[place // (2 * per)]), place % per

    def at(self, yl, hops):
        return yl * NZ + self.zat(hops)


class ColPlace:
    def __init__(self):
        me = lax.axis_index("col")
        self.yh = me // (2 * NX)
        self.x = lax.rem(me // 2, NX)
        self.core = lax.rem(me, 2)
        self.right = {"col": self.at(self.yh, 1, self.core)}
        self.left = {"col": self.at(self.yh, NX - 1, self.core)}
        self.across = {"col": self.at(1 - self.yh, 0, self.core)}
        self.sibling = {"col": self.at(self.yh, 0, 1 - self.core)}
        self.mates = [(dy, h) for dy in (0, 1) for h in range(NX) if (dy, h) != (0, 0)]

    def mate(self, dy, h):
        return {"col": self.at(self.yh + dy - 2 * self.yh * dy, h, self.core)}

    def xat(self, hops):
        return lax.rem(self.x + hops + NX, NX)

    ORDER = (2, 1, 3, 0)

    def place(self, tile, per):
        block = tile // per
        hops = (block // 2 % NX - self.x + NX) % NX
        rank = jnp.zeros_like(tile)
        for n, h in enumerate(self.ORDER):
            rank = jnp.where(hops == h, n, rank)
        rank = rank + jnp.where(block % 2 == self.core, NX, 0)
        return (rank * 2 + block // (2 * NX)) * per + tile % per

    def spot(self, place, per):
        rank = place // (2 * per)
        core = self.core if rank >= NX else 1 - self.core
        return place // per % 2, self.xat(self.ORDER[rank % NX]), core, place % per

    def at(self, yh, hops, core):
        return (yh * NX + self.xat(hops)) * 2 + core


def order_slots(rows, row_place, cols, col_place, live, n_tiles, plan):
    slots = rows.shape[1]
    places = plan.shape[1]
    steps = (slots + n_tiles) // 2
    sub = lax.broadcasted_iota(jnp.int32, (slots, slots), 0)
    lane = lax.broadcasted_iota(jnp.int32, (slots, slots), 1)
    k_col = sub[:, :1]
    live_row, live_col = lane[:1] < live, sub[:, :1] < live
    tile = lax.broadcasted_iota(jnp.int32, (n_tiles, slots), 0)
    place = lax.broadcasted_iota(jnp.int32, (slots, places), 1)
    tile_sub = lax.broadcasted_iota(jnp.int32, (n_tiles, places), 0)
    tile_lane = lax.broadcasted_iota(jnp.int32, (n_tiles, places), 1)

    def turn(row):
        return jnp.sum(jnp.where(sub == lane, row, 0), axis=1, keepdims=True)

    out = []
    for key, source in ((row_place, cols), (col_place, rows)):
        same = (turn(key) == key) & (sub < lane) & live_col
        rank = jnp.sum(jnp.where(same, 1, 0), axis=0, keepdims=True)
        number = jnp.sum(jnp.where((tile == key) & live_row, 1, 0), axis=1, keepdims=True)
        pairs = (number + 1) >> 1
        base = 2 * jnp.sum(jnp.where(tile < key, pairs, 0), axis=0, keepdims=True)
        at = turn(jnp.where(live_row, base + rank, -1))
        hit = at == place
        slot = slots + jnp.sum(jnp.where(hit, k_col - slots, 0), axis=0, keepdims=True)
        read = jnp.sum(jnp.where(hit, turn(source), 0), axis=0, keepdims=True)
        fresh = jnp.sum(jnp.where(hit & (turn(rank) == 0), 1, 0), axis=0, keepdims=True)
        upto = jnp.sum(jnp.where(tile_sub <= tile_lane, pairs, 0), axis=0, keepdims=True)
        some = jnp.sum(jnp.where(tile_sub == tile_lane, number, 0), axis=0, keepdims=True)
        final = jnp.where(some > 0, upto - 1, steps)
        out += [slot, read, fresh, final]
    for n, x in enumerate(out):
        plan[pl.ds(n, 1)] = x


EARLY = 4
LOOPS = 2


def multiply(flip, plan, tiles, tab, stash, put):
    steps = stash.shape[0] - 1
    early = EARLY * tab.shape[0] // 2
    first = 4 if flip else 0
    side = 0 if flip else 1
    shape = stash.shape[1:]

    def run_steps(start, number, acc):
        def some(g, acc):
            for u in range(number // LOOPS):
                p = start + g * (number // LOOPS) + u
                k = [plan[first, 2 * p + i] for i in (0, 1)]
                q = [plan[first + 1, 2 * p + i] for i in (0, 1)]
                left = jnp.concatenate([tiles[i] for i in k], axis=side)
                right = jnp.concatenate([tab[i] for i in q], axis=0)
                prod = lax.dot_general(left, right, (((side,), (0,)), ((), ())), preferred_element_type=F32)
                fresh = plan[first + 2, 2 * p] == 1
                acc = jnp.where(fresh, 0.0, acc) + prod
                stash[p] = acc.astype(stash.dtype)
            return acc

        return lax.fori_loop(0, LOOPS, some, acc)

    stash[steps] = jnp.zeros(shape, stash.dtype)
    acc = run_steps(0, early, jnp.zeros(shape, F32))
    for t in range(EARLY):
        put(t, stash[plan[first + 3, t]])
    yield
    run_steps(early, steps - early, acc)
    for t in range(EARLY, tab.shape[0]):
        put(t, stash[plan[first + 3, t]])
        if (t + 1) % EARLY == 0:
            yield


def add_into(dst, *terms):
    total = dst[...].astype(F32)
    for t in terms:
        total = total + t[...].astype(F32)
    dst[...] = total.astype(dst.dtype)


def row_parts(rows):
    cut = (rows * 7 // 16) // 16 * 16
    rest = rows - cut
    return (0, cut, cut // 2 // 16 * 16), (cut, rest, -(-rest // 2 // 16) * 16)


def hop_rows(part, d, h):
    base, n, half = part
    if h < NZ // 2:
        return base, n
    return (base, half) if d == 1 else (base + half, n - half)


def gather_row(s, p, tag, own, tab):
    first, rest = row_parts(tab.shape[2])
    top = NZ // 2
    mine, other = p.yl, 1 - p.yl
    ways = ((1, p.right), (-1, p.left))

    def blk(yl, h, ds):
        return tab.at[yl, p.zat(h), pl.ds(*ds)]

    def push(key, b, to):
        s.send((tag,) + key, b, b, to)

    streams = (("b", mine, rest), ("a", mine, first), ("c", other, first))

    def begin(key, ds, to):
        s.send((tag,) + key, own.at[pl.ds(*ds)], blk(mine, 0, ds), to)

    begin(("ya",), first[:2], p.across)
    for name, yl, part in streams[:2]:
        for d, to in ways:
            begin((name, d, 1), part[:2], to)
    begin(("yb", 0), rest[:2], p.across)
    yield
    s.wait((tag, "ya"), blk(other, 0, first[:2]), p.across)
    for d, to in ways:
        push(("c", d, 1), blk(other, 0, first[:2]), to)
    for h in range(1, top + 1):
        for name, yl, part in streams:
            yield
            for d, to in ways:
                s.wait((tag, name, d, h), blk(yl, -d * h, hop_rows(part, d, h)), to)
                if h < top:
                    push((name, d, h + 1), blk(yl, -d * h, hop_rows(part, d, h + 1)), to)
                if name == "b" and (h < top or d == -1):
                    push(("yb", -d * h), blk(mine, -d * h, rest[:2]), p.across)
    yield
    for h in [0] + [d * h for h in range(1, top) for d in (1, -1)] + [top]:
        s.wait((tag, "yb", h), blk(other, h, rest[:2]), p.across)


def reduce_row(s, p, tag, part, ybuf, abuf, cbuf, bbuf, fbuf):
    first, rest = row_parts(part.shape[2])
    top = NZ // 2
    mine, other = p.yl, 1 - p.yl
    ways = ((1, p.right, 0), (-1, p.left, 1))
    streams = (("c", other, first, cbuf), ("a", mine, first, abuf), ("b", mine, rest, bbuf))

    def blk(yl, h, ds):
        return part.at[yl, p.zat(h), pl.ds(*ds)]

    def hop(name, yl, piece, buf, d, to, n, h):
        lo, m = hop_rows(piece, d, h)
        s.send((tag, name, d, h), blk(yl, d * h, (lo, m)), buf.at[h - 1, n, pl.ds(lo - piece[0], m)], to)

    def crossed(h):
        s.wait((tag, "yb", h), ybuf.at[h + top - 1], p.across)
        add_into(blk(mine, h, rest[:2]), ybuf.at[h + top - 1])

    s.send((tag, "yb", top), blk(other, top, rest[:2]), ybuf.at[2 * top - 1], p.across)
    for st in streams[:2]:
        for w in ways:
            hop(*st, *w, top)
    yield
    for h in [d * h for h in range(top - 1, 0, -1) for d in (1, -1)] + [0]:
        s.send((tag, "yb", h), blk(other, h, rest[:2]), ybuf.at[h + top - 1], p.across)
        yield
    crossed(top)
    for w in ways:
        hop(*streams[2], *w, top)
    for h in range(top - 1, 0, -1):
        for name, yl, piece, buf in streams:
            yield
            for d, to, n in ways:
                if name == "b":
                    crossed(d * h)
                lo, m = hop_rows(piece, d, h + 1)
                got = buf.at[h, n, pl.ds(lo - piece[0], m)]
                s.wait((tag, name, d, h + 1), got, to)
                add_into(blk(yl, d * h, (lo, m)), got)
                hop(name, yl, piece, buf, d, to, n, h)
    for name, yl, piece, buf in streams:
        yield
        for d, to, n in ways:
            s.wait((tag, name, d, 1), buf.at[0, n], to)
        if name == "b":
            crossed(0)
        add_into(blk(yl, 0, piece[:2]), buf.at[0, 0], buf.at[0, 1])
        if name == "c":
            s.send((tag, "f"), blk(other, 0, first[:2]), fbuf, p.across)
    yield
    s.wait((tag, "f"), fbuf, p.across)
    add_into(blk(mine, 0, first[:2]), fbuf)


def reduce_row_scratch(rows, feats):
    (_, m, _), (_, n, _) = row_parts(rows)
    top = NZ // 2
    return [
        pltpu.VMEM((NZ, n, feats), BF16),
        pltpu.VMEM((top, 2, m, feats), BF16),
        pltpu.VMEM((top, 2, m, feats), BF16),
        pltpu.VMEM((top, 2, n, feats), BF16),
        pltpu.VMEM((m, feats), BF16),
    ]


def col_parts(rows):
    na = rows // 2
    return na, rows - na


def reduce_col(s, p, tag, part, cbuf, xa2, xa1, xb2, xb1, yb, ya):
    na, nb = col_parts(part.shape[3])
    a_, b_ = pl.ds(0, na), pl.ds(na, nb)
    mine, other, core, sib = p.yh, 1 - p.yh, p.core, 1 - p.core
    ways = ((1, p.right, 0), (-1, p.left, 1))
    groups = (("o", other, 1), ("m", mine, 0))

    def a_cut(n):
        return pl.ds(n * (na // 2), na // 2)

    def b_cut(n, base):
        return pl.ds(base + n * (nb // 2), nb // 2)

    def whole(h):
        return cbuf.at[:, p.xat(h)]

    def crossed(h):
        s.wait((tag, "yb", h), yb.at[h % NX], p.across)
        add_into(part.at[mine, p.xat(h), core, b_], yb.at[h % NX])

    for h in (2, 1, -1, 0):
        s.send((tag, "c", h), part.at[:, p.xat(h), sib], whole(h), p.sibling)
        yield
    for h in (2, 1, -1, 0):
        s.wait((tag, "c", h), whole(h), p.sibling)
        add_into(part.at[:, p.xat(h), core], whole(h))
        if h == 2:
            for name, yh, i in groups:
                for d, to, n in ways:
                    s.send((tag, "xa2", name, d), part.at[yh, p.xat(2), core, a_cut(n)], xa2.at[i, a_cut(n)], to)
        s.send((tag, "yb", h), part.at[other, p.xat(h), core, b_], yb.at[h % NX], p.across)
    for name, yh, i in groups:
        yield
        for d, to, n in ways:
            s.wait((tag, "xa2", name, d), xa2.at[i, a_cut(n)], to)
            add_into(part.at[yh, p.xat(d), core, a_cut(n)], xa2.at[i, a_cut(n)])
            s.send((tag, "xa1", name, d), part.at[yh, p.xat(d), core, a_], xa1.at[n, i], to)
        if name == "o":
            yield
            crossed(2)
            for d, to, n in ways:
                s.send((tag, "xb2", d), part.at[mine, p.xat(2), core, b_cut(n, na)], xb2.at[b_cut(n, 0)], to)
    yield
    name, yh, i = groups[0]
    for d, to, n in ways:
        s.wait((tag, "xa1", name, d), xa1.at[n, i], to)
    add_into(part.at[yh, p.x, core, a_], xa1.at[0, i], xa1.at[1, i])
    s.send((tag, "ya"), part.at[other, p.x, core, a_], ya, p.across)
    yield
    for d, to, n in ways:
        crossed(d)
        s.wait((tag, "xb2", d), xb2.at[b_cut(n, 0)], to)
        add_into(part.at[mine, p.xat(d), core, b_cut(n, na)], xb2.at[b_cut(n, 0)])
        s.send((tag, "xb1", d), part.at[mine, p.xat(d), core, b_], xb1.at[n], to)
    yield
    name, yh, i = groups[1]
    for d, to, n in ways:
        s.wait((tag, "xa1", name, d), xa1.at[n, i], to)
    add_into(part.at[yh, p.x, core, a_], xa1.at[0, i], xa1.at[1, i])
    s.wait((tag, "yb", 0), yb.at[0], p.across)
    yield
    for d, to, n in ways:
        s.wait((tag, "xb1", d), xb1.at[n], to)
    add_into(part.at[mine, p.x, core, b_], yb.at[0], xb1.at[0], xb1.at[1])
    yield
    s.wait((tag, "ya"), ya, p.across)
    add_into(part.at[mine, p.x, core, a_], ya)


def reduce_col_scratch(n_yh, n_x, rows, feats):
    na, nb = col_parts(rows)
    return [
        pltpu.VMEM((n_yh, n_x, rows, feats), BF16),
        pltpu.VMEM((n_yh, na, feats), BF16),
        pltpu.VMEM((2, n_yh, na, feats), BF16),
        pltpu.VMEM((nb, feats), BF16),
        pltpu.VMEM((2, nb, feats), BF16),
        pltpu.VMEM((n_x, nb, feats), BF16),
        pltpu.VMEM((na, feats), BF16),
    ]


def gather_col(s, p, tag, tab):
    na, nb = col_parts(tab.shape[3])
    a_, b_ = pl.ds(0, na), pl.ds(na, nb)
    mine, other, core = p.yh, 1 - p.yh, p.core
    ways = ((1, p.right, 0), (-1, p.left, 1))

    def a_cut(n):
        return pl.ds(n * (na // 2), na // 2)

    def b_cut(n):
        return pl.ds(na + n * (nb // 2), nb // 2)

    def blk(yh, h, ds):
        return tab.at[yh, p.xat(h), core, ds]

    def push(key, b, to):
        s.send((tag,) + key, b, b, to)

    def took(key, b):
        s.wait((tag,) + key, b, p.sibling)

    def share(h, name, ds):
        push(("c", h, name), tab.at[:, p.xat(h), core, ds], p.sibling)

    push(("ya",), blk(mine, 0, a_), p.across)
    for d, to, n in ways:
        push(("b", d), blk(mine, 0, b_), to)
    for d, to, n in ways:
        push(("m", d), blk(mine, 0, a_), to)
    push(("yb", 0), blk(mine, 0, b_), p.across)
    yield
    for d, to, n in ways:
        took(("b", d), blk(mine, -d, b_))
        push(("b2", d), blk(mine, -d, b_cut(n)), to)
        push(("yb", -d), blk(mine, -d, b_), p.across)
    yield
    took(("ya",), blk(other, 0, a_))
    for d, to, n in ways:
        push(("o", d), blk(other, 0, a_), to)
    share(0, "a", a_)
    yield
    for d, to, n in ways:
        took(("m", d), blk(mine, -d, a_))
        push(("m2", d), blk(mine, -d, a_cut(n)), to)
    took(("yb", 0), blk(other, 0, b_))
    share(0, "b", b_)
    yield
    for d, to, n in ways:
        took(("b2", d), blk(mine, 2, b_cut(n)))
    push(("yb", 2), blk(mine, 2, b_), p.across)
    yield
    for d, to, n in ways:
        took(("o", d), blk(other, -d, a_))
        push(("o2", d), blk(other, -d, a_cut(n)), to)
        share(-d, "a", a_)
    yield
    for d in (1, -1):
        took(("yb", d), blk(other, d, b_))
        share(d, "b", b_)
    yield
    for name, yh in (("m2", mine), ("o2", other)):
        for d, to, n in ways:
            took((name, d), blk(yh, 2, a_cut(n)))
    share(2, "a", a_)
    took(("yb", 2), blk(other, 2, b_))
    share(2, "b", b_)
    yield
    for h in (0, 1, -1, 2):
        for name, ds in (("a", a_), ("b", b_)):
            s.wait((tag, "c", h, name), tab.at[:, p.xat(h), 1 - core, ds], p.sibling)


def sum_weight(s, p, q, wpart, wc, wd, wy, wz, wtab, scale):
    core, sib = p.core, 1 - p.core
    s.send("wc", wpart.at[:, :, sib], wc, p.sibling)
    yield
    s.wait("wc", wc, p.sibling)
    mine = wpart.at[:, :, core]
    mine[...] = mine[...] + wc[...]
    for dy, h in p.mates:
        yh = p.yh + dy - 2 * p.yh * dy
        s.send(("wd", dy, h), wpart.at[yh, p.xat(h), core], wd.at[dy * NX + h], p.mate(dy, h))
    yield
    total = wpart[p.yh, p.x, core]
    for dy, h in p.mates:
        s.wait(("wd", dy, h), wd.at[dy * NX + h], p.mate(dy, h))
        total = total + wd[dy * NX + h]
    wy[0] = total
    s.send("wy", wy.at[0], wy.at[1], q.across)
    yield
    s.wait("wy", wy.at[1], q.across)
    wz[q.z] = wy[0] + wy[1]
    for h in range(1, NZ):
        s.send(("wz", h), wz.at[q.z], wz.at[q.z], {"row": q.at(q.yl, h)})
    yield
    for h in range(1, NZ):
        s.wait(("wz", h), wz.at[q.zat(-h)], q.across)
    total = wz[0]
    for z in range(1, NZ):
        total = total + wz[z]
    own = wtab.at[p.yh, p.x, core]
    own[...] = total * scale
    for dy, h in p.mates:
        s.send(("w", dy, h), own, own, p.mate(dy, h))
    yield
    for dy, h in p.mates:
        yh = p.yh + dy - 2 * p.yh * dy
        s.wait(("w", dy, h), wtab.at[yh, p.xat(-h), core], p.sibling)
    s.send("ws", wtab.at[:, :, core], wtab.at[:, :, core], p.sibling)
    yield
    s.wait("ws", wtab.at[:, :, sib], p.sibling)


def drain(steps):
    for _ in steps:
        pass


def layer_kernel(
    scale, x_ref, tiles_ref, tr_ref, tc_ref, cnt_ref, w_ref, g_ref, out_ref, wg_ref,
    xtab, etab, tiles, stash, part, back, plan, splan, tr, tc, cnt, w, g, wpart, wc, wd, wy, wz, *rest,
):
    n_col, n_row = 7, 5
    for_col, for_row, (send_sem, recv_sem, sems) = rest[:n_col], rest[n_col : n_col + n_row], rest[n_col + n_row :]
    slots, edge, _ = tiles_ref.shape
    rows, feats = x_ref.shape
    per = rows // edge
    p, q = ColPlace(), RowPlace()
    mr, mc = lax.axis_index("row"), lax.axis_index("col")

    barrier = pltpu.get_barrier_semaphore()
    peers = [p.sibling, q.across] + [p.mate(dy, h) for dy, h in p.mates]
    peers += [{"row": q.at(q.yl, h)} for h in range(1, NZ)]
    for peer in peers:
        pl.semaphore_signal(barrier, inc=1, device_id=peer, device_id_type=MESH)
    loads = [
        pltpu.make_async_copy(tr_ref.at[mr], tr, sems.at[0]),
        pltpu.make_async_copy(tc_ref.at[mr], tc, sems.at[1]),
        pltpu.make_async_copy(cnt_ref, cnt, sems.at[2]),
        pltpu.make_async_copy(x_ref, xtab.at[q.yl, q.z], sems.at[3]),
        pltpu.make_async_copy(tiles_ref, tiles.at[pl.ds(0, slots)], sems.at[4]),
        pltpu.make_async_copy(w_ref, w, sems.at[5]),
        pltpu.make_async_copy(g_ref, g, sems.at[6]),
    ]
    for c in loads:
        c.start()
    tiles[slots] = jnp.zeros((edge, edge), tiles.dtype)
    pl.semaphore_wait(barrier, len(peers))

    s = Sender(send_sem, recv_sem)
    gather = gather_row(s, q, "gr", x_ref, xtab)
    next(gather)
    n_tiles = stash.shape[0] * 2 - 2 - slots
    for c in loads[:3]:
        c.wait()
    t_rows, t_cols = tr[pl.ds(mc, 1)], tc[pl.ds(mc, 1)]
    order_slots(t_rows, p.place(t_rows, per), t_cols, q.place(t_cols, per), cnt[mr, mc], n_tiles, plan)
    to_scalars = pltpu.make_async_copy(plan, splan, sems.at[7])
    to_scalars.start()
    drain(gather)
    to_scalars.wait()
    for c in loads[3:]:
        c.wait()

    def put_part(place, value):
        yh, x, core, n = p.spot(place, per)
        part[yh, x, core, pl.ds(n * edge, edge)] = value

    product = multiply(False, splan, tiles, xtab.reshape(n_tiles, edge, feats), stash, put_part)
    next(product)
    reduce = reduce_col(s, p, "rc", part, *for_col)
    before, s.sent = s.sent, []
    for _ in range(NX - 1):
        next(reduce)
        next(product)
    next(reduce)
    drain(product)
    for c in before:
        c.wait_send()
    drain(reduce)

    agg = part[p.yh, p.x, p.core]
    pre = jnp.dot(agg, w[...], preferred_element_type=F32)
    logistic = jax.nn.sigmoid(pre)
    upstream = g[...].astype(F32)
    d_pre = (upstream * logistic * (1.0 + pre * (1.0 - logistic))).astype(BF16)
    e = lax.dot_general(d_pre, w[...], (((1,), (1,)), ((), ())), preferred_element_type=F32)
    etab[p.yh, p.x, p.core] = e.astype(BF16)
    before, s.sent = s.sent, []
    gather = gather_col(s, p, "gc", etab)
    next(gather)
    out_ref[0] = (pre * logistic).astype(BF16)
    wg = lax.dot_general(agg, d_pre, (((0,), (0,)), ((), ())), preferred_element_type=F32)
    wpart[...] = wg.reshape(wpart.shape)
    weights = sum_weight(s, p, q, wpart, wc, wd, wy, wz, wg_ref, scale)
    next(weights)
    for c in before:
        c.wait_send()
    for _ in range(3):
        next(gather)
    next(weights)
    drain(gather)
    next(weights)

    def put_back(place, value):
        yl, z, n = q.spot(place, per)
        back[yl, z, pl.ds(n * edge, edge)] = value

    product = multiply(True, splan, tiles, etab.reshape(n_tiles, edge, feats), stash, put_back)
    next(product)
    before, s.sent = s.sent, []
    reduce = reduce_row(s, q, "rr", back, *for_row)
    for _ in range(NZ - 1):
        next(reduce)
        next(product)
    next(reduce)
    drain(product)
    next(weights)
    for c in before:
        c.wait_send()
    for _ in range(7):
        next(reduce)
    next(weights)
    for _ in range(5):
        next(reduce)
    next(weights)
    drain(reduce)
    out_ref[1] = back[q.yl, q.z]
    drain(weights)
    s.finish()


def layer(*args):
    x, tiles, tile_rows = args[:3]
    rows, feats = x.shape
    slots, edge, _ = tiles.shape
    n_row, n_col, _ = tile_rows.shape
    n_yh = n_col // (2 * NX)
    n_tiles = n_col * rows // edge
    steps = (slots + n_tiles) // 2
    n_w = feats // n_col
    hbm = pl.BlockSpec(memory_space=pltpu.HBM)
    vmem = pltpu.VMEM
    return pl.pallas_call(
        functools.partial(layer_kernel, 1.0 / math.sqrt(rows * n_row * n_col)),
        out_shape=(
            vmem((2, rows, feats), BF16),
            vmem((n_yh, NX, 2, n_w, feats), F32),
        ),
        in_specs=[hbm] * 7,
        out_specs=[pl.BlockSpec(memory_space=vmem)] * 2,
        scratch_shapes=[
            vmem((n_row // NZ, NZ, rows, feats), BF16),
            vmem((n_yh, NX, 2, rows, feats), BF16),
            vmem((slots + 1, edge, edge), BF16),
            vmem((steps + 1, edge, feats), BF16),
            vmem((n_yh, NX, 2, rows, feats), BF16),
            vmem((n_row // NZ, NZ, rows, feats), BF16),
            vmem((8, PLACES), jnp.int32),
            pltpu.SMEM((8, PLACES), jnp.int32),
            vmem((n_col, slots), jnp.int32),
            vmem((n_col, slots), jnp.int32),
            pltpu.SMEM((n_row, n_col), jnp.int32),
            vmem((feats, feats), BF16),
            vmem((rows, feats), BF16),
            vmem((n_yh, NX, 2, n_w, feats), F32),
            vmem((n_yh, NX, n_w, feats), F32),
            vmem((n_yh * NX, n_w, feats), F32),
            vmem((2, n_w, feats), F32),
            vmem((NZ, n_w, feats), F32),
        ]
        + reduce_col_scratch(n_yh, NX, rows, feats)
        + reduce_row_scratch(rows, feats)
        + [
            pltpu.SemaphoreType.DMA((256,)),
            pltpu.SemaphoreType.DMA((256,)),
            pltpu.SemaphoreType.DMA((8,)),
        ],
        compiler_params=pltpu.CompilerParams(
            collective_id=1, has_side_effects=True, vmem_limit_bytes=48 << 20
        ),
        name="layer",
    )(*[pltpu.with_memory_space_constraint(a, pltpu.HBM) for a in args])


def per_device(node_features, tile_values, tile_rows, tile_cols, tile_count, weight, cotangent):
    results, wgrad = layer(
        node_features[0, 0], tile_values[0, 0], tile_rows, tile_cols, tile_count, weight, cotangent[0, 0]
    )
    return results[:1, None], results[1:, None], wgrad.reshape(weight.shape)


def solution(mesh):
    in_specs = (
        P("col", "row", None, None),
        P("row", "col", None, None, None),
        P(),
        P(),
        P(),
        P(),
        P("row", "col", None, None),
    )
    out_specs = (P("row", "col", None, None), P("col", "row", None, None), P())
    return jax.shard_map(
        per_device, mesh=mesh, in_specs=in_specs, out_specs=out_specs, check_vma=False
    )
```
